32 devices in a mesh: req: 8 (over z, y), head: 4 (over x, core).
Axes of the slice: x: 2, y: 2, z: 4, core: 2. Of those that a mesh axis runs over, the one named last changes fastest.
Arguments:
- tokens: bfloat16 [64, 1024], P('req'), may hold values from -6 to 6
- lengths: int32 [64], P('req'), may hold values from 1 to 512, as said below
- slot_owner: int32 [64], P('req'), may hold values from 0 to 63, as said below
- positions: int32 [64], P('req'), may hold values from 0 to 8191
- variates: int32 [64], P('req'), may hold values from 0 to 7
- cache_variates: int32 [64, 512], P('req'), may hold values from 0 to 7
- kv_cache: bfloat16 [2, 2, 64, 512, 1024], P(None, None, 'req', None, 'head'), may hold values from -6 to 6
- attn_gain: float32 [2, 1024], replicated, may hold values from 0.1 to 1.9
- ffn_gain: float32 [2, 1024], replicated, may hold values from 0.1 to 1.9
- qkv_weight: bfloat16 [2, 1024, 3072], P(None, None, 'head'), may hold values from -0.1875 to 0.1875
- out_weight: bfloat16 [2, 1024, 1024], P(None, 'head'), may hold values from -0.1875 to 0.1875
- gate_up_weight: bfloat16 [2, 2, 1024, 4096], P(None, None, None, 'head'), may hold values from -0.1875 to 0.1875
- down_weight: bfloat16 [2, 4096, 1024], P(None, 'head'), may hold values from -0.09375 to 0.09375
- variate_bias: float32 [2, 2, 16], P(None, None, 'head'), may hold values from -2 to 300
Outputs:
- next_states: bfloat16 [64, 1024], P(('req', 'head'))
The draws below stay inside these ranges and needn't reach their ends.
Inputs may be any that keep to these rules, and one draw needn't show every extreme that they name: `lengths`: live cache positions of each request; the largest is exactly 512 in every draw. `slot_owner`: each request is held in exactly one slot; taken in an order of non-increasing length, the requests fill slot t of every req index in turn t = 0, 1, ..., the req indices in rising order on even turns and in falling order on odd ones; no two slots of one req index hold requests of the same device of next_states (the same 2 consecutive requests).
All inputs are finite; a program needn't handle non-finite values.
Results may differ from the reference program's by a relative error of at most 0.02.
Values may be sent and summed in bfloat16 or wider, within the bound.
No kernel may reach another device: no remote copies, remote signals or barrier semaphores. Data moves between devices by JAX's collectives and lax.ppermute only.
A program may use at most 64 MiB of HBM per device.

```python
import jax
import jax.numpy as jnp
from jax import lax

D = 1024
HEADS = 16
HD = 64
FF = 4096
LAYERS = 2
REQ_DEV = 8
CAP = 512
VARIATES = 8
REQUESTS = 64
SHARE = 2


def draw_variate_bias(key, part):
    first_key = jax.random.fold_in(key, 0)
    modest = jax.random.uniform(first_key, (LAYERS, 2, HEADS), jnp.float32, -2.0, 2.0)
    return modest


def dealing_plan(key):
    base_key = jax.random.fold_in(key, 17)
    short_key, long_key, pick_key, order_key = jax.random.split(base_key, 4)
    short_len = jax.random.randint(short_key, (REQUESTS,), 1, CAP // 4 + 1)
    long_len = jax.random.randint(long_key, (REQUESTS,), CAP // 2, CAP + 1)
    is_long = jax.random.randint(pick_key, (REQUESTS,), 0, 64) == 0
    values = jnp.where(is_long, long_len, short_len).astype(jnp.int32)
    values = values.at[0].set(CAP)
    ordered = -jnp.sort(-values)
    groups = REQUESTS // REQ_DEV
    owner_devices = REQUESTS // SHARE
    device_order = jax.random.permutation(order_key, owner_devices).astype(jnp.int32)
    rank = jnp.arange(REQUESTS, dtype=jnp.int32)
    turn = rank // groups
    place = rank % groups
    per_turn = groups // SHARE
    device_of_rank = device_order[turn * per_turn + place // SHARE]
    request_of_rank = device_of_rank * SHARE + place % SHARE
    group_of_rank = jnp.where(turn % 2 == 0, place, groups - 1 - place)
    slot_of_rank = group_of_rank * REQ_DEV + turn
    lengths_out = jnp.zeros((REQUESTS,), jnp.int32).at[request_of_rank].set(ordered)
    owners_out = jnp.zeros((REQUESTS,), jnp.int32).at[slot_of_rank].set(request_of_rank)
    return (lengths_out, owners_out)


def draw_lengths(key, part):
    return dealing_plan(key)[0]


def draw_slot_owner(key, part):
    return dealing_plan(key)[1]


def touch_ends(result, stream_key, smallest, high):
    spot = [jax.random.randint(jax.random.fold_in(stream_key, axis), (), 0, length) for axis, length in enumerate(result.shape)]
    widest = result.shape.index(max(result.shape))
    next_to = spot[:widest] + [(spot[widest] + 1) % result.shape[widest]] + spot[widest + 1:]
    return result.at[tuple(spot)].set(smallest).at[tuple(next_to)].set(high)


def levels(stream_key, dims, shards, low, largest):
    level = 1.0
    for axis_at, blocks in shards:
        heights = jax.random.uniform(jax.random.fold_in(jax.random.fold_in(stream_key, 6), axis_at), (blocks,), jnp.float32, low / len(shards), largest / len(shards))
        level = level * jnp.repeat(jnp.exp(heights), dims[axis_at] // blocks).reshape((-1,) + (1,) * (len(dims) - 1 - axis_at))
    return level


def bell_draw(rng, extent, width, limit, shards=(), kind=jnp.bfloat16):
    array = width * jax.random.normal(rng, extent, jnp.float32)
    if shards:
        array = array * levels(rng, extent, shards, -0.22, 0.18)
    return jnp.clip(array, -limit, limit).astype(kind)


def setup_inputs(seed: int = 0) -> dict:
    streams_of = jax.random.split(jax.random.key(seed), 15)
    tokens = bell_draw(streams_of[0], (REQUESTS, D), 1.0, 6.0, ((0, 8),))
    lengths = draw_lengths(jax.random.fold_in(streams_of[14], 71), 0)
    slot_owner = draw_slot_owner(jax.random.fold_in(streams_of[14], 71), 0)
    positions = touch_ends(jax.random.randint(streams_of[3], (REQUESTS,), 0, 8192), jax.random.fold_in(streams_of[3], 1), 0, 8191).astype(jnp.int32)
    variates = touch_ends(jax.random.randint(streams_of[4], (REQUESTS,), 0, VARIATES), jax.random.fold_in(streams_of[4], 1), 0, VARIATES - 1).astype(jnp.int32)
    cache_variates = touch_ends(jax.random.randint(streams_of[5], (REQUESTS, CAP), 0, VARIATES), jax.random.fold_in(streams_of[5], 1), 0, VARIATES - 1).astype(jnp.int32)
    kv_cache = bell_draw(streams_of[6], (LAYERS, 2, REQUESTS, CAP, HEADS * HD), 1.0, 6.0, ((2, 8), (4, 4)))
    attn_gain = jnp.clip(1.0 + 0.18 * jax.random.normal(streams_of[7], (LAYERS, D), jnp.float32), 0.1, 1.9)
    ffn_gain = jnp.clip(1.0 + 0.18 * jax.random.normal(streams_of[8], (LAYERS, D), jnp.float32), 0.1, 1.9)
    qkv_weight = bell_draw(streams_of[9], (LAYERS, D, 3 * HEADS * HD), D ** -0.5, 0.1875, ((2, 4),))
    out_weight = bell_draw(streams_of[10], (LAYERS, HEADS * HD, D), (HEADS * HD) ** -0.5, 0.1875, ((1, 4),))
    gate_up_weight = bell_draw(streams_of[11], (LAYERS, 2, D, FF), D ** -0.5, 0.1875, ((3, 4),))
    down_weight = bell_draw(streams_of[12], (LAYERS, FF, D), FF ** -0.5, 0.09375, ((1, 4),))
    variate_bias = draw_variate_bias(jax.random.fold_in(streams_of[14], 71), 0)
    return {"tokens": tokens, "lengths": lengths, "slot_owner": slot_owner, "positions": positions, "variates": variates, "cache_variates": cache_variates, "kv_cache": kv_cache, "attn_gain": attn_gain, "ffn_gain": ffn_gain, "qkv_weight": qkv_weight, "out_weight": out_weight, "gate_up_weight": gate_up_weight, "down_weight": down_weight, "variate_bias": variate_bias}


neg_fill = -1e+30

def rms_scale(stream, gain_row):
    return stream * lax.rsqrt(lax.optimization_barrier(jnp.mean(stream * stream, axis=-1, keepdims=True)) + 1e-06) * gain_row

def rotary(vectors, time_ids):
    half_width = vectors.shape[-1] // 2
    frequency = 10000.0 ** (-2.0 * jnp.arange(half_width, dtype=jnp.float32) / vectors.shape[-1])
    angles = time_ids.astype(jnp.float32)[:, None, None] * frequency[None, None, :]
    cosine = jnp.cos(angles)
    sine_part = jnp.sin(angles)
    front_half = vectors[..., :half_width]
    back_half = vectors[..., half_width:]
    return jnp.concatenate([front_half * cosine - back_half * sine_part, front_half * sine_part + back_half * cosine], axis=-1)

def reference(tokens, lengths, slot_owner, positions, variates, cache_variates, kv_cache, attn_gain, ffn_gain, qkv_weight, out_weight, gate_up_weight, down_weight, variate_bias):
    score_scale = HD ** (-0.5)
    owners = slot_owner
    residual = jnp.take(tokens, owners, axis=0).astype(jnp.float32)
    cache_lengths = jnp.take(lengths, owners)
    time_ids = jnp.take(positions, owners)
    variate_ids = jnp.take(variates, owners)
    for layer_index in range(LAYERS):
        normed = rms_scale(residual, attn_gain[layer_index]).astype(jnp.bfloat16)
        projected = jnp.dot(normed, qkv_weight[layer_index], preferred_element_type=jnp.float32).reshape(REQUESTS, HEADS, 3, HD)
        queries = rotary(projected[:, :, 0], time_ids).astype(jnp.bfloat16)
        key_new = rotary(projected[:, :, 1], time_ids).astype(jnp.bfloat16)
        value_new = projected[:, :, 2].astype(jnp.bfloat16)
        same_bias = variate_bias[layer_index, 0]
        diff_bias = variate_bias[layer_index, 1]

        def one_request(request_items):
            cached_keys, cached_values, cache_var, query_row, key_row, value_row, length_one, variate_one = request_items
            keys_float = cached_keys.reshape(CAP, HEADS, HD).astype(jnp.float32)
            values_float = cached_values.reshape(CAP, HEADS, HD).astype(jnp.float32)
            query_float = query_row.astype(jnp.float32)
            scores = jnp.einsum('hd,chd->hc', query_float, keys_float) * score_scale
            score_bias = jnp.where(cache_var[None, :] == variate_one, same_bias[:, None], diff_bias[:, None])
            scores = scores + score_bias
            live_mask = jnp.arange(CAP, dtype=jnp.int32) < length_one
            scores = jnp.where(live_mask[None, :], scores, neg_fill)
            self_score = lax.optimization_barrier(jnp.sum(query_float * key_row.astype(jnp.float32), axis=-1)) * score_scale + same_bias
            row_top = jnp.maximum(lax.optimization_barrier(jnp.max(scores, axis=1)), self_score)
            weights = jnp.exp(scores - row_top[:, None])
            self_weight = jnp.exp(self_score - row_top)
            denominator = lax.optimization_barrier(jnp.sum(weights, axis=1)) + self_weight
            probs_bf16 = (weights / denominator[:, None]).astype(jnp.bfloat16)
            self_prob = (self_weight / denominator).astype(jnp.bfloat16)
            mixed_heads = jnp.einsum('hc,chd->hd', probs_bf16.astype(jnp.float32), values_float)
            mixed_heads = mixed_heads + self_prob.astype(jnp.float32)[:, None] * value_row.astype(jnp.float32)
            return mixed_heads.reshape(HEADS * HD).astype(jnp.bfloat16)
        attended = lax.map(one_request, (kv_cache[layer_index, 0], kv_cache[layer_index, 1], cache_variates, queries, key_new, value_new, cache_lengths, variate_ids))
        residual = residual + jnp.dot(attended, out_weight[layer_index], preferred_element_type=jnp.float32)
        normed_ffn = rms_scale(residual, ffn_gain[layer_index]).astype(jnp.bfloat16)
        gate_sum = jnp.dot(normed_ffn, gate_up_weight[layer_index, 0], preferred_element_type=jnp.float32)
        up_sum = jnp.dot(normed_ffn, gate_up_weight[layer_index, 1], preferred_element_type=jnp.float32)
        hidden = (jax.nn.silu(gate_sum) * up_sum).astype(jnp.bfloat16)
        residual = residual + jnp.dot(hidden, down_weight[layer_index], preferred_element_type=jnp.float32)
    final_rows = residual.astype(jnp.bfloat16)
    return jnp.zeros_like(final_rows).at[owners].set(final_rows)
```

```python
import functools

import jax
import jax.numpy as jnp
import numpy as np
from jax import lax
from jax.experimental import pallas as pl
from jax.experimental.pallas import tpu as pltpu
from jax.sharding import PartitionSpec as P

HD = 64
LAYERS = 2
META = 128
LOW = 128
CHUNK = 128
NEG = -1e30
F32 = jnp.float32
BF16 = jnp.bfloat16

VMEM = pl.BlockSpec(memory_space=pltpu.VMEM)
SMEM = pl.BlockSpec(memory_space=pltpu.SMEM)
ANY = pl.BlockSpec(memory_space=pl.ANY)
PARAMS = pltpu.CompilerParams(vmem_limit_bytes=32 * 2**20)


def iota(shape, dim):
    return lax.broadcasted_iota(jnp.int32, shape, dim)


def rms_scale(stream, gain_row):
    return stream * lax.rsqrt(jnp.mean(stream * stream, axis=-1, keepdims=True) + 1e-06) * gain_row


def pack_kernel(tokens_ref, lengths_ref, positions_ref, variates_ref, out_ref):
    rows, width = tokens_ref.shape
    out_ref[:, :width] = tokens_ref[...]
    row, lane = iota((rows, META), 0), iota((rows, META), 1)
    kind = lane % (META // 2)
    whole = jnp.zeros((rows, META), jnp.int32)
    for i in range(rows):
        values = jnp.where(
            kind == 0, lengths_ref[i], jnp.where(kind == 1, positions_ref[i], variates_ref[i])
        )
        whole = jnp.where(row == i, values, whole)
    digit = jnp.where(lane < META // 2, whole // LOW, whole % LOW)
    out_ref[:, width:] = digit.astype(F32).astype(BF16)


def attention(
    layer,
    stream,
    facts,
    cos,
    sin,
    variates_ref,
    kv_ref,
    gain_ref,
    qkv_ref,
    out_w_ref,
    bias_ref,
    kv_buf,
    scores,
    mixed,
    first_sem,
    more_sem,
    part_ref,
):
    slots, cap = variates_ref.shape
    width = kv_buf.shape[-1]
    heads = width // HD
    chunks = cap // CHUNK
    rows = heads * slots

    lengths = facts[:, 0:1]
    variate = facts[:, 2:3]
    live_slots = [jnp.sum((lengths > c * CHUNK).astype(jnp.int32)) for c in range(chunks)]

    def more_copy(c, s):
        place = pl.ds(c * CHUNK, CHUNK)
        return pltpu.make_async_copy(
            kv_ref.at[layer, :, s, place, :], kv_buf.at[:, s, place, :], more_sem.at[c, s]
        )

    for c in range(1, chunks):

        @pl.loop(0, live_slots[c])
        def _(s, c=c):
            more_copy(c, s).start()

    normed = rms_scale(stream, gain_ref[layer : layer + 1, :]).astype(BF16)
    projected = jnp.dot(normed, qkv_ref[layer], preferred_element_type=F32)

    lane = iota((slots, 128), 1)
    front = lane % HD < HD // 2
    pieces = []
    for j in range(projected.shape[1] // 128):
        u = projected[:, j * 128 : (j + 1) * 128]
        turned = jnp.where(front, -pltpu.roll(u, 96, 1), pltpu.roll(u, 32, 1))
        is_value = (lane + j * 128) % (3 * HD) >= 2 * HD
        pieces.append(jnp.where(is_value, u, u * cos + turned * sin).astype(BF16).astype(F32))
    turned_all = jnp.concatenate(pieces, axis=1)

    column = iota((slots, width), 1)
    of_head = [column // HD == h for h in range(heads)]
    step = 2 * HD
    query = [
        jnp.where(of_head[h], turned_all[:, h * step : h * step + width], 0.0) for h in range(heads)
    ]
    query_all = jnp.concatenate(query, axis=0).astype(BF16)
    next_keys = jnp.concatenate(
        [turned_all[:, HD:], jnp.zeros((slots, HD), F32)], axis=1
    )
    own_score = [
        jnp.sum(query[h] * next_keys[:, h * step : h * step + width], axis=1, keepdims=True) * 0.125
        + bias_ref[layer, 0, h]
        for h in range(heads)
    ]

    row_slot = iota((rows, width), 0) % slots
    score_dims = (((1,), (1,)), ((), ()))

    def score_block(c, s):
        keys = kv_buf[0, s, pl.ds(c * CHUNK, CHUNK), :]
        mine = jnp.where(row_slot == s, query_all, jnp.zeros_like(query_all))
        return lax.dot_general(mine, keys, score_dims, preferred_element_type=F32)

    pltpu.make_async_copy(
        kv_ref.at[layer, :, :, pl.ds(0, CHUNK), :], kv_buf.at[:, :, pl.ds(0, CHUNK), :], first_sem
    ).wait()
    total = score_block(0, 0)
    for s in range(1, slots):
        total = total + score_block(0, s)
    scores[:, :CHUNK] = total
    if chunks > 1:
        scores[:, CHUNK:] = jnp.zeros((rows, cap - CHUNK), F32)
    for c in range(1, chunks):

        @pl.loop(0, live_slots[c])
        def _(s, c=c):
            more_copy(c, s).wait()
            scores[:, c * CHUNK : (c + 1) * CHUNK] += score_block(c, s)

    same = variates_ref[...].astype(F32) == variate
    live = iota((slots, cap), 1).astype(F32) < lengths
    probs = []
    own_prob = []
    for h in range(heads):
        block = scores[h * slots : (h + 1) * slots, :] * 0.125
        block = block + jnp.where(same, bias_ref[layer, 0, h], bias_ref[layer, 1, h])
        block = jnp.where(live, block, NEG)
        top = jnp.maximum(jnp.max(block, axis=1, keepdims=True), own_score[h])
        weight = jnp.exp(block - top)
        own_weight = jnp.exp(own_score[h] - top)
        share = 1.0 / (jnp.sum(weight, axis=1, keepdims=True) + own_weight)
        probs.append(weight * share)
        own_prob.append((own_weight * share).astype(BF16).astype(F32))
    probs_all = jnp.concatenate(probs, axis=0).astype(BF16)
    prob_slot = iota((rows, CHUNK), 0) % slots

    def mix_block(c, s):
        part = probs_all[:, c * CHUNK : (c + 1) * CHUNK]
        mine = jnp.where(prob_slot == s, part, jnp.zeros_like(part))
        values = kv_buf[1, s, pl.ds(c * CHUNK, CHUNK), :]
        return jnp.dot(mine, values, preferred_element_type=F32)

    total = mix_block(0, 0)
    for s in range(1, slots):
        total = total + mix_block(0, s)
    mixed[...] = total
    for c in range(1, chunks):

        @pl.loop(0, live_slots[c])
        def _(s, c=c):
            mixed[...] += mix_block(c, s)

    attended = jnp.zeros((slots, width), F32)
    for h in range(heads):
        value_new = turned_all[:, (h + 1) * step : (h + 1) * step + width]
        attended = jnp.where(
            of_head[h], mixed[h * slots : (h + 1) * slots, :] + own_prob[h] * value_new, attended
        )
    part_ref[...] = jnp.dot(
        attended.astype(BF16), out_w_ref[layer], preferred_element_type=F32
    ).astype(BF16)


def start_first_copy(layer, kv_ref, kv_buf, first_sem):
    pltpu.make_async_copy(
        kv_ref.at[layer, :, :, pl.ds(0, CHUNK), :], kv_buf.at[:, :, pl.ds(0, CHUNK), :], first_sem
    ).start()


def first_attention_kernel(block_count, *refs):
    owner_ref, place_ref, *block_refs = refs[: 2 + block_count]
    (
        frequency_ref,
        variates_ref,
        kv_ref,
        gain_ref,
        qkv_ref,
        out_w_ref,
        bias_ref,
        part_ref,
        stream_ref,
        facts_ref,
        turn_ref,
        kv_buf,
        scores,
        mixed,
        first_sem,
        more_sem,
    ) = refs[2 + block_count :]
    start_first_copy(0, kv_ref, kv_buf, first_sem)
    gathered = jnp.concatenate([ref[...] for ref in block_refs], axis=0)
    slots = variates_ref.shape[0]
    width = stream_ref.shape[1]
    total = gathered.shape[0]
    row, column = iota((slots, total), 0), iota((slots, total), 1)
    own_block = place_ref[0]
    pick = jnp.zeros((slots, total), F32)
    for s in range(slots):
        owner = owner_ref[s]
        source = ((owner // slots) ^ own_block) * slots + owner % slots
        pick = jnp.where((row == s) & (column == source), 1.0, pick)
    picked = jnp.dot(pick.astype(BF16), gathered, preferred_element_type=F32)
    stream = picked[:, :width]
    digits = picked[:, width:]
    facts = digits * float(LOW) + pltpu.roll(digits, META // 2, 1)
    stream_ref[...] = stream
    facts_ref[...] = facts
    angle = facts[:, 1:2] * frequency_ref[...]
    cos, sin = jnp.cos(angle), jnp.sin(angle)
    turn_ref[:, :128] = cos
    turn_ref[:, 128:] = sin
    attention(
        0, stream, facts, cos, sin, variates_ref, kv_ref, gain_ref, qkv_ref, out_w_ref, bias_ref,
        kv_buf, scores, mixed, first_sem, more_sem, part_ref,
    )


def next_attention_kernel(layer, part_count, *refs):
    part_refs = refs[:part_count]
    (
        old_ref,
        facts_ref,
        turn_ref,
        variates_ref,
        kv_ref,
        gain_ref,
        qkv_ref,
        out_w_ref,
        bias_ref,
        part_ref,
        stream_ref,
        kv_buf,
        scores,
        mixed,
        first_sem,
        more_sem,
    ) = refs[part_count:]
    start_first_copy(layer, kv_ref, kv_buf, first_sem)
    stream = old_ref[...]
    for ref in part_refs:
        stream = stream + ref[...].astype(F32)
    stream_ref[...] = stream
    attention(
        layer, stream, facts_ref[...], turn_ref[:, :128], turn_ref[:, 128:], variates_ref, kv_ref,
        gain_ref, qkv_ref, out_w_ref, bias_ref, kv_buf, scores, mixed, first_sem, more_sem, part_ref,
    )


def feed_forward(layer, part_refs, old_ref, gain_ref, gate_up_ref, down_ref):
    stream = old_ref[...]
    for ref in part_refs:
        stream = stream + ref[...].astype(F32)
    normed = rms_scale(stream, gain_ref[layer : layer + 1, :]).astype(BF16)
    gate = jnp.dot(normed, gate_up_ref[layer, 0], preferred_element_type=F32)
    up = jnp.dot(normed, gate_up_ref[layer, 1], preferred_element_type=F32)
    hidden = (gate / (1.0 + jnp.exp(-gate)) * up).astype(BF16)
    return stream, jnp.dot(hidden, down_ref[layer], preferred_element_type=F32)


def feed_forward_kernel(layer, part_count, *refs):
    old_ref, gain_ref, gate_up_ref, down_ref, part_ref, stream_ref = refs[part_count:]
    stream, part = feed_forward(layer, refs[:part_count], old_ref, gain_ref, gate_up_ref, down_ref)
    stream_ref[...] = stream
    part_ref[...] = part.astype(BF16)


def last_feed_forward_kernel(layer, part_count, share, *refs):
    owner_ref, old_ref, gain_ref, gate_up_ref, down_ref, send_ref = refs[part_count:]
    stream, part = feed_forward(layer, refs[:part_count], old_ref, gain_ref, gate_up_ref, down_ref)
    slots, width = stream.shape
    rows = (part + stream * (1.0 / part_count)).astype(BF16)
    row, lane = iota((slots, META), 0), iota((slots, META), 1)
    devices = send_ref.shape[0]
    target, slot = iota((devices, slots), 0), iota((devices, slots), 1)
    flag = jnp.zeros((slots, META), F32)
    place = jnp.zeros((devices, slots), F32)
    for s in range(slots):
        owner = owner_ref[s]
        flag = jnp.where((row == s) & (lane == owner % share), 1.0, flag)
        place = jnp.where((slot == s) & (target == owner // share), 1.0, place)
    payload = jnp.concatenate([rows, flag.astype(BF16)], axis=1)
    send_ref[...] = jnp.dot(place.astype(BF16), payload, preferred_element_type=F32).astype(BF16)


def place_kernel(received_ref, out_ref):
    share, width = out_ref.shape
    flags = received_ref[:, width:]
    rows = lax.dot_general(
        flags, received_ref[:, :width], (((0,), (0,)), ((), ())), preferred_element_type=F32
    )
    out_ref[...] = rows[:share, :].astype(BF16)


def call(kernel, operands, outs, scratch=()):
    specs, arrays = zip(*operands)
    return pl.pallas_call(
        kernel,
        out_shape=[jax.ShapeDtypeStruct(shape, dtype) for shape, dtype in outs],
        in_specs=list(specs),
        out_specs=[VMEM] * len(outs),
        scratch_shapes=list(scratch),
        compiler_params=PARAMS,
    )(*arrays)


def swap(array, axis, mask):
    count = lax.axis_size(axis)
    return lax.ppermute(array, axis, [(i, i ^ mask) for i in range(count)])


def gather_blocks(block, axis):
    count = lax.axis_size(axis)
    pair = jnp.concatenate([block, swap(block, axis, 1)], axis=0)
    blocks = [pair]
    reach = 2
    while reach < count:
        span = min(4, count // reach)
        held = blocks[0] if len(blocks) == 1 else jnp.concatenate(blocks, axis=0)
        blocks = blocks + [swap(held, axis, reach * k) for k in range(1, span)]
        reach *= span
    return blocks


def per_device(
    tokens,
    lengths,
    slot_owner,
    positions,
    variates,
    cache_variates,
    kv_cache,
    attn_gain,
    ffn_gain,
    qkv_weight,
    out_weight,
    gate_up_weight,
    down_weight,
    variate_bias,
):
    slots, width = tokens.shape
    cap, local_width = kv_cache.shape[3:]
    head_count = lax.axis_size("head")
    devices = lax.axis_size("req") * head_count
    share = slots // head_count
    local_heads = local_width // HD

    (packed,) = call(
        pack_kernel,
        [(VMEM, tokens), (SMEM, lengths), (SMEM, positions), (SMEM, variates)],
        [((slots, width + META), BF16)],
    )
    blocks = gather_blocks(packed, "req")
    own_block = lax.axis_index("req").reshape(1)
    exponent = -2.0 * (np.arange(128) % (HD // 2)) / HD
    frequency = jnp.asarray((10000.0**exponent).astype(np.float32)[None, :])

    scratch = [
        pltpu.VMEM((2, slots, cap, local_width), BF16),
        pltpu.VMEM((local_heads * slots, cap), F32),
        pltpu.VMEM((local_heads * slots, local_width), F32),
        pltpu.SemaphoreType.DMA,
        pltpu.SemaphoreType.DMA((cap // CHUNK, slots)),
    ]
    shared = [
        (VMEM, cache_variates),
        (ANY, kv_cache),
        (VMEM, attn_gain),
        (VMEM, qkv_weight),
        (VMEM, out_weight),
        (SMEM, variate_bias),
    ]
    stream_type = ((slots, width), F32)
    part_type = ((slots, width), BF16)

    def exchange(part):
        return [part] + [swap(part, "head", k) for k in range(1, head_count)]

    part, stream, facts, turn = call(
        functools.partial(first_attention_kernel, len(blocks)),
        [(SMEM, slot_owner), (SMEM, own_block)]
        + [(VMEM, block) for block in blocks]
        + [(VMEM, frequency)]
        + shared,
        [part_type, stream_type, ((slots, META), F32), ((slots, 256), F32)],
        scratch,
    )
    for layer in range(LAYERS):
        if layer:
            part, stream = call(
                functools.partial(next_attention_kernel, layer, head_count),
                [(VMEM, p) for p in parts]
                + [(VMEM, stream), (VMEM, facts), (VMEM, turn)]
                + shared,
                [part_type, stream_type],
                scratch,
            )
        parts = exchange(part)
        weights = [(VMEM, ffn_gain), (VMEM, gate_up_weight), (VMEM, down_weight)]
        if layer < LAYERS - 1:
            part, stream = call(
                functools.partial(feed_forward_kernel, layer, head_count),
                [(VMEM, p) for p in parts] + [(VMEM, stream)] + weights,
                [part_type, stream_type],
            )
            parts = exchange(part)
        else:
            (send,) = call(
                functools.partial(last_feed_forward_kernel, layer, head_count, share),
                [(VMEM, p) for p in parts] + [(SMEM, slot_owner), (VMEM, stream)] + weights,
                [((devices, width + META), BF16)],
            )
    received = lax.all_to_all(send, ("req", "head"), 0, 0, tiled=True)
    (out,) = call(place_kernel, [(VMEM, received)], [((share, width), BF16)])
    return out


def solution(mesh):
    return jax.shard_map(
        per_device,
        mesh=mesh,
        in_specs=(
            P("req", None),
            P("req"),
            P("req"),
            P("req"),
            P("req"),
            P("req", None),
            P(None, None, "req", None, "head"),
            P(),
            P(),
            P(None, None, "head"),
            P(None, "head", None),
            P(None, None, None, "head"),
            P(None, "head", None),
            P(None, None, "head"),
        ),
        out_specs=P(("req", "head"), None),
        check_vma=False,
    )
```

```python
import functools

import jax
import jax.numpy as jnp
import numpy as np
from jax import lax
from jax.experimental import pallas as pl
from jax.experimental.pallas import tpu as pltpu
from jax.sharding import PartitionSpec as P

HD = 64
LAYERS = 2
META = 128
LOW = 128
CHUNK = 128
NEG = -1e30
F32 = jnp.float32
BF16 = jnp.bfloat16

VMEM = pl.BlockSpec(memory_space=pltpu.VMEM)
HBM = pl.BlockSpec(memory_space=pltpu.HBM)
PARAMS = pltpu.CompilerParams(vmem_limit_bytes=16 * 2**20)


def iota(shape, dim):
    return lax.broadcasted_iota(jnp.int32, shape, dim)


def rms_scale(stream, gain_row):
    return stream * lax.rsqrt(jnp.mean(stream * stream, axis=-1, keepdims=True) + 1e-06) * gain_row


def copy_all(pairs, sems):
    copies = [pltpu.make_async_copy(src, dst, sems.at[i]) for i, (src, dst) in enumerate(pairs)]
    for copy in copies:
        copy.start()
    for copy in copies:
        copy.wait()


def pack_kernel(
    tokens_ref, lengths_ref, positions_ref, variates_ref, out_ref, length, position, variate, sems
):
    rows, width = tokens_ref.shape
    copy_all(
        [
            (lengths_ref, length),
            (positions_ref, position),
            (variates_ref, variate),
            (tokens_ref, out_ref.at[:, pl.ds(0, width)]),
        ],
        sems,
    )
    row, lane = iota((rows, META), 0), iota((rows, META), 1)
    kind = lane % (META // 2)
    whole = jnp.zeros((rows, META), jnp.int32)
    for i in range(rows):
        values = jnp.where(kind == 0, length[i], jnp.where(kind == 1, position[i], variate[i]))
        whole = jnp.where(row == i, values, whole)
    digit = jnp.where(lane < META // 2, whole // LOW, whole % LOW)
    out_ref[:, width:] = digit.astype(F32).astype(BF16)


def owner_kernel(
    share,
    after_ref,
    owner_ref,
    own_block_ref,
    *refs,
):
    count = (len(refs) - 6) // 2
    sources, (pick_ref, place_ref, flag_ref), outs = refs[:count], refs[count : count + 3], refs[
        count + 3 : -3
    ]
    owner, own_block, sems = refs[-3:]
    copies = [
        pltpu.make_async_copy(src, dst, sems.at[i])
        for i, (src, dst) in enumerate(
            [(owner_ref, owner), (own_block_ref, own_block)] + list(zip(sources, outs))
        )
    ]
    for copy in copies:
        copy.start()
    copies[0].wait()
    copies[1].wait()
    slots, total = pick_ref.shape
    devices = place_ref.shape[0]
    row, column = iota((slots, total), 0), iota((slots, total), 1)
    target, slot = iota((devices, slots), 0), iota((devices, slots), 1)
    flag_row, lane = iota((slots, META), 0), iota((slots, META), 1)
    pick = jnp.zeros((slots, total), F32)
    place = jnp.zeros((devices, slots), F32)
    flag = jnp.zeros((slots, META), F32)
    for s in range(slots):
        request = owner[s]
        source = ((request // slots) ^ own_block[0]) * slots + request % slots
        pick = jnp.where((row == s) & (column == source), 1.0, pick)
        place = jnp.where((slot == s) & (target == request // share), 1.0, place)
        flag = jnp.where((flag_row == s) & (lane == request % share), 1.0, flag)
    pick_ref[...] = pick.astype(BF16)
    place_ref[...] = place.astype(BF16)
    flag_ref[...] = flag.astype(BF16)
    for copy in copies[2:]:
        copy.wait()


def bring_kernel(parts, after_ref, *refs):
    count = len(parts)
    copy_all(
        [(refs[i].at[parts[i]], refs[count + i]) for i in range(count)], refs[2 * count]
    )


def attention(
    layer,
    stream,
    facts,
    cos,
    sin,
    variates_ref,
    kv_ref,
    gain_ref,
    qkv_ref,
    out_w_ref,
    bias_ref,
    scores,
    mixed,
    part_ref,
):
    slots, cap = variates_ref.shape
    width = kv_ref.shape[-1]
    heads = width // HD
    rows = heads * slots

    lengths = facts[:, 0:1]
    variate = facts[:, 2:3]
    longer = jnp.sum((lengths > CHUNK).astype(jnp.int32))

    normed = rms_scale(stream, gain_ref[layer : layer + 1, :]).astype(BF16)
    projected = jnp.dot(normed, qkv_ref[layer], preferred_element_type=F32)

    lane = iota((slots, 128), 1)
    front = lane % HD < HD // 2
    pieces = []
    for j in range(projected.shape[1] // 128):
        u = projected[:, j * 128 : (j + 1) * 128]
        turned = jnp.where(front, -pltpu.roll(u, 96, 1), pltpu.roll(u, 32, 1))
        is_value = (lane + j * 128) % (3 * HD) >= 2 * HD
        pieces.append(jnp.where(is_value, u, u * cos + turned * sin).astype(BF16).astype(F32))
    turned_all = jnp.concatenate(pieces, axis=1)

    column = iota((slots, width), 1)
    of_head = [column // HD == h for h in range(heads)]
    step = 2 * HD
    query = [
        jnp.where(of_head[h], turned_all[:, h * step : h * step + width], 0.0) for h in range(heads)
    ]
    query_all = jnp.concatenate(query, axis=0).astype(BF16)

    score_dims = (((1,), (1,)), ((), ()))
    keys = kv_ref[0, :, :CHUNK, :].reshape(slots * CHUNK, width)
    raw = lax.dot_general(query_all, keys, score_dims, preferred_element_type=F32)
    row_slot = iota((rows, CHUNK), 0) % slots
    total = raw[:, :CHUNK]
    for s in range(1, slots):
        total = jnp.where(row_slot == s, raw[:, s * CHUNK : (s + 1) * CHUNK], total)
    scores[:, :CHUNK] = total
    rest_slot = iota((rows, cap - CHUNK), 0) % slots

    @pl.loop(0, longer)
    def _(s):
        more = lax.dot_general(
            query_all, kv_ref[0, s, CHUNK:, :], score_dims, preferred_element_type=F32
        )
        scores[:, CHUNK:] = jnp.where(rest_slot == s, more, scores[:, CHUNK:])

    next_keys = jnp.concatenate([turned_all[:, HD:], jnp.zeros((slots, HD), F32)], axis=1)
    own_score = [
        jnp.sum(query[h] * next_keys[:, h * step : h * step + width], axis=1, keepdims=True) * 0.125
        + bias_ref[layer, 0:1, h : h + 1]
        for h in range(heads)
    ]
    same = variates_ref[...].astype(F32) == variate
    live = iota((slots, cap), 1).astype(F32) < lengths
    probs = []
    own_prob = []
    for h in range(heads):
        block = scores[h * slots : (h + 1) * slots, :] * 0.125
        block = block + jnp.where(
            same, bias_ref[layer, 0:1, h : h + 1], bias_ref[layer, 1:2, h : h + 1]
        )
        block = jnp.where(live, block, NEG)
        top = jnp.maximum(jnp.max(block, axis=1, keepdims=True), own_score[h])
        weight = jnp.exp(block - top)
        own_weight = jnp.exp(own_score[h] - top)
        share = 1.0 / (jnp.sum(weight, axis=1, keepdims=True) + own_weight)
        probs.append(weight * share)
        own_prob.append((own_weight * share).astype(BF16).astype(F32))
    probs_all = jnp.concatenate(probs, axis=0).astype(BF16)
    first = probs_all[:, :CHUNK]
    spread = jnp.concatenate(
        [jnp.where(row_slot == s, first, jnp.zeros_like(first)) for s in range(slots)], axis=1
    )
    values = kv_ref[1, :, :CHUNK, :].reshape(slots * CHUNK, width)
    mixed[...] = jnp.dot(spread, values, preferred_element_type=F32)
    rest = probs_all[:, CHUNK:]

    @pl.loop(0, longer)
    def _(s):
        mine = jnp.where(rest_slot == s, rest, jnp.zeros_like(rest))
        mixed[...] += jnp.dot(mine, kv_ref[1, s, CHUNK:, :], preferred_element_type=F32)

    attended = jnp.zeros((slots, width), F32)
    for h in range(heads):
        value_new = turned_all[:, (h + 1) * step : (h + 1) * step + width]
        attended = jnp.where(
            of_head[h], mixed[h * slots : (h + 1) * slots, :] + own_prob[h] * value_new, attended
        )
    part_ref[...] = jnp.dot(
        attended.astype(BF16), out_w_ref[layer], preferred_element_type=F32
    ).astype(BF16)


def first_attention_kernel(block_count, *refs):
    (
        pick_ref,
        frequency_ref,
        variates_ref,
        kv_ref,
        gain_ref,
        qkv_ref,
        out_w_ref,
        bias_ref,
        part_ref,
        stream_ref,
        facts_ref,
        turn_ref,
        scores,
        mixed,
    ) = refs[block_count:]
    gathered = jnp.concatenate([ref[...] for ref in refs[:block_count]], axis=0)
    width = stream_ref.shape[1]
    picked = jnp.dot(pick_ref[...], gathered, preferred_element_type=F32)
    stream = picked[:, :width]
    digits = picked[:, width:]
    facts = digits * float(LOW) + pltpu.roll(digits, META // 2, 1)
    stream_ref[...] = stream
    facts_ref[...] = facts
    angle = facts[:, 1:2] * frequency_ref[...]
    cos, sin = jnp.cos(angle), jnp.sin(angle)
    turn_ref[:, :128] = cos
    turn_ref[:, 128:] = sin
    attention(
        0, stream, facts, cos, sin, variates_ref, kv_ref, gain_ref, qkv_ref, out_w_ref, bias_ref,
        scores, mixed, part_ref,
    )


def next_attention_kernel(layer, part_count, *refs):
    (
        old_ref,
        facts_ref,
        turn_ref,
        variates_ref,
        kv_ref,
        gain_ref,
        qkv_ref,
        out_w_ref,
        bias_ref,
        part_ref,
        stream_ref,
        scores,
        mixed,
    ) = refs[part_count:]
    stream = old_ref[...]
    for ref in refs[:part_count]:
        stream = stream + ref[...].astype(F32)
    stream_ref[...] = stream
    attention(
        layer, stream, facts_ref[...], turn_ref[:, :128], turn_ref[:, 128:], variates_ref, kv_ref,
        gain_ref, qkv_ref, out_w_ref, bias_ref, scores, mixed, part_ref,
    )


def feed_forward(layer, part_refs, old_ref, gain_ref, gate_up_ref, down_ref):
    stream = old_ref[...]
    for ref in part_refs:
        stream = stream + ref[...].astype(F32)
    normed = rms_scale(stream, gain_ref[layer : layer + 1, :]).astype(BF16)
    gate = jnp.dot(normed, gate_up_ref[0], preferred_element_type=F32)
    up = jnp.dot(normed, gate_up_ref[1], preferred_element_type=F32)
    hidden = (gate / (1.0 + jnp.exp(-gate)) * up).astype(BF16)
    return stream, jnp.dot(hidden, down_ref[...], preferred_element_type=F32)


def feed_forward_kernel(layer, part_count, *refs):
    old_ref, gain_ref, gate_up_ref, down_ref, part_ref, stream_ref = refs[part_count:]
    stream, part = feed_forward(layer, refs[:part_count], old_ref, gain_ref, gate_up_ref, down_ref)
    stream_ref[...] = stream
    part_ref[...] = part.astype(BF16)


def last_feed_forward_kernel(layer, part_count, *refs):
    place_ref, flag_ref, old_ref, gain_ref, gate_up_ref, down_ref, send_ref = refs[part_count:]
    stream, part = feed_forward(layer, refs[:part_count], old_ref, gain_ref, gate_up_ref, down_ref)
    rows = (part + stream * (1.0 / part_count)).astype(BF16)
    half = rows.shape[1] // 2
    for i in range(2):
        payload = jnp.concatenate([rows[:, i * half : (i + 1) * half], flag_ref[...]], axis=1)
        spread = jnp.dot(place_ref[...], payload, preferred_element_type=F32)
        send_ref[:, i, :] = spread.astype(BF16)


def place_kernel(received_ref, out_ref):
    share, width = out_ref.shape
    half = width // 2
    for i in range(2):
        rows = lax.dot_general(
            received_ref[:, i, half:],
            received_ref[:, i, :half],
            (((0,), (0,)), ((), ())),
            preferred_element_type=F32,
        )
        out_ref[:, i * half : (i + 1) * half] = rows[:share, :].astype(BF16)


def call(kernel, operands, outs, scratch=()):
    specs, arrays = zip(*operands)
    return pl.pallas_call(
        kernel,
        out_shape=[pltpu.VMEM(shape, dtype) for shape, dtype in outs],
        in_specs=list(specs),
        out_specs=[VMEM] * len(outs),
        scratch_shapes=list(scratch),
        compiler_params=PARAMS,
    )(*arrays)


def bring(after, sources):
    return call(
        functools.partial(bring_kernel, [layer for _, layer in sources]),
        [(HBM, after)] + [(HBM, array) for array, _ in sources],
        [
            (tuple(n for n, i in zip(array.shape, index) if i is None), array.dtype)
            for array, index in ((a, i + (None,) * (a.ndim - len(i))) for a, i in sources)
        ],
        [pltpu.SemaphoreType.DMA((len(sources),))],
    )


def swap(array, axis, mask):
    count = lax.axis_size(axis)
    return lax.ppermute(array, axis, [(i, i ^ mask) for i in range(count)])


def gather_blocks(block, axis):
    count = lax.axis_size(axis)
    pair = jnp.concatenate([block, swap(block, axis, 1)], axis=0)
    blocks = [pair]
    reach = 2
    while reach < count:
        span = min(4, count // reach)
        held = blocks[0] if len(blocks) == 1 else jnp.concatenate(blocks, axis=0)
        blocks = blocks + [swap(held, axis, reach * k) for k in range(1, span)]
        reach *= span
    return blocks


def per_device(
    tokens,
    lengths,
    slot_owner,
    positions,
    variates,
    cache_variates,
    kv_cache,
    attn_gain,
    ffn_gain,
    qkv_weight,
    out_weight,
    gate_up_weight,
    down_weight,
    variate_bias,
):
    slots, width = tokens.shape
    cap, local_width = kv_cache.shape[3:]
    head_count = lax.axis_size("head")
    devices = lax.axis_size("req") * head_count
    share = slots // head_count
    local_heads = local_width // HD

    total = slots * lax.axis_size("req")
    whole_row = [pltpu.SMEM((slots,), jnp.int32)] * 3
    (packed,) = call(
        pack_kernel,
        [(HBM, tokens), (HBM, lengths), (HBM, positions), (HBM, variates)],
        [((slots, width + META), BF16)],
        whole_row + [pltpu.SemaphoreType.DMA((4,))],
    )
    exponent = -2.0 * (np.arange(128) % (HD // 2)) / HD
    frequency = jnp.asarray((10000.0**exponent).astype(np.float32)[None, :])
    own_block = lax.axis_index("req").reshape(1)
    sources = [
        cache_variates, attn_gain, ffn_gain, qkv_weight, out_weight, variate_bias, frequency,
    ]
    pick, place, flag, *held = call(
        functools.partial(owner_kernel, share),
        [(HBM, packed), (HBM, slot_owner), (HBM, own_block)] + [(HBM, x) for x in sources],
        [((slots, total), BF16), ((devices, slots), BF16), ((slots, META), BF16)]
        + [(x.shape, x.dtype) for x in sources],
        [
            pltpu.SMEM((slots,), jnp.int32),
            pltpu.SMEM((1,), jnp.int32),
            pltpu.SemaphoreType.DMA((len(sources) + 2,)),
        ],
    )
    cache_variates, attn_gain, ffn_gain, qkv_weight, out_weight, variate_bias, frequency = held
    blocks = gather_blocks(packed, "req")
    kv, gate_up, down = bring(
        blocks[0], [(kv_cache, (0,)), (gate_up_weight, (0,)), (down_weight, (0,))]
    )

    scratch = [
        pltpu.VMEM((local_heads * slots, cap), F32),
        pltpu.VMEM((local_heads * slots, local_width), F32),
    ]
    stream_type = ((slots, width), F32)
    part_type = ((slots, width), BF16)

    def exchange(part):
        return [part] + [swap(part, "head", k) for k in range(1, head_count)]

    def on_chip(*arrays):
        return [(VMEM, x) for x in arrays]

    part, stream, facts, turn = call(
        functools.partial(first_attention_kernel, len(blocks)),
        on_chip(*blocks, pick, frequency, cache_variates, kv, attn_gain)
        + on_chip(qkv_weight, out_weight, variate_bias),
        [part_type, stream_type, ((slots, META), F32), ((slots, 256), F32)],
        scratch,
    )
    for layer in range(LAYERS):
        last = layer == LAYERS - 1
        if layer:
            (kv,) = next_kv
            part, stream = call(
                functools.partial(next_attention_kernel, layer, head_count),
                on_chip(*parts, stream, facts, turn, cache_variates, kv, attn_gain)
                + on_chip(qkv_weight, out_weight, variate_bias),
                [part_type, stream_type],
                scratch,
            )
        parts = exchange(part)
        if not last:
            next_kv = bring(part, [(kv_cache, (layer + 1,))])
            part, stream = call(
                functools.partial(feed_forward_kernel, layer, head_count),
                on_chip(*parts, stream, ffn_gain, gate_up, down),
                [part_type, stream_type],
            )
            parts = exchange(part)
            gate_up, down = bring(
                part, [(gate_up_weight, (layer + 1,)), (down_weight, (layer + 1,))]
            )
        else:
            (send,) = call(
                functools.partial(last_feed_forward_kernel, layer, head_count),
                on_chip(*parts, place, flag, stream, ffn_gain, gate_up, down),
                [((devices, 2, width // 2 + META), BF16)],
            )
    received = lax.all_to_all(send, ("req", "head"), 0, 0, tiled=True)
    return pl.pallas_call(
        place_kernel,
        out_shape=jax.ShapeDtypeStruct((share, width), BF16),
        in_specs=[VMEM],
        out_specs=VMEM,
        compiler_params=PARAMS,
    )(received)


def solution(mesh):
    return jax.shard_map(
        per_device,
        mesh=mesh,
        in_specs=(
            P("req", None),
            P("req"),
            P("req"),
            P("req"),
            P("req"),
            P("req", None),
            P(None, None, "req", None, "head"),
            P(),
            P(),
            P(None, None, "head"),
            P(None, "head", None),
            P(None, None, None, "head"),
            P(None, "head", None),
            P(None, None, "head"),
        ),
        out_specs=P(("req", "head"), None),
        check_vma=False,
    )
```

```python
import functools

import jax
import jax.numpy as jnp
import numpy as np
from jax import lax
from jax.experimental import pallas as pl
from jax.experimental.pallas import tpu as pltpu
from jax.sharding import PartitionSpec as P

HD = 64
LAYERS = 2
META = 128
LOW = 128
CHUNK = 128
NEG = -1e30
F32 = jnp.float32
BF16 = jnp.bfloat16

VMEM = pl.BlockSpec(memory_space=pltpu.VMEM)
HBM = pl.BlockSpec(memory_space=pltpu.HBM)
ANY = pl.BlockSpec(memory_space=pl.ANY)
PARAMS = pltpu.CompilerParams(vmem_limit_bytes=16 * 2**20)


def iota(shape, dim):
    return lax.broadcasted_iota(jnp.int32, shape, dim)


def rms_scale(stream, gain_row):
    return stream * lax.rsqrt(jnp.mean(stream * stream, axis=-1, keepdims=True) + 1e-06) * gain_row


def copy_all(pairs, sems):
    copies = [pltpu.make_async_copy(src, dst, sems.at[i]) for i, (src, dst) in enumerate(pairs)]
    for copy in copies:
        copy.start()
    for copy in copies:
        copy.wait()


def pack_kernel(
    tokens_ref, lengths_ref, positions_ref, variates_ref, out_ref, length, position, variate, sems
):
    rows, width = tokens_ref.shape
    copy_all(
        [
            (lengths_ref, length),
            (positions_ref, position),
            (variates_ref, variate),
            (tokens_ref, out_ref.at[:, pl.ds(0, width)]),
        ],
        sems,
    )
    row, lane = iota((rows, META), 0), iota((rows, META), 1)
    kind = lane % (META // 2)
    whole = jnp.zeros((rows, META), jnp.int32)
    for i in range(rows):
        values = jnp.where(kind == 0, length[i], jnp.where(kind == 1, position[i], variate[i]))
        whole = jnp.where(row == i, values, whole)
    digit = jnp.where(lane < META // 2, whole // LOW, whole % LOW)
    out_ref[:, width:] = digit.astype(F32).astype(BF16)


def owner_kernel(
    share,
    after_ref,
    owner_ref,
    own_block_ref,
    *refs,
):
    count = (len(refs) - 6) // 2
    sources, (pick_ref, place_ref, flag_ref), outs = refs[:count], refs[count : count + 3], refs[
        count + 3 : -3
    ]
    owner, own_block, sems = refs[-3:]
    copies = [
        pltpu.make_async_copy(src, dst, sems.at[i])
        for i, (src, dst) in enumerate(
            [(owner_ref, owner), (own_block_ref, own_block)] + list(zip(sources, outs))
        )
    ]
    for copy in copies:
        copy.start()
    copies[0].wait()
    copies[1].wait()
    slots, total = pick_ref.shape
    devices = place_ref.shape[0]
    row, column = iota((slots, total), 0), iota((slots, total), 1)
    target, slot = iota((devices, slots), 0), iota((devices, slots), 1)
    flag_row, lane = iota((slots, META), 0), iota((slots, META), 1)
    pick = jnp.zeros((slots, total), F32)
    place = jnp.zeros((devices, slots), F32)
    flag = jnp.zeros((slots, META), F32)
    for s in range(slots):
        request = owner[s]
        source = ((request // slots) ^ own_block[0]) * slots + request % slots
        pick = jnp.where((row == s) & (column == source), 1.0, pick)
        place = jnp.where((slot == s) & (target == request // share), 1.0, place)
        flag = jnp.where((flag_row == s) & (lane == request % share), 1.0, flag)
    pick_ref[...] = pick.astype(BF16)
    place_ref[...] = place.astype(BF16)
    flag_ref[...] = flag.astype(BF16)
    for copy in copies[2:]:
        copy.wait()


def bring_kernel(parts, after_ref, *refs):
    count = len(parts)
    copy_all(
        [(refs[i].at[parts[i]], refs[count + i]) for i in range(count)], refs[2 * count]
    )


def attention(
    layer,
    stream,
    facts,
    cos,
    sin,
    variates_ref,
    kv_ref,
    gain_ref,
    qkv_ref,
    out_w_ref,
    bias_ref,
    scores,
    mixed,
    part_ref,
):
    slots, cap = variates_ref.shape
    width = kv_ref.shape[-1]
    heads = width // HD
    rows = heads * slots

    lengths = facts[:, 0:1]
    variate = facts[:, 2:3]
    longer = jnp.sum((lengths > CHUNK).astype(jnp.int32))

    normed = rms_scale(stream, gain_ref[layer : layer + 1, :]).astype(BF16)
    projected = jnp.dot(normed, qkv_ref[layer], preferred_element_type=F32)

    lane = iota((slots, 128), 1)
    front = lane % HD < HD // 2
    pieces = []
    for j in range(projected.shape[1] // 128):
        u = projected[:, j * 128 : (j + 1) * 128]
        turned = jnp.where(front, -pltpu.roll(u, 96, 1), pltpu.roll(u, 32, 1))
        is_value = (lane + j * 128) % (3 * HD) >= 2 * HD
        pieces.append(jnp.where(is_value, u, u * cos + turned * sin).astype(BF16).astype(F32))
    turned_all = jnp.concatenate(pieces, axis=1)

    column = iota((slots, width), 1)
    of_head = [column // HD == h for h in range(heads)]
    step = 2 * HD
    query = [
        jnp.where(of_head[h], turned_all[:, h * step : h * step + width], 0.0) for h in range(heads)
    ]
    query_all = jnp.concatenate(query, axis=0).astype(BF16)

    score_dims = (((1,), (1,)), ((), ()))
    keys = kv_ref[0, :, :CHUNK, :].reshape(slots * CHUNK, width)
    raw = lax.dot_general(query_all, keys, score_dims, preferred_element_type=F32)
    row_slot = iota((rows, CHUNK), 0) % slots
    total = raw[:, :CHUNK]
    for s in range(1, slots):
        total = jnp.where(row_slot == s, raw[:, s * CHUNK : (s + 1) * CHUNK], total)
    scores[:, :CHUNK] = total
    rest_slot = iota((rows, cap - CHUNK), 0) % slots

    @pl.loop(0, longer)
    def _(s):
        more = lax.dot_general(
            query_all, kv_ref[0, s, CHUNK:, :], score_dims, preferred_element_type=F32
        )
        scores[:, CHUNK:] = jnp.where(rest_slot == s, more, scores[:, CHUNK:])

    next_keys = jnp.concatenate([turned_all[:, HD:], jnp.zeros((slots, HD), F32)], axis=1)
    own_score = [
        jnp.sum(query[h] * next_keys[:, h * step : h * step + width], axis=1, keepdims=True) * 0.125
        + bias_ref[layer, 0:1, h : h + 1]
        for h in range(heads)
    ]
    same = variates_ref[...].astype(F32) == variate
    live = iota((slots, cap), 1).astype(F32) < lengths
    probs = []
    own_prob = []
    for h in range(heads):
        block = scores[h * slots : (h + 1) * slots, :] * 0.125
        block = block + jnp.where(
            same, bias_ref[layer, 0:1, h : h + 1], bias_ref[layer, 1:2, h : h + 1]
        )
        block = jnp.where(live, block, NEG)
        top = jnp.maximum(jnp.max(block, axis=1, keepdims=True), own_score[h])
        weight = jnp.exp(block - top)
        own_weight = jnp.exp(own_score[h] - top)
        share = 1.0 / (jnp.sum(weight, axis=1, keepdims=True) + own_weight)
        probs.append(weight * share)
        own_prob.append((own_weight * share).astype(BF16).astype(F32))
    probs_all = jnp.concatenate(probs, axis=0).astype(BF16)
    first = probs_all[:, :CHUNK]
    spread = jnp.concatenate(
        [jnp.where(row_slot == s, first, jnp.zeros_like(first)) for s in range(slots)], axis=1
    )
    values = kv_ref[1, :, :CHUNK, :].reshape(slots * CHUNK, width)
    mixed[...] = jnp.dot(spread, values, preferred_element_type=F32)
    rest = probs_all[:, CHUNK:]

    @pl.loop(0, longer)
    def _(s):
        mine = jnp.where(rest_slot == s, rest, jnp.zeros_like(rest))
        mixed[...] += jnp.dot(mine, kv_ref[1, s, CHUNK:, :], preferred_element_type=F32)

    attended = jnp.zeros((slots, width), F32)
    for h in range(heads):
        value_new = turned_all[:, (h + 1) * step : (h + 1) * step + width]
        attended = jnp.where(
            of_head[h], mixed[h * slots : (h + 1) * slots, :] + own_prob[h] * value_new, attended
        )
    part_ref[...] = jnp.dot(
        attended.astype(BF16), out_w_ref[layer], preferred_element_type=F32
    ).astype(BF16)


def first_attention_kernel(block_count, *refs):
    (
        pick_ref,
        frequency_ref,
        variates_ref,
        kv_ref,
        gain_ref,
        qkv_ref,
        out_w_ref,
        bias_ref,
        part_ref,
        stream_ref,
        facts_ref,
        turn_ref,
        scores,
        mixed,
    ) = refs[block_count:]
    gathered = jnp.concatenate([ref[...] for ref in refs[:block_count]], axis=0)
    width = stream_ref.shape[1]
    picked = jnp.dot(pick_ref[...], gathered, preferred_element_type=F32)
    stream = picked[:, :width]
    digits = picked[:, width:]
    facts = digits * float(LOW) + pltpu.roll(digits, META // 2, 1)
    stream_ref[...] = stream
    facts_ref[...] = facts
    angle = facts[:, 1:2] * frequency_ref[...]
    cos, sin = jnp.cos(angle), jnp.sin(angle)
    turn_ref[:, :128] = cos
    turn_ref[:, 128:] = sin
    attention(
        0, stream, facts, cos, sin, variates_ref, kv_ref, gain_ref, qkv_ref, out_w_ref, bias_ref,
        scores, mixed, part_ref,
    )


def next_attention_kernel(layer, part_count, *refs):
    (
        old_ref,
        facts_ref,
        turn_ref,
        variates_ref,
        kv_ref,
        gain_ref,
        qkv_ref,
        out_w_ref,
        bias_ref,
        part_ref,
        stream_ref,
        scores,
        mixed,
    ) = refs[part_count:]
    stream = old_ref[...]
    for ref in refs[:part_count]:
        stream = stream + ref[...].astype(F32)
    stream_ref[...] = stream
    attention(
        layer, stream, facts_ref[...], turn_ref[:, :128], turn_ref[:, 128:], variates_ref, kv_ref,
        gain_ref, qkv_ref, out_w_ref, bias_ref, scores, mixed, part_ref,
    )


def feed_forward(layer, part_refs, old_ref, gain_ref, gate_up_ref, down_ref):
    stream = old_ref[...]
    for ref in part_refs:
        stream = stream + ref[...].astype(F32)
    normed = rms_scale(stream, gain_ref[layer : layer + 1, :]).astype(BF16)
    gate = jnp.dot(normed, gate_up_ref[0], preferred_element_type=F32)
    up = jnp.dot(normed, gate_up_ref[1], preferred_element_type=F32)
    hidden = (gate / (1.0 + jnp.exp(-gate)) * up).astype(BF16)
    return stream, jnp.dot(hidden, down_ref[...], preferred_element_type=F32)


def feed_forward_kernel(layer, part_count, *refs):
    old_ref, gain_ref, gate_up_ref, down_ref, part_ref, stream_ref = refs[part_count:]
    stream, part = feed_forward(layer, refs[:part_count], old_ref, gain_ref, gate_up_ref, down_ref)
    stream_ref[...] = stream
    part_ref[...] = part.astype(BF16)


def last_feed_forward_kernel(layer, part_count, *refs):
    place_ref, flag_ref, old_ref, gain_ref, gate_up_ref, down_ref, send_ref = refs[part_count:]
    stream, part = feed_forward(layer, refs[:part_count], old_ref, gain_ref, gate_up_ref, down_ref)
    rows = (part + stream * (1.0 / part_count)).astype(BF16)
    half = rows.shape[1] // 2
    for i in range(2):
        payload = jnp.concatenate([rows[:, i * half : (i + 1) * half], flag_ref[...]], axis=1)
        spread = jnp.dot(place_ref[...], payload, preferred_element_type=F32)
        send_ref[:, i, :] = spread.astype(BF16)


def place_kernel(received_ref, out_ref):
    share, width = out_ref.shape
    half = width // 2
    for i in range(2):
        rows = lax.dot_general(
            received_ref[:, i, half:],
            received_ref[:, i, :half],
            (((0,), (0,)), ((), ())),
            preferred_element_type=F32,
        )
        out_ref[:, i * half : (i + 1) * half] = rows[:share, :].astype(BF16)


def call(kernel, operands, outs, scratch=()):
    specs = [spec for spec, _ in operands]
    arrays = [
        pltpu.with_memory_space_constraint(array, pltpu.HBM) if spec is HBM else array
        for spec, array in operands
    ]
    return pl.pallas_call(
        kernel,
        out_shape=[pltpu.VMEM(shape, dtype) for shape, dtype in outs],
        in_specs=specs,
        out_specs=[VMEM] * len(outs),
        scratch_shapes=list(scratch),
        compiler_params=PARAMS,
    )(*arrays)


def bring(after, sources):
    return call(
        functools.partial(bring_kernel, [layer for _, layer in sources]),
        [(ANY, after)] + [(HBM, array) for array, _ in sources],
        [
            (tuple(n for n, i in zip(array.shape, index) if i is None), array.dtype)
            for array, index in ((a, i + (None,) * (a.ndim - len(i))) for a, i in sources)
        ],
        [pltpu.SemaphoreType.DMA((len(sources),))],
    )


def swap(array, axis, mask):
    count = lax.axis_size(axis)
    return lax.ppermute(array, axis, [(i, i ^ mask) for i in range(count)])


def gather_blocks(block, axis):
    count = lax.axis_size(axis)
    pair = jnp.concatenate([block, swap(block, axis, 1)], axis=0)
    blocks = [pair]
    reach = 2
    while reach < count:
        span = min(4, count // reach)
        held = blocks[0] if len(blocks) == 1 else jnp.concatenate(blocks, axis=0)
        blocks = blocks + [swap(held, axis, reach * k) for k in range(1, span)]
        reach *= span
    return blocks


def per_device(
    tokens,
    lengths,
    slot_owner,
    positions,
    variates,
    cache_variates,
    kv_cache,
    attn_gain,
    ffn_gain,
    qkv_weight,
    out_weight,
    gate_up_weight,
    down_weight,
    variate_bias,
):
    slots, width = tokens.shape
    cap, local_width = kv_cache.shape[3:]
    head_count = lax.axis_size("head")
    devices = lax.axis_size("req") * head_count
    share = slots // head_count
    local_heads = local_width // HD

    total = slots * lax.axis_size("req")
    whole_row = [pltpu.SMEM((slots,), jnp.int32)] * 3
    (packed,) = call(
        pack_kernel,
        [(HBM, tokens), (HBM, lengths), (HBM, positions), (HBM, variates)],
        [((slots, width + META), BF16)],
        whole_row + [pltpu.SemaphoreType.DMA((4,))],
    )
    exponent = -2.0 * (np.arange(128) % (HD // 2)) / HD
    frequency = jnp.asarray((10000.0**exponent).astype(np.float32)[None, :])
    own_block = lax.axis_index("req").reshape(1)
    sources = [
        cache_variates, attn_gain, ffn_gain, qkv_weight, out_weight, variate_bias, frequency,
    ]
    pick, place, flag, *held = call(
        functools.partial(owner_kernel, share),
        [(ANY, packed), (HBM, slot_owner), (HBM, own_block)] + [(HBM, x) for x in sources],
        [((slots, total), BF16), ((devices, slots), BF16), ((slots, META), BF16)]
        + [(x.shape, x.dtype) for x in sources],
        [
            pltpu.SMEM((slots,), jnp.int32),
            pltpu.SMEM((1,), jnp.int32),
            pltpu.SemaphoreType.DMA((len(sources) + 2,)),
        ],
    )
    cache_variates, attn_gain, ffn_gain, qkv_weight, out_weight, variate_bias, frequency = held
    blocks = gather_blocks(packed, "req")
    kv, gate_up, down = bring(
        blocks[0], [(kv_cache, (0,)), (gate_up_weight, (0,)), (down_weight, (0,))]
    )

    scratch = [
        pltpu.VMEM((local_heads * slots, cap), F32),
        pltpu.VMEM((local_heads * slots, local_width), F32),
    ]
    stream_type = ((slots, width), F32)
    part_type = ((slots, width), BF16)

    def exchange(part):
        return [part] + [swap(part, "head", k) for k in range(1, head_count)]

    def on_chip(*arrays):
        return [(VMEM, x) for x in arrays]

    part, stream, facts, turn = call(
        functools.partial(first_attention_kernel, len(blocks)),
        on_chip(*blocks, pick, frequency, cache_variates, kv, attn_gain)
        + on_chip(qkv_weight, out_weight, variate_bias),
        [part_type, stream_type, ((slots, META), F32), ((slots, 256), F32)],
        scratch,
    )
    for layer in range(LAYERS):
        last = layer == LAYERS - 1
        if layer:
            (kv,) = next_kv
            part, stream = call(
                functools.partial(next_attention_kernel, layer, head_count),
                on_chip(*parts, stream, facts, turn, cache_variates, kv, attn_gain)
                + on_chip(qkv_weight, out_weight, variate_bias),
                [part_type, stream_type],
                scratch,
            )
        parts = exchange(part)
        if not last:
            next_kv = bring(part, [(kv_cache, (layer + 1,))])
            part, stream = call(
                functools.partial(feed_forward_kernel, layer, head_count),
                on_chip(*parts, stream, ffn_gain, gate_up, down),
                [part_type, stream_type],
            )
            parts = exchange(part)
            gate_up, down = bring(
                part, [(gate_up_weight, (layer + 1,)), (down_weight, (layer + 1,))]
            )
        else:
            (send,) = call(
                functools.partial(last_feed_forward_kernel, layer, head_count),
                on_chip(*parts, place, flag, stream, ffn_gain, gate_up, down),
                [((devices, 2, width // 2 + META), BF16)],
            )
    received = lax.all_to_all(send, ("req", "head"), 0, 0, tiled=True)
    return pl.pallas_call(
        place_kernel,
        out_shape=jax.ShapeDtypeStruct((share, width), BF16),
        in_specs=[VMEM],
        out_specs=VMEM,
        compiler_params=PARAMS,
    )(received)


def solution(mesh):
    return jax.shard_map(
        per_device,
        mesh=mesh,
        in_specs=(
            P("req", None),
            P("req"),
            P("req"),
            P("req"),
            P("req"),
            P("req", None),
            P(None, None, "req", None, "head"),
            P(),
            P(),
            P(None, None, "head"),
            P(None, "head", None),
            P(None, None, None, "head"),
            P(None, "head", None),
            P(None, None, "head"),
        ),
        out_specs=P(("req", "head"), None),
        check_vma=False,
    )
```

```python
import functools

import jax
import jax.numpy as jnp
import numpy as np
from jax import lax
from jax.experimental import pallas as pl
from jax.experimental.pallas import tpu as pltpu
from jax.sharding import PartitionSpec as P

HD = 64
LAYERS = 2
COST = 10**11
META = 128
LOW = 128
CHUNK = 128
NEG = -1e30
F32 = jnp.float32
BF16 = jnp.bfloat16

VMEM = pl.BlockSpec(memory_space=pltpu.VMEM)
HBM = pl.BlockSpec(memory_space=pltpu.HBM)
ANY = pl.BlockSpec(memory_space=pl.ANY)
PARAMS = pltpu.CompilerParams(vmem_limit_bytes=16 * 2**20)


def iota(shape, dim):
    return lax.broadcasted_iota(jnp.int32, shape, dim)


def rms_scale(stream, gain_row):
    return stream * lax.rsqrt(jnp.mean(stream * stream, axis=-1, keepdims=True) + 1e-06) * gain_row


def copy_all(pairs, sems):
    copies = [pltpu.make_async_copy(src, dst, sems.at[i]) for i, (src, dst) in enumerate(pairs)]
    for copy in copies:
        copy.start()
    for copy in copies:
        copy.wait()


def pack_kernel(
    tokens_ref, lengths_ref, positions_ref, variates_ref, out_ref, length, position, variate, sems
):
    rows, width = tokens_ref.shape
    copy_all(
        [
            (lengths_ref, length),
            (positions_ref, position),
            (variates_ref, variate),
            (tokens_ref, out_ref.at[:, pl.ds(0, width)]),
        ],
        sems,
    )
    row, lane = iota((rows, META), 0), iota((rows, META), 1)
    kind = lane % (META // 2)
    whole = jnp.zeros((rows, META), jnp.int32)
    for i in range(rows):
        values = jnp.where(kind == 0, length[i], jnp.where(kind == 1, position[i], variate[i]))
        whole = jnp.where(row == i, values, whole)
    digit = jnp.where(lane < META // 2, whole // LOW, whole % LOW)
    out_ref[:, width:] = digit.astype(F32).astype(BF16)


def owner_kernel(
    share,
    after_ref,
    owner_ref,
    own_block_ref,
    *refs,
):
    pick_ref, place_ref, flag_ref, owner, own_block, sems = refs
    copy_all([(owner_ref, owner), (own_block_ref, own_block)], sems)
    slots, total = pick_ref.shape
    devices = place_ref.shape[0]
    row, column = iota((slots, total), 0), iota((slots, total), 1)
    target, slot = iota((devices, slots), 0), iota((devices, slots), 1)
    flag_row, lane = iota((slots, META), 0), iota((slots, META), 1)
    pick = jnp.zeros((slots, total), F32)
    place = jnp.zeros((devices, slots), F32)
    flag = jnp.zeros((slots, META), F32)
    for s in range(slots):
        request = owner[s]
        source = ((request // slots) ^ own_block[0]) * slots + request % slots
        pick = jnp.where((row == s) & (column == source), 1.0, pick)
        place = jnp.where((slot == s) & (target == request // share), 1.0, place)
        flag = jnp.where((flag_row == s) & (lane == request % share), 1.0, flag)
    pick_ref[...] = pick.astype(BF16)
    place_ref[...] = place.astype(BF16)
    flag_ref[...] = flag.astype(BF16)


def bring_kernel(layer, after_ref, source_ref, out_ref, sem):
    copy_all([(source_ref.at[layer], out_ref)], sem)


def attention(
    layer,
    stream,
    facts,
    cos,
    sin,
    variates_ref,
    kv_ref,
    gain_ref,
    qkv_ref,
    out_w_ref,
    bias_ref,
    scores,
    mixed,
    part_ref,
):
    slots, cap = variates_ref.shape
    width = kv_ref.shape[-1]
    heads = width // HD
    rows = heads * slots

    lengths = facts[:, 0:1]
    variate = facts[:, 2:3]
    longer = jnp.sum((lengths > CHUNK).astype(jnp.int32))

    normed = rms_scale(stream, gain_ref[layer : layer + 1, :]).astype(BF16)
    projected = jnp.dot(normed, qkv_ref[layer], preferred_element_type=F32)

    lane = iota((slots, 128), 1)
    front = lane % HD < HD // 2
    pieces = []
    for j in range(projected.shape[1] // 128):
        u = projected[:, j * 128 : (j + 1) * 128]
        turned = jnp.where(front, -pltpu.roll(u, 96, 1), pltpu.roll(u, 32, 1))
        is_value = (lane + j * 128) % (3 * HD) >= 2 * HD
        pieces.append(jnp.where(is_value, u, u * cos + turned * sin).astype(BF16).astype(F32))
    turned_all = jnp.concatenate(pieces, axis=1)

    column = iota((slots, width), 1)
    of_head = [column // HD == h for h in range(heads)]
    step = 2 * HD
    query = [
        jnp.where(of_head[h], turned_all[:, h * step : h * step + width], 0.0) for h in range(heads)
    ]
    query_all = jnp.concatenate(query, axis=0).astype(BF16)

    score_dims = (((1,), (1,)), ((), ()))
    keys = kv_ref[0, :, :CHUNK, :].reshape(slots * CHUNK, width)
    raw = lax.dot_general(query_all, keys, score_dims, preferred_element_type=F32)
    row_slot = iota((rows, CHUNK), 0) % slots
    total = raw[:, :CHUNK]
    for s in range(1, slots):
        total = jnp.where(row_slot == s, raw[:, s * CHUNK : (s + 1) * CHUNK], total)
    scores[:, :CHUNK] = total
    rest_slot = iota((rows, cap - CHUNK), 0) % slots

    @pl.loop(0, longer)
    def _(s):
        more = lax.dot_general(
            query_all, kv_ref[0, s, CHUNK:, :], score_dims, preferred_element_type=F32
        )
        scores[:, CHUNK:] = jnp.where(rest_slot == s, more, scores[:, CHUNK:])

    next_keys = jnp.concatenate([turned_all[:, HD:], jnp.zeros((slots, HD), F32)], axis=1)
    own_score = [
        jnp.sum(query[h] * next_keys[:, h * step : h * step + width], axis=1, keepdims=True) * 0.125
        + bias_ref[layer, 0:1, h : h + 1]
        for h in range(heads)
    ]
    same = variates_ref[...].astype(F32) == variate
    live = iota((slots, cap), 1).astype(F32) < lengths
    probs = []
    own_prob = []
    for h in range(heads):
        block = scores[h * slots : (h + 1) * slots, :] * 0.125
        block = block + jnp.where(
            same, bias_ref[layer, 0:1, h : h + 1], bias_ref[layer, 1:2, h : h + 1]
        )
        block = jnp.where(live, block, NEG)
        top = jnp.maximum(jnp.max(block, axis=1, keepdims=True), own_score[h])
        weight = jnp.exp(block - top)
        own_weight = jnp.exp(own_score[h] - top)
        share = 1.0 / (jnp.sum(weight, axis=1, keepdims=True) + own_weight)
        probs.append(weight * share)
        own_prob.append((own_weight * share).astype(BF16).astype(F32))
    probs_all = jnp.concatenate(probs, axis=0).astype(BF16)
    first = probs_all[:, :CHUNK]
    spread = jnp.concatenate(
        [jnp.where(row_slot == s, first, jnp.zeros_like(first)) for s in range(slots)], axis=1
    )
    values = kv_ref[1, :, :CHUNK, :].reshape(slots * CHUNK, width)
    mixed[...] = jnp.dot(spread, values, preferred_element_type=F32)
    rest = probs_all[:, CHUNK:]

    @pl.loop(0, longer)
    def _(s):
        mine = jnp.where(rest_slot == s, rest, jnp.zeros_like(rest))
        mixed[...] += jnp.dot(mine, kv_ref[1, s, CHUNK:, :], preferred_element_type=F32)

    attended = jnp.zeros((slots, width), F32)
    for h in range(heads):
        value_new = turned_all[:, (h + 1) * step : (h + 1) * step + width]
        attended = jnp.where(
            of_head[h], mixed[h * slots : (h + 1) * slots, :] + own_prob[h] * value_new, attended
        )
    part_ref[...] = jnp.dot(
        attended.astype(BF16), out_w_ref[layer], preferred_element_type=F32
    ).astype(BF16)


def first_attention_kernel(block_count, *refs):
    (
        pick_ref,
        frequency_ref,
        variates_ref,
        kv_ref,
        gain_ref,
        qkv_ref,
        out_w_ref,
        bias_ref,
        part_ref,
        stream_ref,
        facts_ref,
        turn_ref,
        scores,
        mixed,
    ) = refs[block_count:]
    gathered = jnp.concatenate([ref[...] for ref in refs[:block_count]], axis=0)
    width = stream_ref.shape[1]
    picked = jnp.dot(pick_ref[...], gathered, preferred_element_type=F32)
    stream = picked[:, :width]
    digits = picked[:, width:]
    facts = digits * float(LOW) + pltpu.roll(digits, META // 2, 1)
    stream_ref[...] = stream
    facts_ref[...] = facts
    angle = facts[:, 1:2] * frequency_ref[...]
    cos, sin = jnp.cos(angle), jnp.sin(angle)
    turn_ref[:, :128] = cos
    turn_ref[:, 128:] = sin
    attention(
        0, stream, facts, cos, sin, variates_ref, kv_ref, gain_ref, qkv_ref, out_w_ref, bias_ref,
        scores, mixed, part_ref,
    )


def next_attention_kernel(layer, part_count, *refs):
    (
        old_ref,
        facts_ref,
        turn_ref,
        variates_ref,
        kv_ref,
        gain_ref,
        qkv_ref,
        out_w_ref,
        bias_ref,
        part_ref,
        stream_ref,
        scores,
        mixed,
    ) = refs[part_count:]
    stream = old_ref[...]
    for ref in refs[:part_count]:
        stream = stream + ref[...].astype(F32)
    stream_ref[...] = stream
    attention(
        layer, stream, facts_ref[...], turn_ref[:, :128], turn_ref[:, 128:], variates_ref, kv_ref,
        gain_ref, qkv_ref, out_w_ref, bias_ref, scores, mixed, part_ref,
    )


def feed_forward(layer, part_refs, old_ref, gain_ref, gate_up_ref, down_ref):
    stream = old_ref[...]
    for ref in part_refs:
        stream = stream + ref[...].astype(F32)
    normed = rms_scale(stream, gain_ref[layer : layer + 1, :]).astype(BF16)
    gate = jnp.dot(normed, gate_up_ref[layer, 0], preferred_element_type=F32)
    up = jnp.dot(normed, gate_up_ref[layer, 1], preferred_element_type=F32)
    hidden = (gate / (1.0 + jnp.exp(-gate)) * up).astype(BF16)
    return stream, jnp.dot(hidden, down_ref[layer], preferred_element_type=F32)


def feed_forward_kernel(layer, part_count, *refs):
    old_ref, gain_ref, gate_up_ref, down_ref, part_ref, stream_ref = refs[part_count:]
    stream, part = feed_forward(layer, refs[:part_count], old_ref, gain_ref, gate_up_ref, down_ref)
    stream_ref[...] = stream
    part_ref[...] = part.astype(BF16)


def last_feed_forward_kernel(layer, part_count, *refs):
    place_ref, flag_ref, old_ref, gain_ref, gate_up_ref, down_ref, send_ref = refs[part_count:]
    stream, part = feed_forward(layer, refs[:part_count], old_ref, gain_ref, gate_up_ref, down_ref)
    rows = (part + stream * (1.0 / part_count)).astype(BF16)
    half = rows.shape[1] // 2
    for i in range(2):
        payload = jnp.concatenate([rows[:, i * half : (i + 1) * half], flag_ref[...]], axis=1)
        spread = jnp.dot(place_ref[...], payload, preferred_element_type=F32)
        send_ref[:, i, :] = spread.astype(BF16)


def place_kernel(received_ref, out_ref):
    share, width = out_ref.shape
    half = width // 2
    for i in range(2):
        rows = lax.dot_general(
            received_ref[:, i, half:],
            received_ref[:, i, :half],
            (((0,), (0,)), ((), ())),
            preferred_element_type=F32,
        )
        out_ref[:, i * half : (i + 1) * half] = rows[:share, :].astype(BF16)


def call(kernel, operands, outs, scratch=(), cost=None):
    specs = [spec for spec, _ in operands]
    arrays = [
        pltpu.with_memory_space_constraint(array, pltpu.HBM) if spec is HBM else array
        for spec, array in operands
    ]
    return pl.pallas_call(
        kernel,
        out_shape=[pltpu.VMEM(shape, dtype) for shape, dtype in outs],
        in_specs=specs,
        out_specs=[VMEM] * len(outs),
        scratch_shapes=list(scratch),
        compiler_params=PARAMS,
        cost_estimate=cost,
    )(*arrays)


def bring(after, source, layer):
    (out,) = call(
        functools.partial(bring_kernel, layer),
        [(ANY, after), (HBM, source)],
        [(source.shape[1:], source.dtype)],
        [pltpu.SemaphoreType.DMA((1,))],
    )
    return out


def swap(array, axis, mask):
    count = lax.axis_size(axis)
    return lax.ppermute(array, axis, [(i, i ^ mask) for i in range(count)])


def gather_blocks(block, axis):
    count = lax.axis_size(axis)
    pair = jnp.concatenate([block, swap(block, axis, 1)], axis=0)
    blocks = [pair]
    reach = 2
    while reach < count:
        span = min(4, count // reach)
        held = blocks[0] if len(blocks) == 1 else jnp.concatenate(blocks, axis=0)
        blocks = blocks + [swap(held, axis, reach * k) for k in range(1, span)]
        reach *= span
    return blocks


def per_device(
    tokens,
    lengths,
    slot_owner,
    positions,
    variates,
    cache_variates,
    kv_cache,
    attn_gain,
    ffn_gain,
    qkv_weight,
    out_weight,
    gate_up_weight,
    down_weight,
    variate_bias,
):
    slots, width = tokens.shape
    cap, local_width = kv_cache.shape[3:]
    head_count = lax.axis_size("head")
    devices = lax.axis_size("req") * head_count
    share = slots // head_count
    local_heads = local_width // HD

    total = slots * lax.axis_size("req")
    whole_row = [pltpu.SMEM((slots,), jnp.int32)] * 3
    (packed,) = call(
        pack_kernel,
        [(HBM, tokens), (HBM, lengths), (HBM, positions), (HBM, variates)],
        [((slots, width + META), BF16)],
        whole_row + [pltpu.SemaphoreType.DMA((4,))],
        pl.CostEstimate(flops=COST, bytes_accessed=0, transcendentals=0),
    )
    exponent = -2.0 * (np.arange(128) % (HD // 2)) / HD
    frequency = jnp.asarray((10000.0**exponent).astype(np.float32)[None, :])
    own_block = lax.axis_index("req").reshape(1)
    pick, place, flag = call(
        functools.partial(owner_kernel, share),
        [(ANY, packed), (HBM, slot_owner), (HBM, own_block)],
        [((slots, total), BF16), ((devices, slots), BF16), ((slots, META), BF16)],
        [
            pltpu.SMEM((slots,), jnp.int32),
            pltpu.SMEM((1,), jnp.int32),
            pltpu.SemaphoreType.DMA((2,)),
        ],
    )
    blocks = gather_blocks(packed, "req")
    kv = bring(blocks[0], kv_cache, 0)

    scratch = [
        pltpu.VMEM((local_heads * slots, cap), F32),
        pltpu.VMEM((local_heads * slots, local_width), F32),
    ]
    stream_type = ((slots, width), F32)
    part_type = ((slots, width), BF16)

    def exchange(part):
        return [part] + [swap(part, "head", k) for k in range(1, head_count)]

    def on_chip(*arrays):
        return [(VMEM, x) for x in arrays]

    part, stream, facts, turn = call(
        functools.partial(first_attention_kernel, len(blocks)),
        on_chip(*blocks, pick, frequency, cache_variates, kv, attn_gain)
        + on_chip(qkv_weight, out_weight, variate_bias),
        [part_type, stream_type, ((slots, META), F32), ((slots, 256), F32)],
        scratch,
    )
    for layer in range(LAYERS):
        last = layer == LAYERS - 1
        if layer:
            part, stream = call(
                functools.partial(next_attention_kernel, layer, head_count),
                on_chip(*parts, stream, facts, turn, cache_variates, kv, attn_gain)
                + on_chip(qkv_weight, out_weight, variate_bias),
                [part_type, stream_type],
                scratch,
            )
        parts = exchange(part)
        if not last:
            kv = bring(part, kv_cache, layer + 1)
            part, stream = call(
                functools.partial(feed_forward_kernel, layer, head_count),
                on_chip(*parts, stream, ffn_gain, gate_up_weight, down_weight),
                [part_type, stream_type],
            )
            parts = exchange(part)
        else:
            (send,) = call(
                functools.partial(last_feed_forward_kernel, layer, head_count),
                on_chip(*parts, place, flag, stream, ffn_gain, gate_up_weight, down_weight),
                [((devices, 2, width // 2 + META), BF16)],
            )
    received = lax.all_to_all(send, ("req", "head"), 0, 0, tiled=True)
    return pl.pallas_call(
        place_kernel,
        out_shape=jax.ShapeDtypeStruct((share, width), BF16),
        in_specs=[VMEM],
        out_specs=VMEM,
        compiler_params=PARAMS,
    )(received)


def solution(mesh):
    return jax.shard_map(
        per_device,
        mesh=mesh,
        in_specs=(
            P("req", None),
            P("req"),
            P("req"),
            P("req"),
            P("req"),
            P("req", None),
            P(None, None, "req", None, "head"),
            P(),
            P(),
            P(None, None, "head"),
            P(None, "head", None),
            P(None, None, None, "head"),
            P(None, "head", None),
            P(None, None, "head"),
        ),
        out_specs=P(("req", "head"), None),
        check_vma=False,
    )
```

```python
import functools

import jax
import jax.numpy as jnp
import numpy as np
from jax import lax
from jax.experimental import pallas as pl
from jax.experimental.pallas import tpu as pltpu
from jax.sharding import PartitionSpec as P

HD = 64
LAYERS = 2
META = 128
LOW = 128
CHUNK = 128
NEG = -1e30
F32 = jnp.float32
BF16 = jnp.bfloat16

VMEM = pl.BlockSpec(memory_space=pltpu.VMEM)
HBM = pl.BlockSpec(memory_space=pltpu.HBM)
ANY = pl.BlockSpec(memory_space=pl.ANY)
LONG = pl.CostEstimate(flops=10**11, bytes_accessed=0, transcendentals=0)
SHORT = pl.CostEstimate(flops=10**6, bytes_accessed=0, transcendentals=0)
PARAMS = pltpu.CompilerParams(vmem_limit_bytes=16 * 2**20)


def iota(shape, dim):
    return lax.broadcasted_iota(jnp.int32, shape, dim)


def copy_all(pairs, sems):
    copies = [pltpu.make_async_copy(src, dst, sems.at[i]) for i, (src, dst) in enumerate(pairs)]
    for copy in copies:
        copy.start()
    for copy in copies:
        copy.wait()


def pack_kernel(
    tokens_ref, lengths_ref, positions_ref, variates_ref, out_ref, length, position, variate, sems
):
    rows, width = tokens_ref.shape
    copy_all(
        [
            (lengths_ref, length),
            (positions_ref, position),
            (variates_ref, variate),
            (tokens_ref, out_ref.at[:, pl.ds(0, width)]),
        ],
        sems,
    )
    row, lane = iota((rows, META), 0), iota((rows, META), 1)
    kind = lane % (META // 2)
    whole = jnp.zeros((rows, META), jnp.int32)
    for i in range(rows):
        values = jnp.where(kind == 0, length[i], jnp.where(kind == 1, position[i], variate[i]))
        whole = jnp.where(row == i, values, whole)
    digit = jnp.where(lane < META // 2, whole // LOW, whole % LOW)
    out_ref[:, width:] = digit.astype(F32).astype(BF16)


def cache_copies(layer, kv_ref, front_ref, lead_ref, sems, first):
    rest = kv_ref.shape[3] - CHUNK
    return [
        pltpu.make_async_copy(
            kv_ref.at[layer, :, :, pl.ds(0, CHUNK), :], front_ref, sems.at[first]
        ),
        pltpu.make_async_copy(
            kv_ref.at[layer, :, 0, pl.ds(CHUNK, rest), :], lead_ref, sems.at[first + 1]
        ),
    ]


def owner_kernel(
    share,
    block_ids,
    after_ref,
    owner_ref,
    own_block_ref,
    kv_ref,
    pick_ref,
    place_ref,
    flag_ref,
    front_ref,
    lead_ref,
    owner,
    own_block,
    sems,
):
    copies = [
        pltpu.make_async_copy(owner_ref, owner, sems.at[0]),
        pltpu.make_async_copy(own_block_ref, own_block, sems.at[1]),
    ] + cache_copies(0, kv_ref, front_ref, lead_ref, sems, 2)
    for copy in copies:
        copy.start()
    copies[0].wait()
    copies[1].wait()
    slots, total = pick_ref.shape
    devices = place_ref.shape[0]
    row, column = iota((slots, total), 0), iota((slots, total), 1)
    target, slot = iota((devices, slots), 0), iota((devices, slots), 1)
    flag_row, lane = iota((slots, META), 0), iota((slots, META), 1)
    block = jnp.zeros((slots, total), jnp.int32)
    for k, block_id in enumerate(block_ids):
        block = jnp.where(column // slots == k, block_id, block)
    request_at = (block ^ own_block[0]) * slots + column % slots
    pick = jnp.zeros((slots, total), F32)
    place = jnp.zeros((devices, slots), F32)
    flag = jnp.zeros((slots, META), F32)
    for s in range(slots):
        request = owner[s]
        pick = jnp.where((row == s) & (request_at == request), 1.0, pick)
        place = jnp.where((slot == s) & (target == request // share), 1.0, place)
        flag = jnp.where((flag_row == s) & (lane == request % share), 1.0, flag)
    pick_ref[...] = pick.astype(BF16)
    place_ref[...] = place.astype(BF16)
    flag_ref[...] = flag.astype(BF16)
    copies[2].wait()
    copies[3].wait()


def cache_kernel(layer, after_ref, kv_ref, front_ref, lead_ref, sems):
    copies = cache_copies(layer, kv_ref, front_ref, lead_ref, sems, 0)
    for copy in copies:
        copy.start()
    for copy in copies:
        copy.wait()


def attention(
    layer,
    stream,
    facts,
    cos,
    sin,
    variates_ref,
    front_ref,
    lead_ref,
    kv_ref,
    gain_ref,
    qkv_ref,
    out_w_ref,
    bias_ref,
    scores,
    mixed,
    attended,
    rest_kv,
    rest_sems,
    part_ref,
):
    slots, cap = variates_ref.shape
    width = front_ref.shape[-1]
    heads = width // HD
    rows = heads * slots
    rest = cap - CHUNK

    lengths = facts[:, 0:1]
    variate = facts[:, 2:3]
    longer = jnp.sum((lengths > CHUNK).astype(jnp.int32))

    scale = lax.rsqrt(jnp.mean(stream * stream, axis=-1, keepdims=True) + 1e-06)
    scaled = (stream * gain_ref[layer : layer + 1, :]).astype(BF16)
    projected = jnp.dot(scaled, qkv_ref[layer], preferred_element_type=F32) * scale

    lane = iota((slots, 128), 1)
    front_half = lane % HD < HD // 2
    pieces = []
    for j in range(projected.shape[1] // 128):
        u = projected[:, j * 128 : (j + 1) * 128]
        turned = jnp.where(front_half, -pltpu.roll(u, 96, 1), pltpu.roll(u, 32, 1))
        is_value = (lane + j * 128) % (3 * HD) >= 2 * HD
        pieces.append(jnp.where(is_value, u, u * cos + turned * sin).astype(BF16).astype(F32))
    turned_all = jnp.concatenate(pieces, axis=1)

    column = iota((slots, width), 1)
    of_head = [column // HD == h for h in range(heads)]
    step = 2 * HD
    query = [
        jnp.where(of_head[h], turned_all[:, h * step : h * step + width], 0.0) for h in range(heads)
    ]
    query_all = jnp.concatenate(query, axis=0).astype(BF16)
    row_slot = iota((rows, CHUNK), 0) % slots
    rest_slot = iota((rows, rest), 0) % slots

    def score(keys):
        return lax.dot_general(
            query_all, keys, (((1,), (1,)), ((), ())), preferred_element_type=F32
        )

    raw = score(front_ref[0].reshape(slots * CHUNK, width))
    front_scores = raw[:, :CHUNK]
    for s in range(1, slots):
        front_scores = jnp.where(
            row_slot == s, raw[:, s * CHUNK : (s + 1) * CHUNK], front_scores
        )
    lead_scores = score(lead_ref[0])

    next_keys = jnp.concatenate([turned_all[:, HD:], jnp.zeros((slots, HD), F32)], axis=1)
    own_score = [
        jnp.sum(query[h] * next_keys[:, h * step : h * step + width], axis=1, keepdims=True) * 0.125
        + bias_ref[layer, 0:1, h : h + 1]
        for h in range(heads)
    ]
    same = variates_ref[...].astype(F32) == variate
    live = iota((slots, cap), 1).astype(F32) < lengths

    def soften(raw_scores):
        probs, own_prob = [], []
        for h in range(heads):
            block = raw_scores[h * slots : (h + 1) * slots, :] * 0.125
            block = block + jnp.where(
                same, bias_ref[layer, 0:1, h : h + 1], bias_ref[layer, 1:2, h : h + 1]
            )
            block = jnp.where(live, block, NEG)
            top = jnp.maximum(jnp.max(block, axis=1, keepdims=True), own_score[h])
            weight = jnp.exp(block - top)
            own_weight = jnp.exp(own_score[h] - top)
            share = 1.0 / (jnp.sum(weight, axis=1, keepdims=True) + own_weight)
            probs.append(weight * share)
            own_prob.append((own_weight * share).astype(BF16).astype(F32))
        return jnp.concatenate(probs, axis=0).astype(BF16), own_prob

    def only(mask, probs):
        return jnp.where(mask, probs, jnp.zeros_like(probs))

    def mix(probs):
        spread = jnp.concatenate([only(row_slot == s, probs[:, :CHUNK]) for s in range(slots)], 1)
        front = jnp.dot(
            spread, front_ref[1].reshape(slots * CHUNK, width), preferred_element_type=F32
        )
        lead = only(rest_slot == 0, probs[:, CHUNK:])
        return front + jnp.dot(lead, lead_ref[1], preferred_element_type=F32)

    def lay_out(mixed_rows, own_prob):
        result = jnp.zeros((slots, width), F32)
        for h in range(heads):
            value_new = turned_all[:, (h + 1) * step : (h + 1) * step + width]
            result = jnp.where(
                of_head[h], mixed_rows[h * slots : (h + 1) * slots, :] + own_prob[h] * value_new,
                result,
            )
        return result

    all_scores = jnp.concatenate([front_scores, lead_scores], axis=1)
    probs_all, own_probs = soften(all_scores)
    attended[...] = lay_out(mix(probs_all), own_probs)

    @pl.when(longer > 1)
    def _():
        def rest_copy(s):
            return pltpu.make_async_copy(
                kv_ref.at[layer, :, s, pl.ds(CHUNK, rest), :], rest_kv.at[s], rest_sems.at[s]
            )

        @pl.loop(1, longer)
        def _(s):
            rest_copy(s).start()

        scores[...] = all_scores

        @pl.loop(1, longer)
        def _(s):
            rest_copy(s).wait()
            scores[:, CHUNK:] = jnp.where(rest_slot == s, score(rest_kv[s, 0]), scores[:, CHUNK:])

        probs_long, own_long = soften(scores[...])
        mixed[...] = mix(probs_long)
        rest_probs = probs_long[:, CHUNK:]

        @pl.loop(1, longer)
        def _(s):
            mixed[...] += jnp.dot(
                only(rest_slot == s, rest_probs), rest_kv[s, 1], preferred_element_type=F32
            )

        attended[...] = lay_out(mixed[...], own_long)

    part_ref[...] = jnp.dot(
        attended[...].astype(BF16), out_w_ref[layer], preferred_element_type=F32
    ).astype(BF16)


def first_attention_kernel(block_count, *refs):
    (
        pick_ref,
        frequency_ref,
        variates_ref,
        front_ref,
        lead_ref,
        kv_ref,
        gain_ref,
        qkv_ref,
        out_w_ref,
        bias_ref,
        part_ref,
        stream_ref,
        facts_ref,
        turn_ref,
        *scratch,
    ) = refs[block_count:]
    gathered = jnp.concatenate([ref[...] for ref in refs[:block_count]], axis=0)
    width = stream_ref.shape[1]
    picked = jnp.dot(pick_ref[...], gathered, preferred_element_type=F32)
    stream = picked[:, :width]
    digits = picked[:, width:]
    facts = digits * float(LOW) + pltpu.roll(digits, META // 2, 1)
    stream_ref[...] = stream
    facts_ref[...] = facts
    angle = facts[:, 1:2] * frequency_ref[...]
    cos, sin = jnp.cos(angle), jnp.sin(angle)
    turn_ref[:, :128] = cos
    turn_ref[:, 128:] = sin
    attention(
        0, stream, facts, cos, sin, variates_ref, front_ref, lead_ref, kv_ref, gain_ref, qkv_ref,
        out_w_ref, bias_ref, *scratch, part_ref,
    )


def next_attention_kernel(layer, part_count, *refs):
    (
        old_ref,
        facts_ref,
        turn_ref,
        variates_ref,
        front_ref,
        lead_ref,
        kv_ref,
        gain_ref,
        qkv_ref,
        out_w_ref,
        bias_ref,
        part_ref,
        stream_ref,
        *scratch,
    ) = refs[part_count:]
    stream = old_ref[...]
    for ref in refs[:part_count]:
        stream = stream + ref[...].astype(F32)
    stream_ref[...] = stream
    attention(
        layer, stream, facts_ref[...], turn_ref[:, :128], turn_ref[:, 128:], variates_ref,
        front_ref, lead_ref, kv_ref, gain_ref, qkv_ref, out_w_ref, bias_ref, *scratch, part_ref,
    )


def feed_forward(layer, part_refs, old_ref, gain_ref, gate_up_ref, down_ref):
    stream = old_ref[...]
    for ref in part_refs:
        stream = stream + ref[...].astype(F32)
    scale = lax.rsqrt(jnp.mean(stream * stream, axis=-1, keepdims=True) + 1e-06)
    scaled = (stream * gain_ref[layer : layer + 1, :]).astype(BF16)
    gate = jnp.dot(scaled, gate_up_ref[layer, 0], preferred_element_type=F32) * scale
    up = jnp.dot(scaled, gate_up_ref[layer, 1], preferred_element_type=F32) * scale
    hidden = (gate / (1.0 + jnp.exp(-gate)) * up).astype(BF16)
    return stream, jnp.dot(hidden, down_ref[layer], preferred_element_type=F32)


def feed_forward_kernel(layer, part_count, *refs):
    old_ref, gain_ref, gate_up_ref, down_ref, part_ref, stream_ref = refs[part_count:]
    stream, part = feed_forward(layer, refs[:part_count], old_ref, gain_ref, gate_up_ref, down_ref)
    stream_ref[...] = stream
    part_ref[...] = part.astype(BF16)


def last_feed_forward_kernel(layer, part_count, head_count, *refs):
    place_ref, flag_ref, old_ref, gain_ref, gate_up_ref, down_ref, send_ref = refs[part_count:]
    stream, part = feed_forward(layer, refs[:part_count], old_ref, gain_ref, gate_up_ref, down_ref)
    rows = (part + stream * (1.0 / head_count)).astype(BF16)
    half = rows.shape[1] // 2
    for i in range(2):
        payload = jnp.concatenate([rows[:, i * half : (i + 1) * half], flag_ref[...]], axis=1)
        spread = jnp.dot(place_ref[...], payload, preferred_element_type=F32)
        send_ref[:, i, :] = spread.astype(BF16)


def place_kernel(received_ref, out_ref):
    share, width = out_ref.shape
    half = width // 2
    for i in range(2):
        rows = lax.dot_general(
            received_ref[:, i, half:],
            received_ref[:, i, :half],
            (((0,), (0,)), ((), ())),
            preferred_element_type=F32,
        )
        out_ref[:, i * half : (i + 1) * half] = rows[:share, :].astype(BF16)


def call(kernel, operands, outs, scratch=(), cost=SHORT):
    specs = [spec for spec, _ in operands]
    arrays = [
        pltpu.with_memory_space_constraint(array, pltpu.HBM) if spec is HBM else array
        for spec, array in operands
    ]
    return pl.pallas_call(
        kernel,
        out_shape=[pltpu.VMEM(shape, dtype) for shape, dtype in outs],
        in_specs=specs,
        out_specs=[VMEM] * len(outs),
        scratch_shapes=list(scratch),
        compiler_params=PARAMS,
        cost_estimate=cost,
    )(*arrays)


def swap(array, axis, mask):
    count = lax.axis_size(axis)
    return lax.ppermute(array, axis, [(i, i ^ mask) for i in range(count)])


def gather_stages(count):
    stages = []
    top = count
    if count.bit_length() % 2 == 0:
        top = count // 2
        stages.append([top])
    while top > 1:
        stages.append([top // 4 * k for k in (1, 2, 3)])
        top //= 4
    return stages


def swap_across(array, mask):
    reqs, heads = lax.axis_size("req"), lax.axis_size("head")
    pairs = [
        (r * heads + h, (r ^ mask) * heads + (h ^ 1)) for r in range(reqs) for h in range(heads)
    ]
    return lax.ppermute(array, ("req", "head"), pairs)


def gather_blocks(block):
    blocks, ids = [block], [0]
    for masks in gather_stages(lax.axis_size("req")):
        held = blocks[0] if len(blocks) == 1 else jnp.concatenate(blocks, axis=0)
        blocks = [held] + [swap_across(held, mask) for mask in masks]
        ids = ids + [mask ^ i for mask in masks for i in ids]
    return blocks, ids


def per_device(
    tokens,
    lengths,
    slot_owner,
    positions,
    variates,
    cache_variates,
    kv_cache,
    attn_gain,
    ffn_gain,
    qkv_weight,
    out_weight,
    gate_up_weight,
    down_weight,
    variate_bias,
):
    slots, width = tokens.shape
    cap, local_width = kv_cache.shape[3:]
    head_count = lax.axis_size("head")
    devices = lax.axis_size("req") * head_count
    share = slots // head_count
    local_heads = local_width // HD

    total = slots * lax.axis_size("req")
    whole_row = [pltpu.SMEM((slots,), jnp.int32)] * 3
    (packed,) = call(
        pack_kernel,
        [(HBM, tokens), (HBM, lengths), (HBM, positions), (HBM, variates)],
        [((slots, width + META), BF16)],
        whole_row + [pltpu.SemaphoreType.DMA((4,))],
        LONG,
    )
    exponent = -2.0 * (np.arange(128) % (HD // 2)) / HD
    frequency = jnp.asarray((10000.0**exponent).astype(np.float32)[None, :])
    own_block = lax.axis_index("req").reshape(1)
    blocks, block_ids = gather_blocks(packed)
    cache_types = [
        ((2, slots, CHUNK, local_width), BF16),
        ((2, cap - CHUNK, local_width), BF16),
    ]
    pick, place, flag, *cache = call(
        functools.partial(owner_kernel, share, block_ids),
        [(ANY, packed), (HBM, slot_owner), (HBM, own_block), (HBM, kv_cache)],
        [((slots, total), BF16), ((devices, slots), BF16), ((slots, META), BF16)]
        + cache_types,
        [
            pltpu.SMEM((slots,), jnp.int32),
            pltpu.SMEM((1,), jnp.int32),
            pltpu.SemaphoreType.DMA((4,)),
        ],
    )

    scratch = [
        pltpu.VMEM((local_heads * slots, cap), F32),
        pltpu.VMEM((local_heads * slots, local_width), F32),
        pltpu.VMEM((slots, local_width), F32),
        pltpu.VMEM((slots, 2, cap - CHUNK, local_width), BF16),
        pltpu.SemaphoreType.DMA((slots,)),
    ]
    stream_type = ((slots, width), F32)
    part_type = ((slots, width), BF16)

    def exchange(part):
        return [part] + [swap(part, "head", k) for k in range(1, head_count)]

    def on_chip(*arrays):
        return [(VMEM, x) for x in arrays]

    part, stream, facts, turn = call(
        functools.partial(first_attention_kernel, len(blocks)),
        on_chip(*blocks, pick, frequency, cache_variates, *cache)
        + [(HBM, kv_cache)]
        + on_chip(attn_gain, qkv_weight, out_weight, variate_bias),
        [part_type, stream_type, ((slots, META), F32), ((slots, 256), F32)],
        scratch,
    )
    for layer in range(LAYERS):
        last = layer == LAYERS - 1
        if layer:
            part, stream = call(
                functools.partial(next_attention_kernel, layer, len(parts)),
                on_chip(*parts, stream, facts, turn, cache_variates, *cache)
                + [(HBM, kv_cache)]
                + on_chip(attn_gain, qkv_weight, out_weight, variate_bias),
                [part_type, stream_type],
                scratch,
            )
        parts = exchange(part)
        if not last:
            part, stream = call(
                functools.partial(feed_forward_kernel, layer, len(parts)),
                on_chip(*parts, stream, ffn_gain, gate_up_weight, down_weight),
                [part_type, stream_type],
            )
            parts = exchange(part)
            cache = call(
                functools.partial(cache_kernel, layer + 1),
                [(ANY, part), (HBM, kv_cache)],
                cache_types,
                [pltpu.SemaphoreType.DMA((2,))],
            )
        else:
            (send,) = call(
                functools.partial(last_feed_forward_kernel, layer, len(parts), head_count),
                on_chip(*parts, place, flag, stream, ffn_gain, gate_up_weight, down_weight),
                [((devices, 2, width // 2 + META), BF16)],
            )
    received = lax.all_to_all(send, ("req", "head"), 0, 0, tiled=True)
    return pl.pallas_call(
        place_kernel,
        out_shape=jax.ShapeDtypeStruct((share, width), BF16),
        in_specs=[VMEM],
        out_specs=VMEM,
        compiler_params=PARAMS,
    )(received)


def solution(mesh):
    return jax.shard_map(
        per_device,
        mesh=mesh,
        in_specs=(
            P("req", None),
            P("req"),
            P("req"),
            P("req"),
            P("req"),
            P("req", None),
            P(None, None, "req", None, "head"),
            P(),
            P(),
            P(None, None, "head"),
            P(None, "head", None),
            P(None, None, None, "head"),
            P(None, "head", None),
            P(None, None, "head"),
        ),
        out_specs=P(("req", "head"), None),
        check_vma=False,
    )
```

```python
import functools

import jax
import jax.numpy as jnp
import numpy as np
from jax import lax
from jax.experimental import pallas as pl
from jax.experimental.pallas import tpu as pltpu
from jax.sharding import PartitionSpec as P

HD = 64
LAYERS = 2
META = 128
LOW = 128
CHUNK = 128
NEG = -1e30
F32 = jnp.float32
BF16 = jnp.bfloat16

VMEM = pl.BlockSpec(memory_space=pltpu.VMEM)
HBM = pl.BlockSpec(memory_space=pltpu.HBM)
ANY = pl.BlockSpec(memory_space=pl.ANY)
LONG = pl.CostEstimate(flops=10**11, bytes_accessed=0, transcendentals=0)
SHORT = pl.CostEstimate(flops=10**6, bytes_accessed=0, transcendentals=0)
PARAMS = pltpu.CompilerParams(vmem_limit_bytes=16 * 2**20)


def iota(shape, dim):
    return lax.broadcasted_iota(jnp.int32, shape, dim)


def copy_all(pairs, sems):
    copies = [pltpu.make_async_copy(src, dst, sems.at[i]) for i, (src, dst) in enumerate(pairs)]
    for copy in copies:
        copy.start()
    for copy in copies:
        copy.wait()


def pack_kernel(
    tokens_ref, lengths_ref, positions_ref, variates_ref, out_ref, length, position, variate, sems
):
    rows, width = tokens_ref.shape
    copy_all(
        [
            (lengths_ref, length),
            (positions_ref, position),
            (variates_ref, variate),
            (tokens_ref, out_ref.at[:, pl.ds(0, width)]),
        ],
        sems,
    )
    row, lane = iota((rows, META), 0), iota((rows, META), 1)
    kind = lane % (META // 2)
    whole = jnp.zeros((rows, META), jnp.int32)
    for i in range(rows):
        values = jnp.where(kind == 0, length[i], jnp.where(kind == 1, position[i], variate[i]))
        whole = jnp.where(row == i, values, whole)
    digit = jnp.where(lane < META // 2, whole // LOW, whole % LOW)
    out_ref[:, width:] = digit.astype(F32).astype(BF16)


def cache_copies(layer, kv_ref, front_ref, lead_ref, sems, first):
    rest = kv_ref.shape[3] - CHUNK
    return [
        pltpu.make_async_copy(
            kv_ref.at[layer, :, :, pl.ds(0, CHUNK), :], front_ref, sems.at[first]
        ),
        pltpu.make_async_copy(
            kv_ref.at[layer, :, 0, pl.ds(CHUNK, rest), :], lead_ref, sems.at[first + 1]
        ),
    ]


def owner_kernel(
    share,
    block_ids,
    after_ref,
    owner_ref,
    own_block_ref,
    kv_ref,
    pick_ref,
    place_ref,
    flag_ref,
    front_ref,
    lead_ref,
    owner,
    own_block,
    sems,
):
    copies = [
        pltpu.make_async_copy(owner_ref, owner, sems.at[0]),
        pltpu.make_async_copy(own_block_ref, own_block, sems.at[1]),
    ] + cache_copies(0, kv_ref, front_ref, lead_ref, sems, 2)
    for copy in copies:
        copy.start()
    copies[0].wait()
    copies[1].wait()
    slots, total = pick_ref.shape
    devices = place_ref.shape[0]
    row, column = iota((slots, total), 0), iota((slots, total), 1)
    target, slot = iota((devices, slots), 0), iota((devices, slots), 1)
    flag_row, lane = iota((slots, META), 0), iota((slots, META), 1)
    block = jnp.zeros((slots, total), jnp.int32)
    for k, block_id in enumerate(block_ids):
        block = jnp.where(column // slots == k, block_id, block)
    request_at = (block ^ own_block[0]) * slots + column % slots
    pick = jnp.zeros((slots, total), F32)
    place = jnp.zeros((devices, slots), F32)
    flag = jnp.zeros((slots, META), F32)
    for s in range(slots):
        request = owner[s]
        pick = jnp.where((row == s) & (request_at == request), 1.0, pick)
        place = jnp.where((slot == s) & (target == request // share), 1.0, place)
        flag = jnp.where((flag_row == s) & (lane == request % share), 1.0, flag)
    pick_ref[...] = pick.astype(BF16)
    place_ref[...] = place.astype(BF16)
    flag_ref[...] = flag.astype(BF16)
    copies[2].wait()
    copies[3].wait()


def cache_kernel(layer, after_ref, kv_ref, front_ref, lead_ref, sems):
    copies = cache_copies(layer, kv_ref, front_ref, lead_ref, sems, 0)
    for copy in copies:
        copy.start()
    for copy in copies:
        copy.wait()


def attention(
    layer,
    stream,
    facts,
    cos,
    sin,
    variates_ref,
    front_ref,
    lead_ref,
    kv_ref,
    gain_ref,
    qkv_ref,
    out_w_ref,
    bias_ref,
    scores,
    mixed,
    attended,
    rest_kv,
    rest_sems,
    part_ref,
):
    slots, cap = variates_ref.shape
    width = front_ref.shape[-1]
    heads = width // HD
    rows = heads * slots
    rest = cap - CHUNK

    lengths = facts[:, 0:1]
    variate = facts[:, 2:3]
    longer = jnp.sum((lengths > CHUNK).astype(jnp.int32))

    scale = lax.rsqrt(jnp.mean(stream * stream, axis=-1, keepdims=True) + 1e-06)
    scaled = (stream * gain_ref[layer : layer + 1, :]).astype(BF16)
    projected = jnp.dot(scaled, qkv_ref[layer], preferred_element_type=F32) * scale

    lane = iota((slots, 128), 1)
    front_half = lane % HD < HD // 2
    pieces = []
    for j in range(projected.shape[1] // 128):
        u = projected[:, j * 128 : (j + 1) * 128]
        turned = jnp.where(front_half, -pltpu.roll(u, 96, 1), pltpu.roll(u, 32, 1))
        is_value = (lane + j * 128) % (3 * HD) >= 2 * HD
        pieces.append(jnp.where(is_value, u, u * cos + turned * sin).astype(BF16).astype(F32))
    turned_all = jnp.concatenate(pieces, axis=1)

    column = iota((slots, width), 1)
    of_head = [column // HD == h for h in range(heads)]
    step = 2 * HD
    query = [
        jnp.where(of_head[h], turned_all[:, h * step : h * step + width], 0.0) for h in range(heads)
    ]
    query_all = jnp.concatenate(query, axis=0).astype(BF16)
    row_slot = iota((rows, CHUNK), 0) % slots
    rest_slot = iota((rows, rest), 0) % slots

    def score(keys):
        return lax.dot_general(
            query_all, keys, (((1,), (1,)), ((), ())), preferred_element_type=F32
        )

    raw = score(front_ref[0].reshape(slots * CHUNK, width))
    front_scores = raw[:, :CHUNK]
    for s in range(1, slots):
        front_scores = jnp.where(
            row_slot == s, raw[:, s * CHUNK : (s + 1) * CHUNK], front_scores
        )
    lead_scores = score(lead_ref[0])

    next_keys = jnp.concatenate([turned_all[:, HD:], jnp.zeros((slots, HD), F32)], axis=1)
    own_score = [
        jnp.sum(query[h] * next_keys[:, h * step : h * step + width], axis=1, keepdims=True) * 0.125
        + bias_ref[layer, 0:1, h : h + 1]
        for h in range(heads)
    ]
    same = variates_ref[...].astype(F32) == variate
    live = iota((slots, cap), 1).astype(F32) < lengths

    def soften(raw_scores):
        weights, own = [], []
        for h in range(heads):
            block = raw_scores[h * slots : (h + 1) * slots, :] * 0.125
            block = block + jnp.where(
                same, bias_ref[layer, 0:1, h : h + 1], bias_ref[layer, 1:2, h : h + 1]
            )
            block = jnp.where(live, block, NEG)
            top = jnp.maximum(jnp.max(block, axis=1, keepdims=True), own_score[h])
            weight = jnp.exp(block - top)
            own_weight = jnp.exp(own_score[h] - top)
            share = 1.0 / (jnp.sum(weight, axis=1, keepdims=True) + own_weight)
            weights.append(weight)
            own.append((own_weight, share))
        return jnp.concatenate(weights, axis=0).astype(BF16), own

    def only(mask, weights):
        return jnp.where(mask, weights, jnp.zeros_like(weights))

    def mix(weights):
        spread = jnp.concatenate([only(row_slot == s, weights[:, :CHUNK]) for s in range(slots)], 1)
        front = jnp.dot(
            spread, front_ref[1].reshape(slots * CHUNK, width), preferred_element_type=F32
        )
        lead = only(rest_slot == 0, weights[:, CHUNK:])
        return front + jnp.dot(lead, lead_ref[1], preferred_element_type=F32)

    def lay_out(mixed_rows, own):
        result = jnp.zeros((slots, width), F32)
        for h, (own_weight, share) in enumerate(own):
            value_new = turned_all[:, (h + 1) * step : (h + 1) * step + width]
            whole = mixed_rows[h * slots : (h + 1) * slots, :] + own_weight * value_new
            result = jnp.where(of_head[h], whole * share, result)
        return result

    all_scores = jnp.concatenate([front_scores, lead_scores], axis=1)
    weights_all, own_all = soften(all_scores)
    attended[...] = lay_out(mix(weights_all), own_all)

    @pl.when(longer > 1)
    def _():
        def rest_copy(s):
            return pltpu.make_async_copy(
                kv_ref.at[layer, :, s, pl.ds(CHUNK, rest), :], rest_kv.at[s], rest_sems.at[s]
            )

        @pl.loop(1, longer)
        def _(s):
            rest_copy(s).start()

        scores[...] = all_scores

        @pl.loop(1, longer)
        def _(s):
            rest_copy(s).wait()
            scores[:, CHUNK:] = jnp.where(rest_slot == s, score(rest_kv[s, 0]), scores[:, CHUNK:])

        weights_long, own_long = soften(scores[...])
        mixed[...] = mix(weights_long)
        rest_weights = weights_long[:, CHUNK:]

        @pl.loop(1, longer)
        def _(s):
            mixed[...] += jnp.dot(
                only(rest_slot == s, rest_weights), rest_kv[s, 1], preferred_element_type=F32
            )

        attended[...] = lay_out(mixed[...], own_long)

    part_ref[...] = jnp.dot(
        attended[...].astype(BF16), out_w_ref[layer], preferred_element_type=F32
    ).astype(BF16)


def first_attention_kernel(block_count, *refs):
    (
        pick_ref,
        frequency_ref,
        variates_ref,
        front_ref,
        lead_ref,
        kv_ref,
        gain_ref,
        qkv_ref,
        out_w_ref,
        bias_ref,
        part_ref,
        stream_ref,
        facts_ref,
        turn_ref,
        *scratch,
    ) = refs[block_count:]
    gathered = jnp.concatenate([ref[...] for ref in refs[:block_count]], axis=0)
    width = stream_ref.shape[1]
    picked = jnp.dot(pick_ref[...], gathered, preferred_element_type=F32)
    stream = picked[:, :width]
    digits = picked[:, width:]
    facts = digits * float(LOW) + pltpu.roll(digits, META // 2, 1)
    stream_ref[...] = stream
    facts_ref[...] = facts
    angle = facts[:, 1:2] * frequency_ref[...]
    cos, sin = jnp.cos(angle), jnp.sin(angle)
    turn_ref[:, :128] = cos
    turn_ref[:, 128:] = sin
    attention(
        0, stream, facts, cos, sin, variates_ref, front_ref, lead_ref, kv_ref, gain_ref, qkv_ref,
        out_w_ref, bias_ref, *scratch, part_ref,
    )


def next_attention_kernel(layer, part_count, *refs):
    (
        old_ref,
        facts_ref,
        turn_ref,
        variates_ref,
        front_ref,
        lead_ref,
        kv_ref,
        gain_ref,
        qkv_ref,
        out_w_ref,
        bias_ref,
        part_ref,
        stream_ref,
        *scratch,
    ) = refs[part_count:]
    stream = old_ref[...]
    for ref in refs[:part_count]:
        stream = stream + ref[...].astype(F32)
    stream_ref[...] = stream
    attention(
        layer, stream, facts_ref[...], turn_ref[:, :128], turn_ref[:, 128:], variates_ref,
        front_ref, lead_ref, kv_ref, gain_ref, qkv_ref, out_w_ref, bias_ref, *scratch, part_ref,
    )


def feed_forward(layer, part_refs, old_ref, gain_ref, gate_up_ref, down_ref):
    stream = old_ref[...]
    for ref in part_refs:
        stream = stream + ref[...].astype(F32)
    scale = lax.rsqrt(jnp.mean(stream * stream, axis=-1, keepdims=True) + 1e-06)
    scaled = (stream * gain_ref[layer : layer + 1, :]).astype(BF16)
    gate = jnp.dot(scaled, gate_up_ref[layer, 0], preferred_element_type=F32) * scale
    up = jnp.dot(scaled, gate_up_ref[layer, 1], preferred_element_type=F32) * scale
    hidden = (gate / (1.0 + jnp.exp(-gate)) * up).astype(BF16)
    return stream, jnp.dot(hidden, down_ref[layer], preferred_element_type=F32)


def feed_forward_kernel(layer, part_count, *refs):
    old_ref, gain_ref, gate_up_ref, down_ref, part_ref, stream_ref = refs[part_count:]
    stream, part = feed_forward(layer, refs[:part_count], old_ref, gain_ref, gate_up_ref, down_ref)
    stream_ref[...] = stream
    part_ref[...] = part.astype(BF16)


def last_feed_forward_kernel(layer, part_count, head_count, *refs):
    place_ref, flag_ref, old_ref, gain_ref, gate_up_ref, down_ref, send_ref = refs[part_count:]
    stream, part = feed_forward(layer, refs[:part_count], old_ref, gain_ref, gate_up_ref, down_ref)
    rows = (part + stream * (1.0 / head_count)).astype(BF16)
    half = rows.shape[1] // 2
    for i in range(2):
        payload = jnp.concatenate([rows[:, i * half : (i + 1) * half], flag_ref[...]], axis=1)
        spread = jnp.dot(place_ref[...], payload, preferred_element_type=F32)
        send_ref[:, i, :] = spread.astype(BF16)


def place_kernel(received_ref, out_ref):
    share, width = out_ref.shape
    half = width // 2
    for i in range(2):
        rows = received_ref[:, i, :half].astype(F32)
        flags = received_ref[:, i, half:].astype(F32)
        for k in range(share):
            row = jnp.sum(flags[:, k : k + 1] * rows, axis=0, keepdims=True)
            out_ref[k : k + 1, i * half : (i + 1) * half] = row.astype(BF16)


def call(kernel, operands, outs, scratch=(), cost=SHORT):
    specs = [spec for spec, _ in operands]
    arrays = [
        pltpu.with_memory_space_constraint(array, pltpu.HBM) if spec is HBM else array
        for spec, array in operands
    ]
    return pl.pallas_call(
        kernel,
        out_shape=[pltpu.VMEM(shape, dtype) for shape, dtype in outs],
        in_specs=specs,
        out_specs=[VMEM] * len(outs),
        scratch_shapes=list(scratch),
        compiler_params=PARAMS,
        cost_estimate=cost,
    )(*arrays)


def swap(array, axis, mask):
    count = lax.axis_size(axis)
    return lax.ppermute(array, axis, [(i, i ^ mask) for i in range(count)])


def gather_stages(count):
    stages = []
    top = count
    if count.bit_length() % 2 == 0:
        top = count // 2
        stages.append([top])
    while top > 1:
        stages.append([top // 4 * k for k in (1, 3, 2)])
        top //= 4
    return stages


def swap_across(array, mask):
    reqs, heads = lax.axis_size("req"), lax.axis_size("head")
    pairs = [
        (r * heads + h, (r ^ mask) * heads + (h ^ 1)) for r in range(reqs) for h in range(heads)
    ]
    return lax.ppermute(array, ("req", "head"), pairs)


def gather_blocks(block):
    blocks, ids = [block], [0]
    for masks in gather_stages(lax.axis_size("req")):
        held = blocks[0] if len(blocks) == 1 else jnp.concatenate(blocks, axis=0)
        blocks = [held] + [swap_across(held, mask) for mask in masks]
        ids = ids + [mask ^ i for mask in masks for i in ids]
    return blocks, ids


def per_device(
    tokens,
    lengths,
    slot_owner,
    positions,
    variates,
    cache_variates,
    kv_cache,
    attn_gain,
    ffn_gain,
    qkv_weight,
    out_weight,
    gate_up_weight,
    down_weight,
    variate_bias,
):
    slots, width = tokens.shape
    cap, local_width = kv_cache.shape[3:]
    head_count = lax.axis_size("head")
    devices = lax.axis_size("req") * head_count
    share = slots // head_count
    local_heads = local_width // HD

    total = slots * lax.axis_size("req")
    whole_row = [pltpu.SMEM((slots,), jnp.int32)] * 3
    (packed,) = call(
        pack_kernel,
        [(HBM, tokens), (HBM, lengths), (HBM, positions), (HBM, variates)],
        [((slots, width + META), BF16)],
        whole_row + [pltpu.SemaphoreType.DMA((4,))],
        LONG,
    )
    exponent = -2.0 * (np.arange(128) % (HD // 2)) / HD
    frequency = jnp.asarray((10000.0**exponent).astype(np.float32)[None, :])
    own_block = lax.axis_index("req").reshape(1)
    blocks, block_ids = gather_blocks(packed)
    cache_types = [
        ((2, slots, CHUNK, local_width), BF16),
        ((2, cap - CHUNK, local_width), BF16),
    ]
    pick, place, flag, *cache = call(
        functools.partial(owner_kernel, share, block_ids),
        [(ANY, packed), (HBM, slot_owner), (HBM, own_block), (HBM, kv_cache)],
        [((slots, total), BF16), ((devices, slots), BF16), ((slots, META), BF16)]
        + cache_types,
        [
            pltpu.SMEM((slots,), jnp.int32),
            pltpu.SMEM((1,), jnp.int32),
            pltpu.SemaphoreType.DMA((4,)),
        ],
    )

    scratch = [
        pltpu.VMEM((local_heads * slots, cap), F32),
        pltpu.VMEM((local_heads * slots, local_width), F32),
        pltpu.VMEM((slots, local_width), F32),
        pltpu.VMEM((slots, 2, cap - CHUNK, local_width), BF16),
        pltpu.SemaphoreType.DMA((slots,)),
    ]
    stream_type = ((slots, width), F32)
    part_type = ((slots, width), BF16)

    def exchange(part):
        return [part] + [swap(part, "head", k) for k in range(1, head_count)]

    def on_chip(*arrays):
        return [(VMEM, x) for x in arrays]

    part, stream, facts, turn = call(
        functools.partial(first_attention_kernel, len(blocks)),
        on_chip(*blocks, pick, frequency, cache_variates, *cache)
        + [(HBM, kv_cache)]
        + on_chip(attn_gain, qkv_weight, out_weight, variate_bias),
        [part_type, stream_type, ((slots, META), F32), ((slots, 256), F32)],
        scratch,
    )
    for layer in range(LAYERS):
        last = layer == LAYERS - 1
        if layer:
            part, stream = call(
                functools.partial(next_attention_kernel, layer, len(parts)),
                on_chip(*parts, stream, facts, turn, cache_variates, *cache)
                + [(HBM, kv_cache)]
                + on_chip(attn_gain, qkv_weight, out_weight, variate_bias),
                [part_type, stream_type],
                scratch,
            )
        parts = exchange(part)
        if not last:
            part, stream = call(
                functools.partial(feed_forward_kernel, layer, len(parts)),
                on_chip(*parts, stream, ffn_gain, gate_up_weight, down_weight),
                [part_type, stream_type],
            )
            parts = exchange(part)
            cache = call(
                functools.partial(cache_kernel, layer + 1),
                [(ANY, part), (HBM, kv_cache)],
                cache_types,
                [pltpu.SemaphoreType.DMA((2,))],
            )
        else:
            (send,) = call(
                functools.partial(last_feed_forward_kernel, layer, len(parts), head_count),
                on_chip(*parts, place, flag, stream, ffn_gain, gate_up_weight, down_weight),
                [((devices, 2, width // 2 + META), BF16)],
            )
    received = lax.all_to_all(send, ("req", "head"), 0, 0, tiled=True)
    return pl.pallas_call(
        place_kernel,
        out_shape=jax.ShapeDtypeStruct((share, width), BF16),
        in_specs=[VMEM],
        out_specs=VMEM,
        compiler_params=PARAMS,
    )(received)


def solution(mesh):
    return jax.shard_map(
        per_device,
        mesh=mesh,
        in_specs=(
            P("req", None),
            P("req"),
            P("req"),
            P("req"),
            P("req"),
            P("req", None),
            P(None, None, "req", None, "head"),
            P(),
            P(),
            P(None, None, "head"),
            P(None, "head", None),
            P(None, None, None, "head"),
            P(None, "head", None),
            P(None, None, "head"),
        ),
        out_specs=P(("req", "head"), None),
        check_vma=False,
    )
```

```python
import functools

import jax
import jax.numpy as jnp
import numpy as np
from jax import lax
from jax.experimental import pallas as pl
from jax.experimental.pallas import tpu as pltpu
from jax.sharding import PartitionSpec as P

HD = 64
LAYERS = 2
META = 128
LOW = 128
CHUNK = 128
NEG = -1e30
F32 = jnp.float32
BF16 = jnp.bfloat16

VMEM = pl.BlockSpec(memory_space=pltpu.VMEM)
HBM = pl.BlockSpec(memory_space=pltpu.HBM)
ANY = pl.BlockSpec(memory_space=pl.ANY)
LONG = pl.CostEstimate(flops=10**11, bytes_accessed=0, transcendentals=0)
SHORT = pl.CostEstimate(flops=10**6, bytes_accessed=0, transcendentals=0)
PARAMS = pltpu.CompilerParams(vmem_limit_bytes=16 * 2**20)


def iota(shape, dim):
    return lax.broadcasted_iota(jnp.int32, shape, dim)


def copy_all(pairs, sems):
    copies = [pltpu.make_async_copy(src, dst, sems.at[i]) for i, (src, dst) in enumerate(pairs)]
    for copy in copies:
        copy.start()
    for copy in copies:
        copy.wait()


def pack_kernel(
    tokens_ref, lengths_ref, positions_ref, variates_ref, out_ref, length, position, variate, sems
):
    rows, width = tokens_ref.shape
    copy_all(
        [
            (tokens_ref, out_ref.at[:, pl.ds(0, width)]),
            (lengths_ref, length),
            (positions_ref, position),
            (variates_ref, variate),
        ],
        sems,
    )
    row, lane = iota((rows, META), 0), iota((rows, META), 1)
    kind = lane % (META // 2)
    whole = jnp.zeros((rows, META), jnp.int32)
    for i in range(rows):
        values = jnp.where(kind == 0, length[i], jnp.where(kind == 1, position[i], variate[i]))
        whole = jnp.where(row == i, values, whole)
    digit = jnp.where(lane < META // 2, whole // LOW, whole % LOW)
    out_ref[:, width:] = digit.astype(F32).astype(BF16)


def cache_copies(layer, kv_ref, front_ref, lead_ref, sems, first):
    rest = kv_ref.shape[3] - CHUNK
    return [
        pltpu.make_async_copy(
            kv_ref.at[layer, :, :, pl.ds(0, CHUNK), :], front_ref, sems.at[first]
        ),
        pltpu.make_async_copy(
            kv_ref.at[layer, :, 0, pl.ds(CHUNK, rest), :], lead_ref, sems.at[first + 1]
        ),
    ]


def owner_kernel(
    share,
    heads,
    block_ids,
    after_ref,
    owner_ref,
    own_block_ref,
    kv_ref,
    pick_ref,
    place_ref,
    flag_ref,
    front_ref,
    lead_ref,
    owner,
    own_block,
    sems,
):
    copies = [
        pltpu.make_async_copy(owner_ref, owner, sems.at[0]),
        pltpu.make_async_copy(own_block_ref, own_block, sems.at[1]),
    ] + cache_copies(0, kv_ref, front_ref, lead_ref, sems, 2)
    for copy in copies:
        copy.start()
    copies[0].wait()
    copies[1].wait()
    slots, total = pick_ref.shape
    devices = place_ref.shape[0]
    row, column = iota((slots, total), 0), iota((slots, total), 1)
    target, slot = iota((devices, slots), 0), iota((devices, slots), 1)
    flag_row, flag_part = iota((slots, flag_ref.shape[1]), 0), iota((slots, flag_ref.shape[1]), 1) // 128
    mask = jnp.zeros((slots, total), jnp.int32)
    for k, block_id in enumerate(block_ids):
        mask = jnp.where(column // slots == k, block_id, mask)
    request_at = (mask ^ own_block[0]) * slots + column % slots
    pick = jnp.zeros((slots, total), F32)
    place = jnp.zeros((devices, slots), F32)
    flag = jnp.zeros(flag_ref.shape, F32)
    for s in range(slots):
        request = owner[s]
        pick = jnp.where((row == s) & (request_at == request), 1.0, pick)
        device = request // share
        block = device % heads * (devices // heads) + device // heads
        place = jnp.where((slot == s) & (target == block), 1.0, place)
        flag = jnp.where((flag_row == s) & (flag_part == request % share), 1.0, flag)
    pick_ref[...] = pick.astype(BF16)
    place_ref[...] = place.astype(BF16)
    flag_ref[...] = flag.astype(BF16)
    copies[2].wait()
    copies[3].wait()


def cache_kernel(layer, after_ref, kv_ref, front_ref, lead_ref, sems):
    copies = cache_copies(layer, kv_ref, front_ref, lead_ref, sems, 0)
    for copy in copies:
        copy.start()
    for copy in copies:
        copy.wait()


def attention(
    layer,
    stream,
    facts,
    cos,
    sin,
    variates_ref,
    front_ref,
    lead_ref,
    kv_ref,
    gain_ref,
    qkv_ref,
    out_w_ref,
    bias_ref,
    scores,
    mixed,
    attended,
    rest_kv,
    rest_sems,
    part_ref,
):
    slots, cap = variates_ref.shape
    width = front_ref.shape[-1]
    heads = width // HD
    rows = heads * slots
    rest = cap - CHUNK

    lengths = facts[:, 0:1]
    variate = facts[:, 2:3]
    longer = jnp.sum((lengths > CHUNK).astype(jnp.int32))

    scale = lax.rsqrt(jnp.mean(stream * stream, axis=-1, keepdims=True) + 1e-06)
    scaled = (stream * gain_ref[layer : layer + 1, :]).astype(BF16)
    projected = jnp.dot(scaled, qkv_ref[layer], preferred_element_type=F32) * scale

    lane = iota((slots, 128), 1)
    front_half = lane % HD < HD // 2
    pieces = []
    for j in range(projected.shape[1] // 128):
        u = projected[:, j * 128 : (j + 1) * 128]
        turned = jnp.where(front_half, -pltpu.roll(u, 96, 1), pltpu.roll(u, 32, 1))
        is_value = (lane + j * 128) % (3 * HD) >= 2 * HD
        pieces.append(jnp.where(is_value, u, u * cos + turned * sin).astype(BF16).astype(F32))
    turned_all = jnp.concatenate(pieces, axis=1)

    column = iota((slots, width), 1)
    of_head = [column // HD == h for h in range(heads)]
    step = 2 * HD
    query = [
        jnp.where(of_head[h], turned_all[:, h * step : h * step + width], 0.0) for h in range(heads)
    ]
    query_all = jnp.concatenate(query, axis=0).astype(BF16)
    row_slot = iota((rows, CHUNK), 0) % slots
    rest_slot = iota((rows, rest), 0) % slots

    def score(keys):
        return lax.dot_general(
            query_all, keys, (((1,), (1,)), ((), ())), preferred_element_type=F32
        )

    raw = score(front_ref[0].reshape(slots * CHUNK, width))
    front_scores = raw[:, :CHUNK]
    for s in range(1, slots):
        front_scores = jnp.where(
            row_slot == s, raw[:, s * CHUNK : (s + 1) * CHUNK], front_scores
        )
    lead_scores = score(lead_ref[0])

    next_keys = jnp.concatenate([turned_all[:, HD:], jnp.zeros((slots, HD), F32)], axis=1)
    own_score = [
        jnp.sum(query[h] * next_keys[:, h * step : h * step + width], axis=1, keepdims=True) * 0.125
        + bias_ref[layer, 0:1, h : h + 1]
        for h in range(heads)
    ]
    same = variates_ref[...].astype(F32) == variate
    live = iota((slots, cap), 1).astype(F32) < lengths

    def soften(raw_scores):
        weights, own = [], []
        for h in range(heads):
            block = raw_scores[h * slots : (h + 1) * slots, :] * 0.125
            block = block + jnp.where(
                same, bias_ref[layer, 0:1, h : h + 1], bias_ref[layer, 1:2, h : h + 1]
            )
            block = jnp.where(live, block, NEG)
            top = jnp.maximum(jnp.max(block, axis=1, keepdims=True), own_score[h])
            weight = jnp.exp(block - top)
            own_weight = jnp.exp(own_score[h] - top)
            share = 1.0 / (jnp.sum(weight, axis=1, keepdims=True) + own_weight)
            weights.append(weight)
            own.append((own_weight, share))
        return jnp.concatenate(weights, axis=0).astype(BF16), own

    def only(mask, weights):
        return jnp.where(mask, weights, jnp.zeros_like(weights))

    def mix(weights):
        spread = jnp.concatenate([only(row_slot == s, weights[:, :CHUNK]) for s in range(slots)], 1)
        front = jnp.dot(
            spread, front_ref[1].reshape(slots * CHUNK, width), preferred_element_type=F32
        )
        lead = only(rest_slot == 0, weights[:, CHUNK:])
        return front + jnp.dot(lead, lead_ref[1], preferred_element_type=F32)

    def lay_out(mixed_rows, own):
        result = jnp.zeros((slots, width), F32)
        for h, (own_weight, share) in enumerate(own):
            value_new = turned_all[:, (h + 1) * step : (h + 1) * step + width]
            whole = mixed_rows[h * slots : (h + 1) * slots, :] + own_weight * value_new
            result = jnp.where(of_head[h], whole * share, result)
        return result

    all_scores = jnp.concatenate([front_scores, lead_scores], axis=1)
    weights_all, own_all = soften(all_scores)
    attended[...] = lay_out(mix(weights_all), own_all)

    @pl.when(longer > 1)
    def _():
        def rest_copy(s):
            return pltpu.make_async_copy(
                kv_ref.at[layer, :, s, pl.ds(CHUNK, rest), :], rest_kv.at[s], rest_sems.at[s]
            )

        @pl.loop(1, longer)
        def _(s):
            rest_copy(s).start()

        scores[...] = all_scores

        @pl.loop(1, longer)
        def _(s):
            rest_copy(s).wait()
            scores[:, CHUNK:] = jnp.where(rest_slot == s, score(rest_kv[s, 0]), scores[:, CHUNK:])

        weights_long, own_long = soften(scores[...])
        mixed[...] = mix(weights_long)
        rest_weights = weights_long[:, CHUNK:]

        @pl.loop(1, longer)
        def _(s):
            mixed[...] += jnp.dot(
                only(rest_slot == s, rest_weights), rest_kv[s, 1], preferred_element_type=F32
            )

        attended[...] = lay_out(mixed[...], own_long)

    part_ref[...] = jnp.dot(
        attended[...].astype(BF16), out_w_ref[layer], preferred_element_type=F32
    ).astype(BF16)


def first_attention_kernel(block_count, *refs):
    (
        pick_ref,
        frequency_ref,
        variates_ref,
        front_ref,
        lead_ref,
        kv_ref,
        gain_ref,
        qkv_ref,
        out_w_ref,
        bias_ref,
        part_ref,
        stream_ref,
        facts_ref,
        turn_ref,
        *scratch,
    ) = refs[block_count:]
    gathered = jnp.concatenate([ref[...] for ref in refs[:block_count]], axis=0)
    width = stream_ref.shape[1]
    picked = jnp.dot(pick_ref[...], gathered, preferred_element_type=F32)
    stream = picked[:, :width]
    digits = picked[:, width:]
    facts = digits * float(LOW) + pltpu.roll(digits, META // 2, 1)
    stream_ref[...] = stream
    facts_ref[...] = facts
    angle = facts[:, 1:2] * frequency_ref[...]
    cos, sin = jnp.cos(angle), jnp.sin(angle)
    turn_ref[:, :128] = cos
    turn_ref[:, 128:] = sin
    attention(
        0, stream, facts, cos, sin, variates_ref, front_ref, lead_ref, kv_ref, gain_ref, qkv_ref,
        out_w_ref, bias_ref, *scratch, part_ref,
    )


def next_attention_kernel(layer, part_count, *refs):
    (
        old_ref,
        facts_ref,
        turn_ref,
        variates_ref,
        front_ref,
        lead_ref,
        kv_ref,
        gain_ref,
        qkv_ref,
        out_w_ref,
        bias_ref,
        part_ref,
        stream_ref,
        *scratch,
    ) = refs[part_count:]
    stream = old_ref[...]
    for ref in refs[:part_count]:
        stream = stream + ref[...].astype(F32)
    stream_ref[...] = stream
    attention(
        layer, stream, facts_ref[...], turn_ref[:, :128], turn_ref[:, 128:], variates_ref,
        front_ref, lead_ref, kv_ref, gain_ref, qkv_ref, out_w_ref, bias_ref, *scratch, part_ref,
    )


def feed_forward(layer, part_refs, old_ref, gain_ref, gate_up_ref, down_ref):
    stream = old_ref[...]
    for ref in part_refs:
        stream = stream + ref[...].astype(F32)
    scale = lax.rsqrt(jnp.mean(stream * stream, axis=-1, keepdims=True) + 1e-06)
    scaled = (stream * gain_ref[layer : layer + 1, :]).astype(BF16)
    gate = jnp.dot(scaled, gate_up_ref[layer, 0], preferred_element_type=F32) * scale
    up = jnp.dot(scaled, gate_up_ref[layer, 1], preferred_element_type=F32) * scale
    hidden = (gate / (1.0 + jnp.exp(-gate)) * up).astype(BF16)
    return stream, jnp.dot(hidden, down_ref[layer], preferred_element_type=F32)


def feed_forward_kernel(layer, part_count, *refs):
    old_ref, gain_ref, gate_up_ref, down_ref, part_ref, stream_ref = refs[part_count:]
    stream, part = feed_forward(layer, refs[:part_count], old_ref, gain_ref, gate_up_ref, down_ref)
    stream_ref[...] = stream
    part_ref[...] = part.astype(BF16)


def last_feed_forward_kernel(layer, part_count, head_count, *refs):
    place_ref, flag_ref, old_ref, gain_ref, gate_up_ref, down_ref, send_ref = refs[part_count:]
    stream, part = feed_forward(layer, refs[:part_count], old_ref, gain_ref, gate_up_ref, down_ref)
    rows = (part + stream * (1.0 / head_count)).astype(BF16)
    half, tail = rows.shape[1] // 2, flag_ref.shape[1] // 2
    for i in range(2):
        payload = jnp.concatenate(
            [rows[:, i * half : (i + 1) * half], flag_ref[:, i * tail : (i + 1) * tail]], axis=1
        )
        spread = jnp.dot(place_ref[...], payload, preferred_element_type=F32)
        send_ref[:, i, :] = spread.astype(BF16)


def place_kernel(received_ref, out_ref):
    share, width = out_ref.shape
    half = width // 2
    tail = (received_ref.shape[2] - half) // 128
    for k in range(share):
        lanes = slice(half + k % tail * 128, half + (k % tail + 1) * 128)
        flags = received_ref[:, k // tail, lanes].astype(F32)
        mask = jnp.concatenate([flags] * (half // 128), axis=1)
        for i in range(2):
            rows = received_ref[:, i, :half].astype(F32)
            row = jnp.sum(mask * rows, axis=0, keepdims=True)
            out_ref[k : k + 1, i * half : (i + 1) * half] = row.astype(BF16)


def call(kernel, operands, outs, scratch=(), cost=SHORT):
    specs = [spec for spec, _ in operands]
    arrays = [
        pltpu.with_memory_space_constraint(array, pltpu.HBM) if spec is HBM else array
        for spec, array in operands
    ]
    return pl.pallas_call(
        kernel,
        out_shape=[pltpu.VMEM(shape, dtype) for shape, dtype in outs],
        in_specs=specs,
        out_specs=[VMEM] * len(outs),
        scratch_shapes=list(scratch),
        compiler_params=PARAMS,
        cost_estimate=cost,
    )(*arrays)


def swap(array, axis, mask):
    count = lax.axis_size(axis)
    return lax.ppermute(array, axis, [(i, i ^ mask) for i in range(count)])


def gather_stages(count):
    stages = []
    top = count
    if count.bit_length() % 2 == 0:
        top = count // 2
        stages.append([top])
    while top > 1:
        stages.append([top // 4 * k for k in (1, 3, 2)])
        top //= 4
    return stages


def swap_across(array, mask):
    reqs, heads = lax.axis_size("req"), lax.axis_size("head")
    pairs = [
        (r * heads + h, (r ^ mask) * heads + (h ^ 1)) for r in range(reqs) for h in range(heads)
    ]
    return lax.ppermute(array, ("req", "head"), pairs)


def gather_blocks(block):
    blocks, ids = [block], [0]
    for masks in gather_stages(lax.axis_size("req")):
        held = blocks[0] if len(blocks) == 1 else jnp.concatenate(blocks, axis=0)
        blocks = [held] + [swap_across(held, mask) for mask in masks]
        ids = ids + [mask ^ i for mask in masks for i in ids]
    return blocks, ids


def per_device(
    tokens,
    lengths,
    slot_owner,
    positions,
    variates,
    cache_variates,
    kv_cache,
    attn_gain,
    ffn_gain,
    qkv_weight,
    out_weight,
    gate_up_weight,
    down_weight,
    variate_bias,
):
    slots, width = tokens.shape
    cap, local_width = kv_cache.shape[3:]
    head_count = lax.axis_size("head")
    devices = lax.axis_size("req") * head_count
    share = slots // head_count
    tail = 128 * -(-share // 2)
    local_heads = local_width // HD

    total = slots * lax.axis_size("req")
    whole_row = [pltpu.SMEM((slots,), jnp.int32)] * 3
    (packed,) = call(
        pack_kernel,
        [(HBM, tokens), (HBM, lengths), (HBM, positions), (HBM, variates)],
        [((slots, width + META), BF16)],
        whole_row + [pltpu.SemaphoreType.DMA((4,))],
        LONG,
    )
    exponent = -2.0 * (np.arange(128) % (HD // 2)) / HD
    frequency = jnp.asarray((10000.0**exponent).astype(np.float32)[None, :])
    own_block = lax.axis_index("req").reshape(1)
    blocks, block_ids = gather_blocks(packed)
    cache_types = [
        ((2, slots, CHUNK, local_width), BF16),
        ((2, cap - CHUNK, local_width), BF16),
    ]
    pick, place, flag, *cache = call(
        functools.partial(owner_kernel, share, head_count, block_ids),
        [(ANY, packed), (HBM, slot_owner), (HBM, own_block), (HBM, kv_cache)],
        [((slots, total), BF16), ((devices, slots), BF16), ((slots, tail * 2), BF16)]
        + cache_types,
        [
            pltpu.SMEM((slots,), jnp.int32),
            pltpu.SMEM((1,), jnp.int32),
            pltpu.SemaphoreType.DMA((4,)),
        ],
    )

    scratch = [
        pltpu.VMEM((local_heads * slots, cap), F32),
        pltpu.VMEM((local_heads * slots, local_width), F32),
        pltpu.VMEM((slots, local_width), F32),
        pltpu.VMEM((slots, 2, cap - CHUNK, local_width), BF16),
        pltpu.SemaphoreType.DMA((slots,)),
    ]
    stream_type = ((slots, width), F32)
    part_type = ((slots, width), BF16)

    def exchange(part):
        return [part] + [swap(part, "head", k) for k in range(1, head_count)]

    def on_chip(*arrays):
        return [(VMEM, x) for x in arrays]

    part, stream, facts, turn = call(
        functools.partial(first_attention_kernel, len(blocks)),
        on_chip(*blocks, pick, frequency, cache_variates, *cache)
        + [(HBM, kv_cache)]
        + on_chip(attn_gain, qkv_weight, out_weight, variate_bias),
        [part_type, stream_type, ((slots, META), F32), ((slots, 256), F32)],
        scratch,
    )
    for layer in range(LAYERS):
        last = layer == LAYERS - 1
        if layer:
            part, stream = call(
                functools.partial(next_attention_kernel, layer, len(parts)),
                on_chip(*parts, stream, facts, turn, cache_variates, *cache)
                + [(HBM, kv_cache)]
                + on_chip(attn_gain, qkv_weight, out_weight, variate_bias),
                [part_type, stream_type],
                scratch,
            )
        parts = exchange(part)
        if not last:
            part, stream = call(
                functools.partial(feed_forward_kernel, layer, len(parts)),
                on_chip(*parts, stream, ffn_gain, gate_up_weight, down_weight),
                [part_type, stream_type],
            )
            parts = exchange(part)
            cache = call(
                functools.partial(cache_kernel, layer + 1),
                [(ANY, part), (HBM, kv_cache)],
                cache_types,
                [pltpu.SemaphoreType.DMA((2,))],
            )
        else:
            (send,) = call(
                functools.partial(last_feed_forward_kernel, layer, len(parts), head_count),
                on_chip(*parts, place, flag, stream, ffn_gain, gate_up_weight, down_weight),
                [((devices, 2, width // 2 + tail), BF16)],
            )
    received = lax.all_to_all(send, ("head", "req"), 0, 0, tiled=True)
    return pl.pallas_call(
        place_kernel,
        out_shape=jax.ShapeDtypeStruct((share, width), BF16),
        in_specs=[VMEM],
        out_specs=VMEM,
        compiler_params=PARAMS,
    )(received)


def solution(mesh):
    return jax.shard_map(
        per_device,
        mesh=mesh,
        in_specs=(
            P("req", None),
            P("req"),
            P("req"),
            P("req"),
            P("req"),
            P("req", None),
            P(None, None, "req", None, "head"),
            P(),
            P(),
            P(None, None, "head"),
            P(None, "head", None),
            P(None, None, None, "head"),
            P(None, "head", None),
            P(None, None, "head"),
        ),
        out_specs=P(("req", "head"), None),
        check_vma=False,
    )
```

```python
import functools

import jax
import jax.numpy as jnp
import numpy as np
from jax import lax
from jax.experimental import pallas as pl
from jax.experimental.pallas import tpu as pltpu
from jax.sharding import PartitionSpec as P

HD = 64
LAYERS = 2
META = 128
LOW = 128
CHUNK = 128
NEG = -1e30
F32 = jnp.float32
BF16 = jnp.bfloat16

VMEM = pl.BlockSpec(memory_space=pltpu.VMEM)
HBM = pl.BlockSpec(memory_space=pltpu.HBM)
ANY = pl.BlockSpec(memory_space=pl.ANY)
LONG = pl.CostEstimate(flops=10**11, bytes_accessed=0, transcendentals=0)
SHORT = pl.CostEstimate(flops=10**6, bytes_accessed=0, transcendentals=0)
PARAMS = pltpu.CompilerParams(vmem_limit_bytes=16 * 2**20)


def iota(shape, dim):
    return lax.broadcasted_iota(jnp.int32, shape, dim)


def copy_all(pairs, sems):
    copies = [pltpu.make_async_copy(src, dst, sems.at[i]) for i, (src, dst) in enumerate(pairs)]
    for copy in copies:
        copy.start()
    for copy in copies:
        copy.wait()


def pack_kernel(
    tokens_ref, lengths_ref, positions_ref, variates_ref, out_ref, length, position, variate, sems
):
    rows, width = tokens_ref.shape
    copy_all(
        [
            (lengths_ref, length),
            (positions_ref, position),
            (variates_ref, variate),
            (tokens_ref, out_ref.at[:, pl.ds(0, width)]),
        ],
        sems,
    )
    row, lane = iota((rows, META), 0), iota((rows, META), 1)
    kind = lane % (META // 2)
    whole = jnp.zeros((rows, META), jnp.int32)
    for i in range(rows):
        values = jnp.where(kind == 0, length[i], jnp.where(kind == 1, position[i], variate[i]))
        whole = jnp.where(row == i, values, whole)
    digit = jnp.where(lane < META // 2, whole // LOW, whole % LOW)
    out_ref[:, width:] = digit.astype(F32).astype(BF16)


def cache_copies(layer, kv_ref, front_ref, lead_ref, sems, first):
    rest = kv_ref.shape[3] - CHUNK
    return [
        pltpu.make_async_copy(
            kv_ref.at[layer, :, :, pl.ds(0, CHUNK), :], front_ref, sems.at[first]
        ),
        pltpu.make_async_copy(
            kv_ref.at[layer, :, 0, pl.ds(CHUNK, rest), :], lead_ref, sems.at[first + 1]
        ),
    ]


def owner_kernel(
    share,
    heads,
    block_ids,
    after_ref,
    owner_ref,
    own_block_ref,
    kv_ref,
    pick_ref,
    place_ref,
    flag_ref,
    front_ref,
    lead_ref,
    owner,
    own_block,
    sems,
):
    copies = [
        pltpu.make_async_copy(owner_ref, owner, sems.at[0]),
        pltpu.make_async_copy(own_block_ref, own_block, sems.at[1]),
    ] + cache_copies(0, kv_ref, front_ref, lead_ref, sems, 2)
    for copy in copies:
        copy.start()
    copies[0].wait()
    copies[1].wait()
    slots, total = pick_ref.shape
    devices = place_ref.shape[0]
    row, column = iota((slots, total), 0), iota((slots, total), 1)
    target, slot = iota((devices, slots), 0), iota((devices, slots), 1)
    flag_row, flag_part = iota((slots, flag_ref.shape[1]), 0), iota((slots, flag_ref.shape[1]), 1) // 128
    mask = jnp.zeros((slots, total), jnp.int32)
    for k, block_id in enumerate(block_ids):
        mask = jnp.where(column // slots == k, block_id, mask)
    request_at = (mask ^ own_block[0]) * slots + column % slots
    pick = jnp.zeros((slots, total), F32)
    place = jnp.zeros((devices, slots), F32)
    flag = jnp.zeros(flag_ref.shape, F32)
    for s in range(slots):
        request = owner[s]
        pick = jnp.where((row == s) & (request_at == request), 1.0, pick)
        device = request // share
        head = device % heads
        block = (devices // heads - 1 - device // heads) * heads + head % 2 * (heads // 2) + head // 2
        place = jnp.where((slot == s) & (target == block), 1.0, place)
        flag = jnp.where((flag_row == s) & (flag_part == request % share), 1.0, flag)
    pick_ref[...] = pick.astype(BF16)
    place_ref[...] = place.astype(BF16)
    flag_ref[...] = flag.astype(BF16)
    copies[2].wait()
    copies[3].wait()


def cache_kernel(layer, after_ref, kv_ref, front_ref, lead_ref, sems):
    copies = cache_copies(layer, kv_ref, front_ref, lead_ref, sems, 0)
    for copy in copies:
        copy.start()
    for copy in copies:
        copy.wait()


def attention(
    layer,
    stream,
    facts,
    cos,
    sin,
    variates_ref,
    front_ref,
    lead_ref,
    kv_ref,
    gain_ref,
    qkv_ref,
    out_w_ref,
    bias_ref,
    scores,
    mixed,
    attended,
    rest_kv,
    rest_sems,
    part_ref,
):
    slots, cap = variates_ref.shape
    width = front_ref.shape[-1]
    heads = width // HD
    rows = heads * slots
    rest = cap - CHUNK

    lengths = facts[:, 0:1]
    variate = facts[:, 2:3]
    longer = jnp.sum((lengths > CHUNK).astype(jnp.int32))

    scale = lax.rsqrt(jnp.mean(stream * stream, axis=-1, keepdims=True) + 1e-06)
    scaled = (stream * gain_ref[layer : layer + 1, :]).astype(BF16)
    projected = jnp.dot(scaled, qkv_ref[layer], preferred_element_type=F32) * scale

    lane = iota((slots, 128), 1)
    front_half = lane % HD < HD // 2
    pieces = []
    for j in range(projected.shape[1] // 128):
        u = projected[:, j * 128 : (j + 1) * 128]
        turned = jnp.where(front_half, -pltpu.roll(u, 96, 1), pltpu.roll(u, 32, 1))
        is_value = (lane + j * 128) % (3 * HD) >= 2 * HD
        pieces.append(jnp.where(is_value, u, u * cos + turned * sin).astype(BF16).astype(F32))
    turned_all = jnp.concatenate(pieces, axis=1)

    column = iota((slots, width), 1)
    of_head = [column // HD == h for h in range(heads)]
    step = 2 * HD
    query = [
        jnp.where(of_head[h], turned_all[:, h * step : h * step + width], 0.0) for h in range(heads)
    ]
    query_all = jnp.concatenate(query, axis=0).astype(BF16)
    row_slot = iota((rows, CHUNK), 0) % slots
    rest_slot = iota((rows, rest), 0) % slots

    def score(keys):
        return lax.dot_general(
            query_all, keys, (((1,), (1,)), ((), ())), preferred_element_type=F32
        )

    raw = score(front_ref[0].reshape(slots * CHUNK, width))
    front_scores = raw[:, :CHUNK]
    for s in range(1, slots):
        front_scores = jnp.where(
            row_slot == s, raw[:, s * CHUNK : (s + 1) * CHUNK], front_scores
        )
    lead_scores = score(lead_ref[0])

    next_keys = jnp.concatenate([turned_all[:, HD:], jnp.zeros((slots, HD), F32)], axis=1)
    own_score = [
        jnp.sum(query[h] * next_keys[:, h * step : h * step + width], axis=1, keepdims=True) * 0.125
        + bias_ref[layer, 0:1, h : h + 1]
        for h in range(heads)
    ]
    same = variates_ref[...].astype(F32) == variate
    live = iota((slots, cap), 1).astype(F32) < lengths

    def soften(raw_scores):
        weights, own = [], []
        for h in range(heads):
            block = raw_scores[h * slots : (h + 1) * slots, :] * 0.125
            block = block + jnp.where(
                same, bias_ref[layer, 0:1, h : h + 1], bias_ref[layer, 1:2, h : h + 1]
            )
            block = jnp.where(live, block, NEG)
            top = jnp.maximum(jnp.max(block, axis=1, keepdims=True), own_score[h])
            weight = jnp.exp(block - top)
            own_weight = jnp.exp(own_score[h] - top)
            share = 1.0 / (jnp.sum(weight, axis=1, keepdims=True) + own_weight)
            weights.append(weight)
            own.append((own_weight, share))
        return jnp.concatenate(weights, axis=0).astype(BF16), own

    def only(mask, weights):
        return jnp.where(mask, weights, jnp.zeros_like(weights))

    def mix(weights):
        spread = jnp.concatenate([only(row_slot == s, weights[:, :CHUNK]) for s in range(slots)], 1)
        front = jnp.dot(
            spread, front_ref[1].reshape(slots * CHUNK, width), preferred_element_type=F32
        )
        lead = only(rest_slot == 0, weights[:, CHUNK:])
        return front + jnp.dot(lead, lead_ref[1], preferred_element_type=F32)

    def lay_out(mixed_rows, own):
        result = jnp.zeros((slots, width), F32)
        for h, (own_weight, share) in enumerate(own):
            value_new = turned_all[:, (h + 1) * step : (h + 1) * step + width]
            whole = mixed_rows[h * slots : (h + 1) * slots, :] + own_weight * value_new
            result = jnp.where(of_head[h], whole * share, result)
        return result

    all_scores = jnp.concatenate([front_scores, lead_scores], axis=1)
    weights_all, own_all = soften(all_scores)
    attended[...] = lay_out(mix(weights_all), own_all)

    @pl.when(longer > 1)
    def _():
        def rest_copy(s):
            return pltpu.make_async_copy(
                kv_ref.at[layer, :, s, pl.ds(CHUNK, rest), :], rest_kv.at[s], rest_sems.at[s]
            )

        @pl.loop(1, longer)
        def _(s):
            rest_copy(s).start()

        scores[...] = all_scores

        @pl.loop(1, longer)
        def _(s):
            rest_copy(s).wait()
            scores[:, CHUNK:] = jnp.where(rest_slot == s, score(rest_kv[s, 0]), scores[:, CHUNK:])

        weights_long, own_long = soften(scores[...])
        mixed[...] = mix(weights_long)
        rest_weights = weights_long[:, CHUNK:]

        @pl.loop(1, longer)
        def _(s):
            mixed[...] += jnp.dot(
                only(rest_slot == s, rest_weights), rest_kv[s, 1], preferred_element_type=F32
            )

        attended[...] = lay_out(mixed[...], own_long)

    part_ref[...] = jnp.dot(
        attended[...].astype(BF16), out_w_ref[layer], preferred_element_type=F32
    ).astype(BF16)


def first_attention_kernel(block_count, *refs):
    (
        pick_ref,
        frequency_ref,
        variates_ref,
        front_ref,
        lead_ref,
        kv_ref,
        gain_ref,
        qkv_ref,
        out_w_ref,
        bias_ref,
        part_ref,
        stream_ref,
        facts_ref,
        turn_ref,
        *scratch,
    ) = refs[block_count:]
    gathered = jnp.concatenate([ref[...] for ref in refs[:block_count]], axis=0)
    width = stream_ref.shape[1]
    picked = jnp.dot(pick_ref[...], gathered, preferred_element_type=F32)
    stream = picked[:, :width]
    digits = picked[:, width:]
    facts = digits * float(LOW) + pltpu.roll(digits, META // 2, 1)
    stream_ref[...] = stream
    facts_ref[...] = facts
    angle = facts[:, 1:2] * frequency_ref[...]
    cos, sin = jnp.cos(angle), jnp.sin(angle)
    turn_ref[:, :128] = cos
    turn_ref[:, 128:] = sin
    attention(
        0, stream, facts, cos, sin, variates_ref, front_ref, lead_ref, kv_ref, gain_ref, qkv_ref,
        out_w_ref, bias_ref, *scratch, part_ref,
    )


def next_attention_kernel(layer, part_count, *refs):
    (
        old_ref,
        facts_ref,
        turn_ref,
        variates_ref,
        front_ref,
        lead_ref,
        kv_ref,
        gain_ref,
        qkv_ref,
        out_w_ref,
        bias_ref,
        part_ref,
        stream_ref,
        *scratch,
    ) = refs[part_count:]
    stream = old_ref[...]
    for ref in refs[:part_count]:
        stream = stream + ref[...].astype(F32)
    stream_ref[...] = stream
    attention(
        layer, stream, facts_ref[...], turn_ref[:, :128], turn_ref[:, 128:], variates_ref,
        front_ref, lead_ref, kv_ref, gain_ref, qkv_ref, out_w_ref, bias_ref, *scratch, part_ref,
    )


def feed_forward(layer, part_refs, old_ref, gain_ref, gate_up_ref, down_ref):
    stream = old_ref[...]
    for ref in part_refs:
        stream = stream + ref[...].astype(F32)
    scale = lax.rsqrt(jnp.mean(stream * stream, axis=-1, keepdims=True) + 1e-06)
    scaled = (stream * gain_ref[layer : layer + 1, :]).astype(BF16)
    gate = jnp.dot(scaled, gate_up_ref[layer, 0], preferred_element_type=F32) * scale
    up = jnp.dot(scaled, gate_up_ref[layer, 1], preferred_element_type=F32) * scale
    hidden = (gate / (1.0 + jnp.exp(-gate)) * up).astype(BF16)
    return stream, jnp.dot(hidden, down_ref[layer], preferred_element_type=F32)


def feed_forward_kernel(layer, part_count, *refs):
    old_ref, gain_ref, gate_up_ref, down_ref, part_ref, stream_ref = refs[part_count:]
    stream, part = feed_forward(layer, refs[:part_count], old_ref, gain_ref, gate_up_ref, down_ref)
    stream_ref[...] = stream
    part_ref[...] = part.astype(BF16)


def last_feed_forward_kernel(layer, part_count, head_count, *refs):
    place_ref, flag_ref, old_ref, gain_ref, gate_up_ref, down_ref, send_ref = refs[part_count:]
    stream, part = feed_forward(layer, refs[:part_count], old_ref, gain_ref, gate_up_ref, down_ref)
    rows = (part + stream * (1.0 / head_count)).astype(BF16)
    half, tail = rows.shape[1] // 2, flag_ref.shape[1] // 2
    for i in range(2):
        payload = jnp.concatenate(
            [rows[:, i * half : (i + 1) * half], flag_ref[:, i * tail : (i + 1) * tail]], axis=1
        )
        spread = jnp.dot(place_ref[...], payload, preferred_element_type=F32)
        send_ref[:, i, :] = spread.astype(BF16)


def place_kernel(received_ref, out_ref):
    share, width = out_ref.shape
    half = width // 2
    tail = (received_ref.shape[2] - half) // 128
    for k in range(share):
        lanes = slice(half + k % tail * 128, half + (k % tail + 1) * 128)
        flags = received_ref[:, k // tail, lanes].astype(F32)
        mask = jnp.concatenate([flags] * (half // 128), axis=1)
        for i in range(2):
            rows = received_ref[:, i, :half].astype(F32)
            row = jnp.sum(mask * rows, axis=0, keepdims=True)
            out_ref[k : k + 1, i * half : (i + 1) * half] = row.astype(BF16)


def call(kernel, operands, outs, scratch=(), cost=SHORT):
    specs = [spec for spec, _ in operands]
    arrays = [
        pltpu.with_memory_space_constraint(array, pltpu.HBM) if spec is HBM else array
        for spec, array in operands
    ]
    return pl.pallas_call(
        kernel,
        out_shape=[pltpu.VMEM(shape, dtype) for shape, dtype in outs],
        in_specs=specs,
        out_specs=[VMEM] * len(outs),
        scratch_shapes=list(scratch),
        compiler_params=PARAMS,
        cost_estimate=cost,
    )(*arrays)


def swap(array, axis, mask):
    count = lax.axis_size(axis)
    return lax.ppermute(array, axis, [(i, i ^ mask) for i in range(count)])


def gather_stages(count):
    stages, reach = [], 1
    while reach < count:
        span = 2 if (count // reach).bit_length() % 2 == 0 else 4
        stages.append([reach * k for k in range(1, span)])
        reach *= span
    return stages


def swap_across(array, mask):
    reqs, heads = lax.axis_size("req"), lax.axis_size("head")
    pairs = [
        (r * heads + h, (r ^ mask) * heads + (h ^ 1)) for r in range(reqs) for h in range(heads)
    ]
    return lax.ppermute(array, ("req", "head"), pairs)


def gather_blocks(block):
    blocks, ids = [block], [0]
    for masks in gather_stages(lax.axis_size("req")):
        held = blocks[0] if len(blocks) == 1 else jnp.concatenate(blocks, axis=0)
        blocks = [held] + [swap_across(held, mask) for mask in masks]
        ids = ids + [mask ^ i for mask in masks for i in ids]
    return blocks, ids


def per_device(
    tokens,
    lengths,
    slot_owner,
    positions,
    variates,
    cache_variates,
    kv_cache,
    attn_gain,
    ffn_gain,
    qkv_weight,
    out_weight,
    gate_up_weight,
    down_weight,
    variate_bias,
):
    slots, width = tokens.shape
    cap, local_width = kv_cache.shape[3:]
    head_count = lax.axis_size("head")
    devices = lax.axis_size("req") * head_count
    share = slots // head_count
    tail = 128 * -(-share // 2)
    local_heads = local_width // HD

    total = slots * lax.axis_size("req")
    whole_row = [pltpu.SMEM((slots,), jnp.int32)] * 3
    (packed,) = call(
        pack_kernel,
        [(HBM, tokens), (HBM, lengths), (HBM, positions), (HBM, variates)],
        [((slots, width + META), BF16)],
        whole_row + [pltpu.SemaphoreType.DMA((4,))],
        LONG,
    )
    exponent = -2.0 * (np.arange(128) % (HD // 2)) / HD
    frequency = jnp.asarray((10000.0**exponent).astype(np.float32)[None, :])
    own_block = lax.axis_index("req").reshape(1)
    blocks, block_ids = gather_blocks(packed)
    cache_types = [
        ((2, slots, CHUNK, local_width), BF16),
        ((2, cap - CHUNK, local_width), BF16),
    ]
    pick, place, flag, *cache = call(
        functools.partial(owner_kernel, share, head_count, block_ids),
        [(ANY, packed), (HBM, slot_owner), (HBM, own_block), (HBM, kv_cache)],
        [((slots, total), BF16), ((devices, slots), BF16), ((slots, tail * 2), BF16)]
        + cache_types,
        [
            pltpu.SMEM((slots,), jnp.int32),
            pltpu.SMEM((1,), jnp.int32),
            pltpu.SemaphoreType.DMA((4,)),
        ],
    )

    scratch = [
        pltpu.VMEM((local_heads * slots, cap), F32),
        pltpu.VMEM((local_heads * slots, local_width), F32),
        pltpu.VMEM((slots, local_width), F32),
        pltpu.VMEM((slots, 2, cap - CHUNK, local_width), BF16),
        pltpu.SemaphoreType.DMA((slots,)),
    ]
    stream_type = ((slots, width), F32)
    part_type = ((slots, width), BF16)

    def exchange(part):
        return [part] + [swap(part, "head", k) for k in range(1, head_count)]

    def on_chip(*arrays):
        return [(VMEM, x) for x in arrays]

    part, stream, facts, turn = call(
        functools.partial(first_attention_kernel, len(blocks)),
        on_chip(*blocks, pick, frequency, cache_variates, *cache)
        + [(HBM, kv_cache)]
        + on_chip(attn_gain, qkv_weight, out_weight, variate_bias),
        [part_type, stream_type, ((slots, META), F32), ((slots, 256), F32)],
        scratch,
    )
    for layer in range(LAYERS):
        last = layer == LAYERS - 1
        if layer:
            part, stream = call(
                functools.partial(next_attention_kernel, layer, len(parts)),
                on_chip(*parts, stream, facts, turn, cache_variates, *cache)
                + [(HBM, kv_cache)]
                + on_chip(attn_gain, qkv_weight, out_weight, variate_bias),
                [part_type, stream_type],
                scratch,
            )
        parts = exchange(part)
        if not last:
            part, stream = call(
                functools.partial(feed_forward_kernel, layer, len(parts)),
                on_chip(*parts, stream, ffn_gain, gate_up_weight, down_weight),
                [part_type, stream_type],
            )
            parts = exchange(part)
            cache = call(
                functools.partial(cache_kernel, layer + 1),
                [(ANY, part), (HBM, kv_cache)],
                cache_types,
                [pltpu.SemaphoreType.DMA((2,))],
            )
        else:
            (send,) = call(
                functools.partial(last_feed_forward_kernel, layer, len(parts), head_count),
                on_chip(*parts, place, flag, stream, ffn_gain, gate_up_weight, down_weight),
                [((devices, 2, width // 2 + tail), BF16)],
            )
    order = [
        r * head_count + h
        for r in reversed(range(lax.axis_size("req")))
        for h in [*range(0, head_count, 2), *range(1, head_count, 2)]
    ]
    received = lax.all_to_all(
        send, ("req", "head"), 0, 0, axis_index_groups=[order], tiled=True
    )
    return pl.pallas_call(
        place_kernel,
        out_shape=jax.ShapeDtypeStruct((share, width), BF16),
        in_specs=[VMEM],
        out_specs=VMEM,
        compiler_params=PARAMS,
    )(received)


def solution(mesh):
    return jax.shard_map(
        per_device,
        mesh=mesh,
        in_specs=(
            P("req", None),
            P("req"),
            P("req"),
            P("req"),
            P("req"),
            P("req", None),
            P(None, None, "req", None, "head"),
            P(),
            P(),
            P(None, None, "head"),
            P(None, "head", None),
            P(None, None, None, "head"),
            P(None, "head", None),
            P(None, None, "head"),
        ),
        out_specs=P(("req", "head"), None),
        check_vma=False,
    )
```

```python
import functools

import jax
import jax.numpy as jnp
import numpy as np
from jax import lax
from jax.experimental import pallas as pl
from jax.experimental.pallas import tpu as pltpu
from jax.sharding import PartitionSpec as P

HD = 64
LAYERS = 2
META = 128
LOW = 128
CHUNK = 128
NEG = -1e30
F32 = jnp.float32
BF16 = jnp.bfloat16

VMEM = pl.BlockSpec(memory_space=pltpu.VMEM)
HBM = pl.BlockSpec(memory_space=pltpu.HBM)
ANY = pl.BlockSpec(memory_space=pl.ANY)
LONG = pl.CostEstimate(flops=10**11, bytes_accessed=0, transcendentals=0)
SHORT = pl.CostEstimate(flops=10**6, bytes_accessed=0, transcendentals=0)
PARAMS = pltpu.CompilerParams(vmem_limit_bytes=16 * 2**20)


def iota(shape, dim):
    return lax.broadcasted_iota(jnp.int32, shape, dim)


def copy_all(pairs, sems):
    copies = [pltpu.make_async_copy(src, dst, sems.at[i]) for i, (src, dst) in enumerate(pairs)]
    for copy in copies:
        copy.start()
    for copy in copies:
        copy.wait()


def pack_kernel(
    tokens_ref, lengths_ref, positions_ref, variates_ref, out_ref, length, position, variate, sems
):
    rows, width = tokens_ref.shape
    copy_all(
        [
            (lengths_ref, length),
            (positions_ref, position),
            (variates_ref, variate),
            (tokens_ref, out_ref.at[:, pl.ds(0, width)]),
        ],
        sems,
    )
    row, lane = iota((rows, META), 0), iota((rows, META), 1)
    kind = lane % (META // 2)
    whole = jnp.zeros((rows, META), jnp.int32)
    for i in range(rows):
        values = jnp.where(kind == 0, length[i], jnp.where(kind == 1, position[i], variate[i]))
        whole = jnp.where(row == i, values, whole)
    digit = jnp.where(lane < META // 2, whole // LOW, whole % LOW)
    out_ref[:, width:] = digit.astype(F32).astype(BF16)


def cache_copies(layer, kv_ref, front_ref, lead_ref, sems, first):
    rest = kv_ref.shape[3] - CHUNK
    return [
        pltpu.make_async_copy(
            kv_ref.at[layer, :, :, pl.ds(0, CHUNK), :], front_ref, sems.at[first]
        ),
        pltpu.make_async_copy(
            kv_ref.at[layer, :, 0, pl.ds(CHUNK, rest), :], lead_ref, sems.at[first + 1]
        ),
    ]


def owner_kernel(
    share,
    heads,
    block_ids,
    after_ref,
    owner_ref,
    own_block_ref,
    kv_ref,
    pick_ref,
    place_ref,
    flag_ref,
    front_ref,
    lead_ref,
    owner,
    own_block,
    sems,
):
    copies = [
        pltpu.make_async_copy(owner_ref, owner, sems.at[0]),
        pltpu.make_async_copy(own_block_ref, own_block, sems.at[1]),
    ] + cache_copies(0, kv_ref, front_ref, lead_ref, sems, 2)
    for copy in copies:
        copy.start()
    copies[0].wait()
    copies[1].wait()
    slots, total = pick_ref.shape
    devices = place_ref.shape[0]
    row, column = iota((slots, total), 0), iota((slots, total), 1)
    target, slot = iota((devices, slots), 0), iota((devices, slots), 1)
    flag_row, flag_part = iota((slots, flag_ref.shape[1]), 0), iota((slots, flag_ref.shape[1]), 1) // 128
    mask = jnp.zeros((slots, total), jnp.int32)
    for k, block_id in enumerate(block_ids):
        mask = jnp.where(column // slots == k, block_id, mask)
    request_at = (mask ^ own_block[0]) * slots + column % slots
    pick = jnp.zeros((slots, total), F32)
    place = jnp.zeros((devices, slots), F32)
    flag = jnp.zeros(flag_ref.shape, F32)
    for s in range(slots):
        request = owner[s]
        pick = jnp.where((row == s) & (request_at == request), 1.0, pick)
        device = request // share
        head = device % heads
        block = (devices // heads - 1 - device // heads) * heads + head % 2 * (heads // 2) + head // 2
        place = jnp.where((slot == s) & (target == block), 1.0, place)
        flag = jnp.where((flag_row == s) & (flag_part == request % share), 1.0, flag)
    pick_ref[...] = pick.astype(BF16)
    place_ref[...] = place.astype(BF16)
    flag_ref[...] = flag.astype(BF16)
    copies[2].wait()
    copies[3].wait()


def cache_kernel(layer, after_ref, kv_ref, front_ref, lead_ref, sems):
    copies = cache_copies(layer, kv_ref, front_ref, lead_ref, sems, 0)
    for copy in copies:
        copy.start()
    for copy in copies:
        copy.wait()


def attention(
    layer,
    stream,
    facts,
    cos,
    sin,
    variates_ref,
    front_ref,
    lead_ref,
    kv_ref,
    gain_ref,
    qkv_ref,
    out_w_ref,
    bias_ref,
    scores,
    mixed,
    attended,
    rest_kv,
    rest_sems,
    part_ref,
):
    slots, cap = variates_ref.shape
    width = front_ref.shape[-1]
    heads = width // HD
    rows = heads * slots
    rest = cap - CHUNK

    lengths = facts[:, 0:1]
    variate = facts[:, 2:3]
    longer = jnp.sum((lengths > CHUNK).astype(jnp.int32))

    scale = lax.rsqrt(jnp.mean(stream * stream, axis=-1, keepdims=True) + 1e-06)
    scaled = (stream * gain_ref[layer : layer + 1, :]).astype(BF16)
    projected = jnp.dot(scaled, qkv_ref[layer], preferred_element_type=F32) * scale

    lane = iota((slots, 128), 1)
    front_half = lane % HD < HD // 2
    pieces = []
    for j in range(projected.shape[1] // 128):
        u = projected[:, j * 128 : (j + 1) * 128]
        turned = jnp.where(front_half, -pltpu.roll(u, 96, 1), pltpu.roll(u, 32, 1))
        is_value = (lane + j * 128) % (3 * HD) >= 2 * HD
        pieces.append(jnp.where(is_value, u, u * cos + turned * sin).astype(BF16).astype(F32))
    turned_all = jnp.concatenate(pieces, axis=1)

    column = iota((slots, width), 1)
    of_head = [column // HD == h for h in range(heads)]
    step = 2 * HD
    query = [
        jnp.where(of_head[h], turned_all[:, h * step : h * step + width], 0.0) for h in range(heads)
    ]
    query_all = jnp.concatenate(query, axis=0).astype(BF16)
    row_slot = iota((rows, CHUNK), 0) % slots
    rest_slot = iota((rows, rest), 0) % slots

    def score(keys):
        return lax.dot_general(
            query_all, keys, (((1,), (1,)), ((), ())), preferred_element_type=F32
        )

    raw = score(front_ref[0].reshape(slots * CHUNK, width))
    front_scores = raw[:, :CHUNK]
    for s in range(1, slots):
        front_scores = jnp.where(
            row_slot == s, raw[:, s * CHUNK : (s + 1) * CHUNK], front_scores
        )
    lead_scores = score(lead_ref[0])

    next_keys = jnp.concatenate([turned_all[:, HD:], jnp.zeros((slots, HD), F32)], axis=1)
    own_score = [
        jnp.sum(query[h] * next_keys[:, h * step : h * step + width], axis=1, keepdims=True) * 0.125
        + bias_ref[layer, 0:1, h : h + 1]
        for h in range(heads)
    ]
    same = variates_ref[...].astype(F32) == variate
    live = iota((slots, cap), 1).astype(F32) < lengths

    def soften(raw_scores):
        weights, own = [], []
        for h in range(heads):
            block = raw_scores[h * slots : (h + 1) * slots, :] * 0.125
            block = block + jnp.where(
                same, bias_ref[layer, 0:1, h : h + 1], bias_ref[layer, 1:2, h : h + 1]
            )
            block = jnp.where(live, block, NEG)
            top = jnp.maximum(jnp.max(block, axis=1, keepdims=True), own_score[h])
            weight = jnp.exp(block - top)
            own_weight = jnp.exp(own_score[h] - top)
            share = 1.0 / (jnp.sum(weight, axis=1, keepdims=True) + own_weight)
            weights.append(weight)
            own.append((own_weight, share))
        return jnp.concatenate(weights, axis=0).astype(BF16), own

    def only(mask, weights):
        return jnp.where(mask, weights, jnp.zeros_like(weights))

    def mix(weights):
        spread = jnp.concatenate([only(row_slot == s, weights[:, :CHUNK]) for s in range(slots)], 1)
        front = jnp.dot(
            spread, front_ref[1].reshape(slots * CHUNK, width), preferred_element_type=F32
        )
        lead = only(rest_slot == 0, weights[:, CHUNK:])
        return front + jnp.dot(lead, lead_ref[1], preferred_element_type=F32)

    def lay_out(mixed_rows, own):
        result = jnp.zeros((slots, width), F32)
        for h, (own_weight, share) in enumerate(own):
            value_new = turned_all[:, (h + 1) * step : (h + 1) * step + width]
            whole = mixed_rows[h * slots : (h + 1) * slots, :] + own_weight * value_new
            result = jnp.where(of_head[h], whole * share, result)
        return result

    all_scores = jnp.concatenate([front_scores, lead_scores], axis=1)
    weights_all, own_all = soften(all_scores)
    attended[...] = lay_out(mix(weights_all), own_all)

    @pl.when(longer > 1)
    def _():
        def rest_copy(s):
            return pltpu.make_async_copy(
                kv_ref.at[layer, :, s, pl.ds(CHUNK, rest), :], rest_kv.at[s], rest_sems.at[s]
            )

        @pl.loop(1, longer)
        def _(s):
            rest_copy(s).start()

        scores[...] = all_scores

        @pl.loop(1, longer)
        def _(s):
            rest_copy(s).wait()
            scores[:, CHUNK:] = jnp.where(rest_slot == s, score(rest_kv[s, 0]), scores[:, CHUNK:])

        weights_long, own_long = soften(scores[...])
        mixed[...] = mix(weights_long)
        rest_weights = weights_long[:, CHUNK:]

        @pl.loop(1, longer)
        def _(s):
            mixed[...] += jnp.dot(
                only(rest_slot == s, rest_weights), rest_kv[s, 1], preferred_element_type=F32
            )

        attended[...] = lay_out(mixed[...], own_long)

    part_ref[...] = jnp.dot(
        attended[...].astype(BF16), out_w_ref[layer], preferred_element_type=F32
    ).astype(BF16)


def first_attention_kernel(block_count, *refs):
    (
        pick_ref,
        frequency_ref,
        variates_ref,
        front_ref,
        lead_ref,
        kv_ref,
        gain_ref,
        qkv_ref,
        out_w_ref,
        bias_ref,
        part_ref,
        stream_ref,
        facts_ref,
        turn_ref,
        *scratch,
    ) = refs[block_count:]
    gathered = jnp.concatenate([ref[...] for ref in refs[:block_count]], axis=0)
    width = stream_ref.shape[1]
    picked = jnp.dot(pick_ref[...], gathered, preferred_element_type=F32)
    stream = picked[:, :width]
    digits = picked[:, width:]
    facts = digits * float(LOW) + pltpu.roll(digits, META // 2, 1)
    stream_ref[...] = stream
    facts_ref[...] = facts
    angle = facts[:, 1:2] * frequency_ref[...]
    cos, sin = jnp.cos(angle), jnp.sin(angle)
    turn_ref[:, :128] = cos
    turn_ref[:, 128:] = sin
    attention(
        0, stream, facts, cos, sin, variates_ref, front_ref, lead_ref, kv_ref, gain_ref, qkv_ref,
        out_w_ref, bias_ref, *scratch, part_ref,
    )


def next_attention_kernel(layer, part_count, *refs):
    (
        old_ref,
        facts_ref,
        turn_ref,
        variates_ref,
        front_ref,
        lead_ref,
        kv_ref,
        gain_ref,
        qkv_ref,
        out_w_ref,
        bias_ref,
        part_ref,
        stream_ref,
        *scratch,
    ) = refs[part_count:]
    stream = old_ref[...]
    for ref in refs[:part_count]:
        stream = stream + ref[...].astype(F32)
    stream_ref[...] = stream
    attention(
        layer, stream, facts_ref[...], turn_ref[:, :128], turn_ref[:, 128:], variates_ref,
        front_ref, lead_ref, kv_ref, gain_ref, qkv_ref, out_w_ref, bias_ref, *scratch, part_ref,
    )


def feed_forward(layer, part_refs, old_ref, gain_ref, gate_up_ref, down_ref):
    stream = old_ref[...]
    for ref in part_refs:
        stream = stream + ref[...].astype(F32)
    scale = lax.rsqrt(jnp.mean(stream * stream, axis=-1, keepdims=True) + 1e-06)
    scaled = (stream * gain_ref[layer : layer + 1, :]).astype(BF16)
    gate = jnp.dot(scaled, gate_up_ref[layer, 0], preferred_element_type=F32) * scale
    up = jnp.dot(scaled, gate_up_ref[layer, 1], preferred_element_type=F32) * scale
    hidden = (gate / (1.0 + jnp.exp(-gate)) * up).astype(BF16)
    return stream, jnp.dot(hidden, down_ref[layer], preferred_element_type=F32)


def feed_forward_kernel(layer, part_count, *refs):
    old_ref, gain_ref, gate_up_ref, down_ref, part_ref, stream_ref = refs[part_count:]
    stream, part = feed_forward(layer, refs[:part_count], old_ref, gain_ref, gate_up_ref, down_ref)
    stream_ref[...] = stream
    part_ref[...] = part.astype(BF16)


def last_feed_forward_kernel(layer, part_count, head_count, *refs):
    place_ref, flag_ref, old_ref, gain_ref, gate_up_ref, down_ref, send_ref = refs[part_count:]
    stream, part = feed_forward(layer, refs[:part_count], old_ref, gain_ref, gate_up_ref, down_ref)
    rows = (part + stream * (1.0 / head_count)).astype(BF16)
    half, tail = rows.shape[1] // 2, flag_ref.shape[1] // 2
    for i in range(2):
        payload = jnp.concatenate(
            [rows[:, i * half : (i + 1) * half], flag_ref[:, i * tail : (i + 1) * tail]], axis=1
        )
        spread = jnp.dot(place_ref[...], payload, preferred_element_type=F32)
        send_ref[:, i, :] = spread.astype(BF16)


def place_kernel(received_ref, out_ref):
    share, width = out_ref.shape
    half = width // 2
    tail = (received_ref.shape[2] - half) // 128
    for k in range(share):
        lanes = slice(half + k % tail * 128, half + (k % tail + 1) * 128)
        flags = received_ref[:, k // tail, lanes].astype(F32)
        mask = jnp.concatenate([flags] * (half // 128), axis=1)
        for i in range(2):
            rows = received_ref[:, i, :half].astype(F32)
            row = jnp.sum(mask * rows, axis=0, keepdims=True)
            out_ref[k : k + 1, i * half : (i + 1) * half] = row.astype(BF16)


def call(kernel, operands, outs, scratch=(), cost=SHORT):
    specs = [spec for spec, _ in operands]
    arrays = [
        pltpu.with_memory_space_constraint(array, pltpu.HBM) if spec is HBM else array
        for spec, array in operands
    ]
    return pl.pallas_call(
        kernel,
        out_shape=[pltpu.VMEM(shape, dtype) for shape, dtype in outs],
        in_specs=specs,
        out_specs=[VMEM] * len(outs),
        scratch_shapes=list(scratch),
        compiler_params=PARAMS,
        cost_estimate=cost,
    )(*arrays)


def swap(array, axis, mask):
    count = lax.axis_size(axis)
    return lax.ppermute(array, axis, [(i, i ^ mask) for i in range(count)])


def gather_stages(count):
    stages, reach = [], 1
    while reach < count:
        span = 2 if (count // reach).bit_length() % 2 == 0 else 4
        stages.append([reach * k for k in range(1, span)])
        reach *= span
    return stages


def swap_across(array, mask):
    reqs, heads = lax.axis_size("req"), lax.axis_size("head")
    pairs = [
        (r * heads + h, (r ^ mask) * heads + (h ^ 1)) for r in range(reqs) for h in range(heads)
    ]
    return lax.ppermute(array, ("req", "head"), pairs)


def gather_ids(count):
    ids = [0]
    for masks in gather_stages(count):
        ids = ids + [mask ^ i for mask in masks for i in ids]
    return ids


def gather_blocks(block, beside):
    blocks, computed = [block], None
    for masks in gather_stages(lax.axis_size("req")):
        held = blocks[0] if len(blocks) == 1 else jnp.concatenate(blocks, axis=0)
        if len(blocks) > 1 and computed is None:
            held, computed = lax.optimization_barrier((held, beside()))
        blocks = [held] + [swap_across(held, mask) for mask in masks]
    return blocks, beside() if computed is None else computed


def per_device(
    tokens,
    lengths,
    slot_owner,
    positions,
    variates,
    cache_variates,
    kv_cache,
    attn_gain,
    ffn_gain,
    qkv_weight,
    out_weight,
    gate_up_weight,
    down_weight,
    variate_bias,
):
    slots, width = tokens.shape
    cap, local_width = kv_cache.shape[3:]
    head_count = lax.axis_size("head")
    devices = lax.axis_size("req") * head_count
    share = slots // head_count
    tail = 128 * -(-share // 2)
    local_heads = local_width // HD

    total = slots * lax.axis_size("req")
    whole_row = [pltpu.SMEM((slots,), jnp.int32)] * 3
    (packed,) = call(
        pack_kernel,
        [(HBM, tokens), (HBM, lengths), (HBM, positions), (HBM, variates)],
        [((slots, width + META), BF16)],
        whole_row + [pltpu.SemaphoreType.DMA((4,))],
        LONG,
    )
    exponent = -2.0 * (np.arange(128) % (HD // 2)) / HD
    frequency = jnp.asarray((10000.0**exponent).astype(np.float32)[None, :])
    own_block = lax.axis_index("req").reshape(1)
    cache_types = [
        ((2, slots, CHUNK, local_width), BF16),
        ((2, cap - CHUNK, local_width), BF16),
    ]
    block_ids = gather_ids(lax.axis_size("req"))

    def beside():
        return call(
            functools.partial(owner_kernel, share, head_count, block_ids),
            [(ANY, packed), (HBM, slot_owner), (HBM, own_block), (HBM, kv_cache)],
            [((slots, total), BF16), ((devices, slots), BF16), ((slots, tail * 2), BF16)]
            + cache_types,
            [
                pltpu.SMEM((slots,), jnp.int32),
                pltpu.SMEM((1,), jnp.int32),
                pltpu.SemaphoreType.DMA((4,)),
            ],
        )

    blocks, (pick, place, flag, *cache) = gather_blocks(packed, beside)

    scratch = [
        pltpu.VMEM((local_heads * slots, cap), F32),
        pltpu.VMEM((local_heads * slots, local_width), F32),
        pltpu.VMEM((slots, local_width), F32),
        pltpu.VMEM((slots, 2, cap - CHUNK, local_width), BF16),
        pltpu.SemaphoreType.DMA((slots,)),
    ]
    stream_type = ((slots, width), F32)
    part_type = ((slots, width), BF16)

    def exchange(part):
        return [part] + [swap(part, "head", k) for k in range(1, head_count)]

    def on_chip(*arrays):
        return [(VMEM, x) for x in arrays]

    part, stream, facts, turn = call(
        functools.partial(first_attention_kernel, len(blocks)),
        on_chip(*blocks, pick, frequency, cache_variates, *cache)
        + [(HBM, kv_cache)]
        + on_chip(attn_gain, qkv_weight, out_weight, variate_bias),
        [part_type, stream_type, ((slots, META), F32), ((slots, 256), F32)],
        scratch,
    )
    for layer in range(LAYERS):
        last = layer == LAYERS - 1
        if layer:
            part, stream = call(
                functools.partial(next_attention_kernel, layer, len(parts)),
                on_chip(*parts, stream, facts, turn, cache_variates, *cache)
                + [(HBM, kv_cache)]
                + on_chip(attn_gain, qkv_weight, out_weight, variate_bias),
                [part_type, stream_type],
                scratch,
            )
        parts = exchange(part)
        if not last:
            cache = call(
                functools.partial(cache_kernel, layer + 1),
                [(ANY, part), (HBM, kv_cache)],
                cache_types,
                [pltpu.SemaphoreType.DMA((2,))],
            )
            part, stream = call(
                functools.partial(feed_forward_kernel, layer, len(parts)),
                on_chip(*parts, stream, ffn_gain, gate_up_weight, down_weight),
                [part_type, stream_type],
            )
            parts = exchange(part)
        else:
            (send,) = call(
                functools.partial(last_feed_forward_kernel, layer, len(parts), head_count),
                on_chip(*parts, place, flag, stream, ffn_gain, gate_up_weight, down_weight),
                [((devices, 2, width // 2 + tail), BF16)],
            )
    order = [
        r * head_count + h
        for r in reversed(range(lax.axis_size("req")))
        for h in [*range(0, head_count, 2), *range(1, head_count, 2)]
    ]
    received = lax.all_to_all(
        send, ("req", "head"), 0, 0, axis_index_groups=[order], tiled=True
    )
    return pl.pallas_call(
        place_kernel,
        out_shape=jax.ShapeDtypeStruct((share, width), BF16),
        in_specs=[VMEM],
        out_specs=VMEM,
        compiler_params=PARAMS,
    )(received)


def solution(mesh):
    return jax.shard_map(
        per_device,
        mesh=mesh,
        in_specs=(
            P("req", None),
            P("req"),
            P("req"),
            P("req"),
            P("req"),
            P("req", None),
            P(None, None, "req", None, "head"),
            P(),
            P(),
            P(None, None, "head"),
            P(None, "head", None),
            P(None, None, None, "head"),
            P(None, "head", None),
            P(None, None, "head"),
        ),
        out_specs=P(("req", "head"), None),
        check_vma=False,
    )
```

```python
import functools

import jax
import jax.numpy as jnp
import numpy as np
from jax import lax
from jax.experimental import pallas as pl
from jax.experimental.pallas import tpu as pltpu
from jax.sharding import PartitionSpec as P

HD = 64
LAYERS = 2
META = 128
LOW = 128
CHUNK = 128
NEG = -1e30
F32 = jnp.float32
BF16 = jnp.bfloat16

VMEM = pl.BlockSpec(memory_space=pltpu.VMEM)
HBM = pl.BlockSpec(memory_space=pltpu.HBM)
ANY = pl.BlockSpec(memory_space=pl.ANY)
LONG = pl.CostEstimate(flops=10**11, bytes_accessed=0, transcendentals=0)
SHORT = pl.CostEstimate(flops=10**6, bytes_accessed=0, transcendentals=0)
PARAMS = pltpu.CompilerParams(vmem_limit_bytes=16 * 2**20)


def iota(shape, dim):
    return lax.broadcasted_iota(jnp.int32, shape, dim)


def copy_all(pairs, sems):
    copies = [pltpu.make_async_copy(src, dst, sems.at[i]) for i, (src, dst) in enumerate(pairs)]
    for copy in copies:
        copy.start()
    for copy in copies:
        copy.wait()


def pack_kernel(
    tokens_ref, lengths_ref, positions_ref, variates_ref, out_ref, length, position, variate, sems
):
    rows, width = tokens_ref.shape
    copy_all(
        [
            (lengths_ref, length),
            (positions_ref, position),
            (variates_ref, variate),
            (tokens_ref, out_ref.at[:, pl.ds(0, width)]),
        ],
        sems,
    )
    row, lane = iota((rows, META), 0), iota((rows, META), 1)
    kind = lane % (META // 2)
    whole = jnp.zeros((rows, META), jnp.int32)
    for i in range(rows):
        values = jnp.where(kind == 0, length[i], jnp.where(kind == 1, position[i], variate[i]))
        whole = jnp.where(row == i, values, whole)
    digit = jnp.where(lane < META // 2, whole // LOW, whole % LOW)
    out_ref[:, width:] = digit.astype(F32).astype(BF16)


def cache_copies(layer, kv_ref, front_ref, lead_ref, sems, first):
    rest = kv_ref.shape[3] - CHUNK
    return [
        pltpu.make_async_copy(
            kv_ref.at[layer, :, :, pl.ds(0, CHUNK), :], front_ref, sems.at[first]
        ),
        pltpu.make_async_copy(
            kv_ref.at[layer, :, 0, pl.ds(CHUNK, rest), :], lead_ref, sems.at[first + 1]
        ),
    ]


def owner_kernel(
    share,
    heads,
    block_ids,
    after_ref,
    owner_ref,
    kv_ref,
    pick_ref,
    place_ref,
    flag_ref,
    front_ref,
    lead_ref,
    owner,
    sems,
):
    copies = [pltpu.make_async_copy(owner_ref, owner, sems.at[0])]
    copies += cache_copies(0, kv_ref, front_ref, lead_ref, sems, 1)
    for copy in copies:
        copy.start()
    copies[0].wait()
    slots, total = pick_ref.shape
    devices = place_ref.shape[0]
    row, column = iota((slots, total), 0), iota((slots, total), 1)
    target, slot = iota((devices, slots), 0), iota((devices, slots), 1)
    flag_row, flag_part = iota((slots, flag_ref.shape[1]), 0), iota((slots, flag_ref.shape[1]), 1) // 128
    mask = jnp.zeros((slots, total), jnp.int32)
    for k, block_id in enumerate(block_ids):
        mask = jnp.where(column // slots == k, block_id, mask)
    request_at = (mask ^ lax.axis_index("req")) * slots + column % slots
    pick = jnp.zeros((slots, total), F32)
    place = jnp.zeros((devices, slots), F32)
    flag = jnp.zeros(flag_ref.shape, F32)
    for s in range(slots):
        request = owner[s]
        pick = jnp.where((row == s) & (request_at == request), 1.0, pick)
        device = request // share
        head = device % heads
        block = (devices // heads - 1 - device // heads) * heads + head % 2 * (heads // 2) + head // 2
        place = jnp.where((slot == s) & (target == block), 1.0, place)
        flag = jnp.where((flag_row == s) & (flag_part == request % share), 1.0, flag)
    pick_ref[...] = pick.astype(BF16)
    place_ref[...] = place.astype(BF16)
    flag_ref[...] = flag.astype(BF16)
    copies[1].wait()
    copies[2].wait()


def cache_kernel(layer, after_ref, kv_ref, front_ref, lead_ref, sems):
    copies = cache_copies(layer, kv_ref, front_ref, lead_ref, sems, 0)
    for copy in copies:
        copy.start()
    for copy in copies:
        copy.wait()


def attention(
    layer,
    stream,
    facts,
    cos,
    sin,
    variates_ref,
    front_ref,
    lead_ref,
    kv_ref,
    gain_ref,
    qkv_ref,
    out_w_ref,
    bias_ref,
    scores,
    mixed,
    attended,
    rest_kv,
    rest_sems,
    part_ref,
):
    slots, cap = variates_ref.shape
    width = front_ref.shape[-1]
    heads = width // HD
    rows = heads * slots
    rest = cap - CHUNK

    lengths = facts[:, 0:1]
    variate = facts[:, 2:3]
    longer = jnp.sum((lengths > CHUNK).astype(jnp.int32))

    scale = lax.rsqrt(jnp.mean(stream * stream, axis=-1, keepdims=True) + 1e-06)
    scaled = (stream * gain_ref[layer : layer + 1, :]).astype(BF16)
    projected = jnp.dot(scaled, qkv_ref[layer], preferred_element_type=F32) * scale

    lane = iota((slots, 128), 1)
    front_half = lane % HD < HD // 2
    pieces = []
    for j in range(projected.shape[1] // 128):
        u = projected[:, j * 128 : (j + 1) * 128]
        turned = jnp.where(front_half, -pltpu.roll(u, 96, 1), pltpu.roll(u, 32, 1))
        is_value = (lane + j * 128) % (3 * HD) >= 2 * HD
        pieces.append(jnp.where(is_value, u, u * cos + turned * sin).astype(BF16).astype(F32))
    turned_all = jnp.concatenate(pieces, axis=1)

    column = iota((slots, width), 1)
    of_head = [column // HD == h for h in range(heads)]
    step = 2 * HD
    query = [
        jnp.where(of_head[h], turned_all[:, h * step : h * step + width], 0.0) for h in range(heads)
    ]
    query_all = jnp.concatenate(query, axis=0).astype(BF16)
    row_slot = iota((rows, CHUNK), 0) % slots
    rest_slot = iota((rows, rest), 0) % slots

    def score(keys):
        return lax.dot_general(
            query_all, keys, (((1,), (1,)), ((), ())), preferred_element_type=F32
        )

    raw = score(front_ref[0].reshape(slots * CHUNK, width))
    front_scores = raw[:, :CHUNK]
    for s in range(1, slots):
        front_scores = jnp.where(
            row_slot == s, raw[:, s * CHUNK : (s + 1) * CHUNK], front_scores
        )
    lead_scores = score(lead_ref[0])

    next_keys = jnp.concatenate([turned_all[:, HD:], jnp.zeros((slots, HD), F32)], axis=1)
    own_score = [
        jnp.sum(query[h] * next_keys[:, h * step : h * step + width], axis=1, keepdims=True) * 0.125
        + bias_ref[layer, 0:1, h : h + 1]
        for h in range(heads)
    ]
    same = variates_ref[...].astype(F32) == variate
    live = iota((slots, cap), 1).astype(F32) < lengths

    def soften(raw_scores):
        weights, own = [], []
        for h in range(heads):
            block = raw_scores[h * slots : (h + 1) * slots, :] * 0.125
            block = block + jnp.where(
                same, bias_ref[layer, 0:1, h : h + 1], bias_ref[layer, 1:2, h : h + 1]
            )
            block = jnp.where(live, block, NEG)
            top = jnp.maximum(jnp.max(block, axis=1, keepdims=True), own_score[h])
            weight = jnp.exp(block - top)
            own_weight = jnp.exp(own_score[h] - top)
            share = 1.0 / (jnp.sum(weight, axis=1, keepdims=True) + own_weight)
            weights.append(weight)
            own.append((own_weight, share))
        return jnp.concatenate(weights, axis=0).astype(BF16), own

    def only(mask, weights):
        return jnp.where(mask, weights, jnp.zeros_like(weights))

    def mix(weights):
        spread = jnp.concatenate([only(row_slot == s, weights[:, :CHUNK]) for s in range(slots)], 1)
        front = jnp.dot(
            spread, front_ref[1].reshape(slots * CHUNK, width), preferred_element_type=F32
        )
        lead = only(rest_slot == 0, weights[:, CHUNK:])
        return front + jnp.dot(lead, lead_ref[1], preferred_element_type=F32)

    def lay_out(mixed_rows, own):
        result = jnp.zeros((slots, width), F32)
        for h, (own_weight, share) in enumerate(own):
            value_new = turned_all[:, (h + 1) * step : (h + 1) * step + width]
            whole = mixed_rows[h * slots : (h + 1) * slots, :] + own_weight * value_new
            result = jnp.where(of_head[h], whole * share, result)
        return result

    all_scores = jnp.concatenate([front_scores, lead_scores], axis=1)
    weights_all, own_all = soften(all_scores)
    attended[...] = lay_out(mix(weights_all), own_all)

    @pl.when(longer > 1)
    def _():
        def rest_copy(s):
            return pltpu.make_async_copy(
                kv_ref.at[layer, :, s, pl.ds(CHUNK, rest), :], rest_kv.at[s], rest_sems.at[s]
            )

        @pl.loop(1, longer)
        def _(s):
            rest_copy(s).start()

        scores[...] = all_scores

        @pl.loop(1, longer)
        def _(s):
            rest_copy(s).wait()
            scores[:, CHUNK:] = jnp.where(rest_slot == s, score(rest_kv[s, 0]), scores[:, CHUNK:])

        weights_long, own_long = soften(scores[...])
        mixed[...] = mix(weights_long)
        rest_weights = weights_long[:, CHUNK:]

        @pl.loop(1, longer)
        def _(s):
            mixed[...] += jnp.dot(
                only(rest_slot == s, rest_weights), rest_kv[s, 1], preferred_element_type=F32
            )

        attended[...] = lay_out(mixed[...], own_long)

    part_ref[...] = jnp.dot(
        attended[...].astype(BF16), out_w_ref[layer], preferred_element_type=F32
    ).astype(BF16)


def first_attention_kernel(block_count, *refs):
    (
        pick_ref,
        frequency_ref,
        variates_ref,
        front_ref,
        lead_ref,
        kv_ref,
        gain_ref,
        qkv_ref,
        out_w_ref,
        bias_ref,
        part_ref,
        stream_ref,
        facts_ref,
        turn_ref,
        *scratch,
    ) = refs[block_count:]
    gathered = jnp.concatenate([ref[...] for ref in refs[:block_count]], axis=0)
    width = stream_ref.shape[1]
    picked = jnp.dot(pick_ref[...], gathered, preferred_element_type=F32)
    stream = picked[:, :width]
    digits = picked[:, width:]
    facts = digits * float(LOW) + pltpu.roll(digits, META // 2, 1)
    stream_ref[...] = stream
    facts_ref[...] = facts
    angle = facts[:, 1:2] * frequency_ref[...]
    cos, sin = jnp.cos(angle), jnp.sin(angle)
    turn_ref[:, :128] = cos
    turn_ref[:, 128:] = sin
    attention(
        0, stream, facts, cos, sin, variates_ref, front_ref, lead_ref, kv_ref, gain_ref, qkv_ref,
        out_w_ref, bias_ref, *scratch, part_ref,
    )


def next_attention_kernel(layer, part_count, *refs):
    (
        old_ref,
        facts_ref,
        turn_ref,
        variates_ref,
        front_ref,
        lead_ref,
        kv_ref,
        gain_ref,
        qkv_ref,
        out_w_ref,
        bias_ref,
        part_ref,
        stream_ref,
        *scratch,
    ) = refs[part_count:]
    stream = old_ref[...]
    for ref in refs[:part_count]:
        stream = stream + ref[...].astype(F32)
    stream_ref[...] = stream
    attention(
        layer, stream, facts_ref[...], turn_ref[:, :128], turn_ref[:, 128:], variates_ref,
        front_ref, lead_ref, kv_ref, gain_ref, qkv_ref, out_w_ref, bias_ref, *scratch, part_ref,
    )


def feed_forward(layer, part_refs, old_ref, gain_ref, gate_up_ref, down_ref):
    stream = old_ref[...]
    for ref in part_refs:
        stream = stream + ref[...].astype(F32)
    scale = lax.rsqrt(jnp.mean(stream * stream, axis=-1, keepdims=True) + 1e-06)
    scaled = (stream * gain_ref[layer : layer + 1, :]).astype(BF16)
    gate = jnp.dot(scaled, gate_up_ref[layer, 0], preferred_element_type=F32) * scale
    up = jnp.dot(scaled, gate_up_ref[layer, 1], preferred_element_type=F32) * scale
    hidden = (gate / (1.0 + jnp.exp(-gate)) * up).astype(BF16)
    return stream, jnp.dot(hidden, down_ref[layer], preferred_element_type=F32)


def feed_forward_kernel(layer, part_count, *refs):
    old_ref, gain_ref, gate_up_ref, down_ref, part_ref, stream_ref = refs[part_count:]
    stream, part = feed_forward(layer, refs[:part_count], old_ref, gain_ref, gate_up_ref, down_ref)
    stream_ref[...] = stream
    part_ref[...] = part.astype(BF16)


def last_feed_forward_kernel(layer, part_count, head_count, *refs):
    place_ref, flag_ref, old_ref, gain_ref, gate_up_ref, down_ref, send_ref = refs[part_count:]
    stream, part = feed_forward(layer, refs[:part_count], old_ref, gain_ref, gate_up_ref, down_ref)
    rows = (part + stream * (1.0 / head_count)).astype(BF16)
    half, tail = rows.shape[1] // 2, flag_ref.shape[1] // 2
    for i in range(2):
        payload = jnp.concatenate(
            [rows[:, i * half : (i + 1) * half], flag_ref[:, i * tail : (i + 1) * tail]], axis=1
        )
        spread = jnp.dot(place_ref[...], payload, preferred_element_type=F32)
        send_ref[:, i, :] = spread.astype(BF16)


def place_kernel(received_ref, out_ref):
    share, width = out_ref.shape
    half = width // 2
    tail = (received_ref.shape[2] - half) // 128
    halves = [received_ref[:, i, :half].astype(F32) for i in range(2)]
    placed = []
    for k in range(share):
        lanes = slice(half + k % tail * 128, half + (k % tail + 1) * 128)
        flags = received_ref[:, k // tail, lanes].astype(F32)
        mask = jnp.concatenate([flags] * (half // 128), axis=1)
        sums = [jnp.sum(mask * rows, axis=0, keepdims=True) for rows in halves]
        placed.append(jnp.concatenate(sums, axis=1))
    out_ref[...] = jnp.concatenate(placed, axis=0).astype(BF16)


def call(kernel, operands, outs, scratch=(), cost=SHORT):
    specs = [spec for spec, _ in operands]
    arrays = [
        pltpu.with_memory_space_constraint(array, pltpu.HBM) if spec is HBM else array
        for spec, array in operands
    ]
    return pl.pallas_call(
        kernel,
        out_shape=[pltpu.VMEM(shape, dtype) for shape, dtype in outs],
        in_specs=specs,
        out_specs=[VMEM] * len(outs),
        scratch_shapes=list(scratch),
        compiler_params=PARAMS,
        cost_estimate=cost,
    )(*arrays)


def swap(array, axis, mask):
    count = lax.axis_size(axis)
    return lax.ppermute(array, axis, [(i, i ^ mask) for i in range(count)])


def gather_stages(count):
    stages, reach = [], 1
    while reach < count:
        span = 2 if (count // reach).bit_length() % 2 == 0 else 4
        stages.append([reach * k for k in range(1, span)])
        reach *= span
    return stages


def swap_across(array, mask):
    reqs, heads = lax.axis_size("req"), lax.axis_size("head")
    pairs = [
        (r * heads + h, (r ^ mask) * heads + (h ^ 1)) for r in range(reqs) for h in range(heads)
    ]
    return lax.ppermute(array, ("req", "head"), pairs)


def gather_blocks(block):
    blocks, ids = [block], [0]
    for masks in gather_stages(lax.axis_size("req")):
        held = blocks[0] if len(blocks) == 1 else jnp.concatenate(blocks, axis=0)
        blocks = [held] + [swap_across(held, mask) for mask in masks]
        ids = ids + [mask ^ i for mask in masks for i in ids]
    return blocks, ids


def per_device(
    tokens,
    lengths,
    slot_owner,
    positions,
    variates,
    cache_variates,
    kv_cache,
    attn_gain,
    ffn_gain,
    qkv_weight,
    out_weight,
    gate_up_weight,
    down_weight,
    variate_bias,
):
    slots, width = tokens.shape
    cap, local_width = kv_cache.shape[3:]
    head_count = lax.axis_size("head")
    devices = lax.axis_size("req") * head_count
    share = slots // head_count
    tail = 128 * -(-share // 2)
    local_heads = local_width // HD

    total = slots * lax.axis_size("req")
    whole_row = [pltpu.SMEM((slots,), jnp.int32)] * 3
    (packed,) = call(
        pack_kernel,
        [(HBM, tokens), (HBM, lengths), (HBM, positions), (HBM, variates)],
        [((slots, width + META), BF16)],
        whole_row + [pltpu.SemaphoreType.DMA((4,))],
        LONG,
    )
    exponent = -2.0 * (np.arange(128) % (HD // 2)) / HD
    frequency = jnp.asarray((10000.0**exponent).astype(np.float32)[None, :])
    blocks, block_ids = gather_blocks(packed)
    cache_types = [
        ((2, slots, CHUNK, local_width), BF16),
        ((2, cap - CHUNK, local_width), BF16),
    ]
    pick, place, flag, *cache = call(
        functools.partial(owner_kernel, share, head_count, block_ids),
        [(ANY, packed), (HBM, slot_owner), (HBM, kv_cache)],
        [((slots, total), BF16), ((devices, slots), BF16), ((slots, tail * 2), BF16)]
        + cache_types,
        [
            pltpu.SMEM((slots,), jnp.int32),
            pltpu.SemaphoreType.DMA((3,)),
        ],
    )

    scratch = [
        pltpu.VMEM((local_heads * slots, cap), F32),
        pltpu.VMEM((local_heads * slots, local_width), F32),
        pltpu.VMEM((slots, local_width), F32),
        pltpu.VMEM((slots, 2, cap - CHUNK, local_width), BF16),
        pltpu.SemaphoreType.DMA((slots,)),
    ]
    stream_type = ((slots, width), F32)
    part_type = ((slots, width), BF16)

    def exchange(part):
        return [part] + [swap(part, "head", k) for k in range(1, head_count)]

    def on_chip(*arrays):
        return [(VMEM, x) for x in arrays]

    part, stream, facts, turn = call(
        functools.partial(first_attention_kernel, len(blocks)),
        on_chip(*blocks, pick, frequency, cache_variates, *cache)
        + [(HBM, kv_cache)]
        + on_chip(attn_gain, qkv_weight, out_weight, variate_bias),
        [part_type, stream_type, ((slots, META), F32), ((slots, 256), F32)],
        scratch,
    )
    for layer in range(LAYERS):
        last = layer == LAYERS - 1
        if layer:
            part, stream = call(
                functools.partial(next_attention_kernel, layer, len(parts)),
                on_chip(*parts, stream, facts, turn, cache_variates, *cache)
                + [(HBM, kv_cache)]
                + on_chip(attn_gain, qkv_weight, out_weight, variate_bias),
                [part_type, stream_type],
                scratch,
            )
        parts = exchange(part)
        if not last:
            part, stream = call(
                functools.partial(feed_forward_kernel, layer, len(parts)),
                on_chip(*parts, stream, ffn_gain, gate_up_weight, down_weight),
                [part_type, stream_type],
            )
            parts = exchange(part)
            cache = call(
                functools.partial(cache_kernel, layer + 1),
                [(ANY, part), (HBM, kv_cache)],
                cache_types,
                [pltpu.SemaphoreType.DMA((2,))],
            )
        else:
            (send,) = call(
                functools.partial(last_feed_forward_kernel, layer, len(parts), head_count),
                on_chip(*parts, place, flag, stream, ffn_gain, gate_up_weight, down_weight),
                [((devices, 2, width // 2 + tail), BF16)],
            )
    order = [
        r * head_count + h
        for r in reversed(range(lax.axis_size("req")))
        for h in [*range(0, head_count, 2), *range(1, head_count, 2)]
    ]
    received = lax.all_to_all(
        send, ("req", "head"), 0, 0, axis_index_groups=[order], tiled=True
    )
    return pl.pallas_call(
        place_kernel,
        out_shape=jax.ShapeDtypeStruct((share, width), BF16),
        in_specs=[VMEM],
        out_specs=VMEM,
        compiler_params=PARAMS,
    )(received)


def solution(mesh):
    return jax.shard_map(
        per_device,
        mesh=mesh,
        in_specs=(
            P("req", None),
            P("req"),
            P("req"),
            P("req"),
            P("req"),
            P("req", None),
            P(None, None, "req", None, "head"),
            P(),
            P(),
            P(None, None, "head"),
            P(None, "head", None),
            P(None, None, None, "head"),
            P(None, "head", None),
            P(None, None, "head"),
        ),
        out_specs=P(("req", "head"), None),
        check_vma=False,
    )
```

```python
import functools

import jax
import jax.numpy as jnp
import numpy as np
from jax import lax
from jax.experimental import pallas as pl
from jax.experimental.pallas import tpu as pltpu
from jax.sharding import PartitionSpec as P

HD = 64
LAYERS = 2
META = 128
LOW = 128
CHUNK = 128
NEG = -1e30
F32 = jnp.float32
BF16 = jnp.bfloat16

VMEM = pl.BlockSpec(memory_space=pltpu.VMEM)
HBM = pl.BlockSpec(memory_space=pltpu.HBM)
ANY = pl.BlockSpec(memory_space=pl.ANY)
LONG = pl.CostEstimate(flops=10**11, bytes_accessed=0, transcendentals=0)
SHORT = pl.CostEstimate(flops=10**6, bytes_accessed=0, transcendentals=0)
PARAMS = pltpu.CompilerParams(vmem_limit_bytes=16 * 2**20)


def iota(shape, dim):
    return lax.broadcasted_iota(jnp.int32, shape, dim)


def copy_all(pairs, sems):
    copies = [pltpu.make_async_copy(src, dst, sems.at[i]) for i, (src, dst) in enumerate(pairs)]
    for copy in copies:
        copy.start()
    for copy in copies:
        copy.wait()


def pack_kernel(
    tokens_ref, lengths_ref, positions_ref, variates_ref, out_ref, length, position, variate, sems
):
    rows, width = tokens_ref.shape
    copy_all(
        [
            (lengths_ref, length),
            (positions_ref, position),
            (variates_ref, variate),
            (tokens_ref, out_ref.at[:, pl.ds(0, width)]),
        ],
        sems,
    )
    row, lane = iota((rows, META), 0), iota((rows, META), 1)
    kind = lane % (META // 2)
    whole = jnp.zeros((rows, META), jnp.int32)
    for i in range(rows):
        values = jnp.where(kind == 0, length[i], jnp.where(kind == 1, position[i], variate[i]))
        whole = jnp.where(row == i, values, whole)
    digit = jnp.where(lane < META // 2, whole // LOW, whole % LOW)
    out_ref[:, width:] = digit.astype(F32).astype(BF16)


def cache_copies(layer, kv_ref, front_ref, lead_ref, sems, first):
    rest = kv_ref.shape[3] - CHUNK
    return [
        pltpu.make_async_copy(
            kv_ref.at[layer, :, :, pl.ds(0, CHUNK), :], front_ref, sems.at[first]
        ),
        pltpu.make_async_copy(
            kv_ref.at[layer, :, 0, pl.ds(CHUNK, rest), :], lead_ref, sems.at[first + 1]
        ),
    ]


def owner_kernel(
    share,
    heads,
    block_ids,
    after_ref,
    owner_ref,
    kv_ref,
    pick_ref,
    place_ref,
    flag_ref,
    front_ref,
    lead_ref,
    owner,
    sems,
):
    copies = [pltpu.make_async_copy(owner_ref, owner, sems.at[0])]
    copies += cache_copies(0, kv_ref, front_ref, lead_ref, sems, 1)
    for copy in copies:
        copy.start()
    copies[0].wait()
    slots, total = pick_ref.shape
    devices = place_ref.shape[0]
    row, column = iota((slots, total), 0), iota((slots, total), 1)
    target, slot = iota((devices, slots), 0), iota((devices, slots), 1)
    flag_row, flag_part = iota((slots, flag_ref.shape[1]), 0), iota((slots, flag_ref.shape[1]), 1) // 128
    mask = jnp.zeros((slots, total), jnp.int32)
    for k, block_id in enumerate(block_ids):
        mask = jnp.where(column // slots == k, block_id, mask)
    request_at = (mask ^ lax.axis_index("req")) * slots + column % slots
    pick = jnp.zeros((slots, total), F32)
    place = jnp.zeros((devices, slots), F32)
    flag = jnp.zeros(flag_ref.shape, F32)
    for s in range(slots):
        request = owner[s]
        pick = jnp.where((row == s) & (request_at == request), 1.0, pick)
        device = request // share
        head = device % heads
        block = (devices // heads - 1 - device // heads) * heads + head % 2 * (heads // 2) + head // 2
        place = jnp.where((slot == s) & (target == block), 1.0, place)
        flag = jnp.where((flag_row == s) & (flag_part == request % share), 1.0, flag)
    pick_ref[...] = pick.astype(BF16)
    place_ref[...] = place.astype(BF16)
    flag_ref[...] = flag.astype(BF16)
    copies[1].wait()
    copies[2].wait()


def cache_kernel(layer, after_ref, kv_ref, front_ref, lead_ref, sems):
    copies = cache_copies(layer, kv_ref, front_ref, lead_ref, sems, 0)
    for copy in copies:
        copy.start()
    for copy in copies:
        copy.wait()


def attention(
    layer,
    stream,
    facts,
    cos,
    sin,
    variates_ref,
    front_ref,
    lead_ref,
    kv_ref,
    gain_ref,
    qkv_ref,
    out_w_ref,
    bias_ref,
    scores,
    mixed,
    attended,
    rest_kv,
    rest_sems,
    part_ref,
):
    slots, cap = variates_ref.shape
    width = front_ref.shape[-1]
    heads = width // HD
    rows = heads * slots
    rest = cap - CHUNK

    lengths = facts[:, 0:1]
    variate = facts[:, 2:3]
    longer = jnp.sum((lengths > CHUNK).astype(jnp.int32))

    scale = lax.rsqrt(jnp.mean(stream * stream, axis=-1, keepdims=True) + 1e-06)
    scaled = (stream * gain_ref[layer : layer + 1, :]).astype(BF16)
    projected = jnp.dot(scaled, qkv_ref[layer], preferred_element_type=F32) * scale

    lane = iota((slots, 128), 1)
    front_half = lane % HD < HD // 2
    pieces = []
    for j in range(projected.shape[1] // 128):
        u = projected[:, j * 128 : (j + 1) * 128]
        turned = jnp.where(front_half, -pltpu.roll(u, 96, 1), pltpu.roll(u, 32, 1))
        is_value = (lane + j * 128) % (3 * HD) >= 2 * HD
        pieces.append(jnp.where(is_value, u, u * cos + turned * sin).astype(BF16).astype(F32))
    turned_all = jnp.concatenate(pieces, axis=1)

    column = iota((slots, width), 1)
    of_head = [column // HD == h for h in range(heads)]
    step = 2 * HD
    query = [
        jnp.where(of_head[h], turned_all[:, h * step : h * step + width], 0.0) for h in range(heads)
    ]
    query_all = jnp.concatenate(query, axis=0).astype(BF16)
    row_slot = iota((rows, CHUNK), 0) % slots
    rest_slot = iota((rows, rest), 0) % slots

    def score(keys):
        return lax.dot_general(
            query_all, keys, (((1,), (1,)), ((), ())), preferred_element_type=F32
        )

    raw = score(front_ref[0].reshape(slots * CHUNK, width))
    front_scores = raw[:, :CHUNK]
    for s in range(1, slots):
        front_scores = jnp.where(
            row_slot == s, raw[:, s * CHUNK : (s + 1) * CHUNK], front_scores
        )
    lead_scores = score(lead_ref[0])

    next_keys = jnp.concatenate([turned_all[:, HD:], jnp.zeros((slots, HD), F32)], axis=1)
    own_score = [
        jnp.sum(query[h] * next_keys[:, h * step : h * step + width], axis=1, keepdims=True) * 0.125
        + bias_ref[layer, 0:1, h : h + 1]
        for h in range(heads)
    ]
    same = variates_ref[...].astype(F32) == variate
    live = iota((slots, cap), 1).astype(F32) < lengths

    def soften(raw_scores):
        weights, own = [], []
        for h in range(heads):
            block = raw_scores[h * slots : (h + 1) * slots, :] * 0.125
            block = block + jnp.where(
                same, bias_ref[layer, 0:1, h : h + 1], bias_ref[layer, 1:2, h : h + 1]
            )
            block = jnp.where(live, block, NEG)
            top = jnp.maximum(jnp.max(block, axis=1, keepdims=True), own_score[h])
            weight = jnp.exp(block - top)
            own_weight = jnp.exp(own_score[h] - top)
            share = 1.0 / (jnp.sum(weight, axis=1, keepdims=True) + own_weight)
            weights.append(weight)
            own.append((own_weight, share))
        return jnp.concatenate(weights, axis=0).astype(BF16), own

    def only(mask, weights):
        return jnp.where(mask, weights, jnp.zeros_like(weights))

    def mix(weights):
        spread = jnp.concatenate([only(row_slot == s, weights[:, :CHUNK]) for s in range(slots)], 1)
        front = jnp.dot(
            spread, front_ref[1].reshape(slots * CHUNK, width), preferred_element_type=F32
        )
        lead = only(rest_slot == 0, weights[:, CHUNK:])
        return front + jnp.dot(lead, lead_ref[1], preferred_element_type=F32)

    def lay_out(mixed_rows, own):
        result = jnp.zeros((slots, width), F32)
        for h, (own_weight, share) in enumerate(own):
            value_new = turned_all[:, (h + 1) * step : (h + 1) * step + width]
            whole = mixed_rows[h * slots : (h + 1) * slots, :] + own_weight * value_new
            result = jnp.where(of_head[h], whole * share, result)
        return result

    all_scores = jnp.concatenate([front_scores, lead_scores], axis=1)
    weights_all, own_all = soften(all_scores)
    attended[...] = lay_out(mix(weights_all), own_all)

    @pl.when(longer > 1)
    def _():
        def rest_copy(s):
            return pltpu.make_async_copy(
                kv_ref.at[layer, :, s, pl.ds(CHUNK, rest), :], rest_kv.at[s], rest_sems.at[s]
            )

        @pl.loop(1, longer)
        def _(s):
            rest_copy(s).start()

        scores[...] = all_scores

        @pl.loop(1, longer)
        def _(s):
            rest_copy(s).wait()
            scores[:, CHUNK:] = jnp.where(rest_slot == s, score(rest_kv[s, 0]), scores[:, CHUNK:])

        weights_long, own_long = soften(scores[...])
        mixed[...] = mix(weights_long)
        rest_weights = weights_long[:, CHUNK:]

        @pl.loop(1, longer)
        def _(s):
            mixed[...] += jnp.dot(
                only(rest_slot == s, rest_weights), rest_kv[s, 1], preferred_element_type=F32
            )

        attended[...] = lay_out(mixed[...], own_long)

    part_ref[...] = jnp.dot(
        attended[...].astype(BF16), out_w_ref[layer], preferred_element_type=F32
    ).astype(BF16)


def first_attention_kernel(block_count, *refs):
    (
        pick_ref,
        frequency_ref,
        variates_ref,
        front_ref,
        lead_ref,
        kv_ref,
        gain_ref,
        qkv_ref,
        out_w_ref,
        bias_ref,
        part_ref,
        stream_ref,
        facts_ref,
        turn_ref,
        *scratch,
    ) = refs[block_count:]
    gathered = jnp.concatenate([ref[...] for ref in refs[:block_count]], axis=0)
    width = stream_ref.shape[1]
    picked = jnp.dot(pick_ref[...], gathered, preferred_element_type=F32)
    stream = picked[:, :width]
    digits = picked[:, width:]
    facts = digits * float(LOW) + pltpu.roll(digits, META // 2, 1)
    stream_ref[...] = stream
    facts_ref[...] = facts
    angle = facts[:, 1:2] * frequency_ref[...]
    cos, sin = jnp.cos(angle), jnp.sin(angle)
    turn_ref[:, :128] = cos
    turn_ref[:, 128:] = sin
    attention(
        0, stream, facts, cos, sin, variates_ref, front_ref, lead_ref, kv_ref, gain_ref, qkv_ref,
        out_w_ref, bias_ref, *scratch, part_ref,
    )


def next_attention_kernel(layer, part_count, *refs):
    (
        old_ref,
        facts_ref,
        turn_ref,
        variates_ref,
        front_ref,
        lead_ref,
        kv_ref,
        gain_ref,
        qkv_ref,
        out_w_ref,
        bias_ref,
        part_ref,
        stream_ref,
        *scratch,
    ) = refs[part_count:]
    stream = old_ref[...]
    for ref in refs[:part_count]:
        stream = stream + ref[...].astype(F32)
    stream_ref[...] = stream
    attention(
        layer, stream, facts_ref[...], turn_ref[:, :128], turn_ref[:, 128:], variates_ref,
        front_ref, lead_ref, kv_ref, gain_ref, qkv_ref, out_w_ref, bias_ref, *scratch, part_ref,
    )


def feed_forward(layer, part_refs, old_ref, gain_ref, gate_up_ref, down_ref):
    stream = old_ref[...]
    for ref in part_refs:
        stream = stream + ref[...].astype(F32)
    scale = lax.rsqrt(jnp.mean(stream * stream, axis=-1, keepdims=True) + 1e-06)
    scaled = (stream * gain_ref[layer : layer + 1, :]).astype(BF16)
    gate = jnp.dot(scaled, gate_up_ref[layer, 0], preferred_element_type=F32) * scale
    up = jnp.dot(scaled, gate_up_ref[layer, 1], preferred_element_type=F32) * scale
    hidden = (gate / (1.0 + jnp.exp(-gate)) * up).astype(BF16)
    return stream, jnp.dot(hidden, down_ref[layer], preferred_element_type=F32)


def feed_forward_kernel(layer, part_count, *refs):
    old_ref, gain_ref, gate_up_ref, down_ref, part_ref, stream_ref = refs[part_count:]
    stream, part = feed_forward(layer, refs[:part_count], old_ref, gain_ref, gate_up_ref, down_ref)
    stream_ref[...] = stream
    part_ref[...] = part.astype(BF16)


def last_feed_forward_kernel(layer, part_count, head_count, *refs):
    place_ref, flag_ref, old_ref, gain_ref, gate_up_ref, down_ref, send_ref = refs[part_count:]
    stream, part = feed_forward(layer, refs[:part_count], old_ref, gain_ref, gate_up_ref, down_ref)
    rows = (part + stream * (1.0 / head_count)).astype(BF16)
    half, tail = rows.shape[1] // 2, flag_ref.shape[1] // 2
    for i in range(2):
        payload = jnp.concatenate(
            [rows[:, i * half : (i + 1) * half], flag_ref[:, i * tail : (i + 1) * tail]], axis=1
        )
        spread = jnp.dot(place_ref[...], payload, preferred_element_type=F32)
        send_ref[:, i, :] = spread.astype(BF16)


def place_kernel(received_ref, out_ref):
    share, width = out_ref.shape
    half = width // 2
    tail = (received_ref.shape[2] - half) // 128
    halves = [received_ref[:, i, :half].astype(F32) for i in range(2)]
    placed = []
    for k in range(share):
        lanes = slice(half + k % tail * 128, half + (k % tail + 1) * 128)
        flags = received_ref[:, k // tail, lanes].astype(F32)
        mask = jnp.concatenate([flags] * (half // 128), axis=1)
        sums = [jnp.sum(mask * rows, axis=0, keepdims=True) for rows in halves]
        placed.append(jnp.concatenate(sums, axis=1))
    out_ref[...] = jnp.concatenate(placed, axis=0).astype(BF16)


def call(kernel, operands, outs, scratch=(), cost=SHORT):
    specs = [spec for spec, _ in operands]
    arrays = [
        pltpu.with_memory_space_constraint(array, pltpu.HBM) if spec is HBM else array
        for spec, array in operands
    ]
    return pl.pallas_call(
        kernel,
        out_shape=[pltpu.VMEM(shape, dtype) for shape, dtype in outs],
        in_specs=specs,
        out_specs=[VMEM] * len(outs),
        scratch_shapes=list(scratch),
        compiler_params=PARAMS,
        cost_estimate=cost,
    )(*arrays)


def swap(array, axis, mask):
    count = lax.axis_size(axis)
    return lax.ppermute(array, axis, [(i, i ^ mask) for i in range(count)])


def gather_stages(count):
    stages, reach = [], 1
    while reach < count:
        span = 2 if (count // reach).bit_length() % 2 == 0 else 4
        stages.append([reach * k for k in range(1, span)])
        reach *= span
    return stages


def swap_across(array, mask):
    reqs, heads = lax.axis_size("req"), lax.axis_size("head")
    pairs = [
        (r * heads + h, (r ^ mask) * heads + (h ^ 1)) for r in range(reqs) for h in range(heads)
    ]
    return lax.ppermute(array, ("req", "head"), pairs)


def gather_blocks(block):
    blocks, ids = [block], [0]
    for masks in gather_stages(lax.axis_size("req")):
        held = blocks[0] if len(blocks) == 1 else jnp.concatenate(blocks, axis=0)
        blocks = [held] + [swap_across(held, mask) for mask in masks]
        ids = ids + [mask ^ i for mask in masks for i in ids]
    return blocks, ids


def per_device(
    tokens,
    lengths,
    slot_owner,
    positions,
    variates,
    cache_variates,
    kv_cache,
    attn_gain,
    ffn_gain,
    qkv_weight,
    out_weight,
    gate_up_weight,
    down_weight,
    variate_bias,
):
    slots, width = tokens.shape
    cap, local_width = kv_cache.shape[3:]
    head_count = lax.axis_size("head")
    devices = lax.axis_size("req") * head_count
    share = slots // head_count
    tail = 128 * -(-share // 2)
    local_heads = local_width // HD

    total = slots * lax.axis_size("req")
    whole_row = [pltpu.SMEM((slots,), jnp.int32)] * 3
    (packed,) = call(
        pack_kernel,
        [(HBM, tokens), (HBM, lengths), (HBM, positions), (HBM, variates)],
        [((slots, width + META), BF16)],
        whole_row + [pltpu.SemaphoreType.DMA((4,))],
        LONG,
    )
    exponent = -2.0 * (np.arange(128) % (HD // 2)) / HD
    frequency = jnp.asarray((10000.0**exponent).astype(np.float32)[None, :])
    blocks, block_ids = gather_blocks(packed)
    cache_types = [
        ((2, slots, CHUNK, local_width), BF16),
        ((2, cap - CHUNK, local_width), BF16),
    ]
    pick, place, flag, *cache = call(
        functools.partial(owner_kernel, share, head_count, block_ids),
        [(ANY, packed), (HBM, slot_owner), (HBM, kv_cache)],
        [((slots, total), BF16), ((devices, slots), BF16), ((slots, tail * 2), BF16)]
        + cache_types,
        [
            pltpu.SMEM((slots,), jnp.int32),
            pltpu.SemaphoreType.DMA((3,)),
        ],
    )

    scratch = [
        pltpu.VMEM((local_heads * slots, cap), F32),
        pltpu.VMEM((local_heads * slots, local_width), F32),
        pltpu.VMEM((slots, local_width), F32),
        pltpu.VMEM((slots, 2, cap - CHUNK, local_width), BF16),
        pltpu.SemaphoreType.DMA((slots,)),
    ]
    stream_type = ((slots, width), F32)
    part_type = ((slots, width), BF16)

    def exchange(part):
        return [part] + [swap(part, "head", k) for k in range(1, head_count)]

    def on_chip(*arrays):
        return [(VMEM, x) for x in arrays]

    part, stream, facts, turn = call(
        functools.partial(first_attention_kernel, len(blocks)),
        on_chip(*blocks, pick, frequency, cache_variates, *cache)
        + [(HBM, kv_cache)]
        + on_chip(attn_gain, qkv_weight, out_weight, variate_bias),
        [part_type, stream_type, ((slots, META), F32), ((slots, 256), F32)],
        scratch,
    )
    for layer in range(LAYERS):
        last = layer == LAYERS - 1
        if layer:
            part, stream = call(
                functools.partial(next_attention_kernel, layer, len(parts)),
                on_chip(*parts, stream, facts, turn, cache_variates, *cache)
                + [(HBM, kv_cache)]
                + on_chip(attn_gain, qkv_weight, out_weight, variate_bias),
                [part_type, stream_type],
                scratch,
            )
        parts = exchange(part)
        if not last:
            cache = call(
                functools.partial(cache_kernel, layer + 1),
                [(ANY, part), (HBM, kv_cache)],
                cache_types,
                [pltpu.SemaphoreType.DMA((2,))],
            )
            part, stream = call(
                functools.partial(feed_forward_kernel, layer, len(parts)),
                on_chip(*parts, stream, ffn_gain, gate_up_weight, down_weight),
                [part_type, stream_type],
            )
            parts = exchange(part)
        else:
            (send,) = call(
                functools.partial(last_feed_forward_kernel, layer, len(parts), head_count),
                on_chip(*parts, place, flag, stream, ffn_gain, gate_up_weight, down_weight),
                [((devices, 2, width // 2 + tail), BF16)],
            )
    order = [
        r * head_count + h
        for r in reversed(range(lax.axis_size("req")))
        for h in [*range(0, head_count, 2), *range(1, head_count, 2)]
    ]
    received = lax.all_to_all(
        send, ("req", "head"), 0, 0, axis_index_groups=[order], tiled=True
    )
    return pl.pallas_call(
        place_kernel,
        out_shape=jax.ShapeDtypeStruct((share, width), BF16),
        in_specs=[VMEM],
        out_specs=VMEM,
        compiler_params=PARAMS,
    )(received)


def solution(mesh):
    return jax.shard_map(
        per_device,
        mesh=mesh,
        in_specs=(
            P("req", None),
            P("req"),
            P("req"),
            P("req"),
            P("req"),
            P("req", None),
            P(None, None, "req", None, "head"),
            P(),
            P(),
            P(None, None, "head"),
            P(None, "head", None),
            P(None, None, None, "head"),
            P(None, "head", None),
            P(None, None, "head"),
        ),
        out_specs=P(("req", "head"), None),
        check_vma=False,
    )
```
